32 devices in a mesh: loop: 16 (over z, x, core), tp: 2 (over y).
Axes of the slice: x: 2, y: 2, z: 4, core: 2. Of those that a mesh axis runs over, the one named last changes fastest.
Arguments:
- mixer_in: bfloat16 [2048, 8192], P('loop', 'tp'), may hold values from -6 to 6
- gate_in: bfloat16 [2048, 8192], P('loop', 'tp'), may hold values from -6 to 6
- residual_in: bfloat16 [2048, 4096], P('loop', 'tp'), may hold values from -6 to 6
- conv_weight: float32 [4, 8192], P(None, 'tp'), may hold values from -3 to 3
- conv_bias: float32 [8192], P('tp'), may hold values from -3 to 3
- state_proj: bfloat16 [8192, 288], P('tp'), may hold values from -0.046875 to 0.046875
- step_proj: bfloat16 [256, 8192], P(None, 'tp'), may hold values from -0.375 to 0.375
- step_bias: float32 [8192], P('tp'), may hold values from -4 to -1
- decay_rate: float32 [16, 8192], P(None, 'tp'), may hold values from 2.4414063e-05 to 4
- skip_gain: float32 [8192], P('tp'), may hold values from 0.25 to 4
- out_proj: bfloat16 [8192, 4096], P('tp', 'loop'), may hold values from -0.09375 to 0.09375
- segment_ids: int32 [2048], replicated, may hold values from 0 to 1, never falling along the last dimension, each value on 1 to 1920 neighbouring positions
- gate_weight: bfloat16 [16, 4096, 6144], P('loop', None, 'tp'), may hold values from -0.09375 to 0.09375
- up_weight: bfloat16 [16, 4096, 6144], P('loop', None, 'tp'), may hold values from -0.09375 to 0.09375
- down_weight: bfloat16 [16, 6144, 4096], P('loop', 'tp'), may hold values from -0.078125 to 0.078125
- routes: int32 [2048, 2], P('loop'), may hold values from 0 to 7, all different within a row; in each aligned block of 128 rows (0 to 127, 128 to 255, ...) at most 40 rows name the same one
- route_weight: float32 [2048, 2], P('loop'), may hold values from 0.2 to 1
- keep_mask: int32 [16, 8], P('loop'), may hold values 0 or 1
Outputs:
- layer_out: bfloat16 [2048, 4096], P('loop', 'tp')
The draws below stay inside these ranges and needn't reach their ends.
Inputs may be any that keep to these rules, and one draw needn't show every extreme that they name: `routes`: in each aligned block of 128 rows, the rows of one device, no expert is named by more than 40 rows.
All inputs are finite; a program needn't handle non-finite values. No bound on the sum of `keep_mask` on one device may be relied on, other than what follows from the above.
Results may differ from the reference program's by a relative error of at most 0.014.
Values may be sent and summed in bfloat16 or wider, within the bound.
No kernel may reach another device: no remote copies, remote signals or barrier semaphores. Data moves between devices by JAX's collectives and lax.ppermute only.
A program may use at most 512 MiB of HBM per device.

```python
import math
import jax
import jax.numpy as jnp
import numpy as np
from jax import lax

D = 4096
DI = 8192
NSTATE = 16
KCONV = 4
RANK = 256
FF = 12288
EXPERTS = 8
TOPK = 2
TOK = 128
LENGTH = 2048
BLOCKS = 16
QUARTERS = 2
CAP = 40
N_TP = 2


def touch_ends(array, rng, low, high):
    dims = array.shape
    index_at = [jax.random.randint(jax.random.fold_in(rng, axis), (), 0, dims[axis]) for axis in range(len(dims))]
    array = array.at[tuple(index_at)].set(low)
    longest = dims.index(max(dims))
    index_at[longest] = (index_at[longest] + 1) % dims[longest]
    return array.at[tuple(index_at)].set(high)


def spiked(entries, stream_key, source, target, shards_of, factor):
    def block_of(dim):
        return (jnp.arange(entries.shape[dim]) // (entries.shape[dim] // shards_of)).reshape((-1,) + (1,) * (entries.ndim - 1 - dim))

    first = jax.random.permutation(stream_key, shards_of)[block_of(target)]
    second = (block_of(target) + shards_of // 2) % shards_of
    return jnp.where((block_of(source) == first) | (block_of(source) == second), factor * entries, entries)


def block_scale(key, extent, split, smallest, largest):
    factor_of, own = 1.0, jax.random.fold_in(key, 6)
    for position, blocks in split:
        draws = jnp.exp(jax.random.uniform(jax.random.fold_in(own, position), (blocks,), jnp.float32, smallest / len(split), largest / len(split)))
        factor_of = factor_of * jnp.repeat(draws, extent[position] // blocks).reshape([-1 if axis == position else 1 for axis in range(len(extent))])
    return factor_of


def split_up(number_of, total, most, lean):
    portions = [(1 << 20) // math.isqrt(grade ** lean) + 1 for grade in range(2, number_of + 1)]
    surplus, counts = total - most - (number_of - 1), [1] * (number_of - 1)
    while surplus > 0:
        candidates = [i for i in range(number_of - 1) if counts[i] < most]
        mass, remaining = sum([portions[i] for i in candidates]), surplus
        for i in candidates:
            more = min(most - counts[i], max(1, remaining * portions[i] // mass), surplus)
            counts[i] = counts[i] + more
            surplus = surplus - more
    return np.array([most] + counts)


def uneven(rng, number_of, total, limit, slope):
    if number_of == 2:
        one = jax.random.randint(rng, (), max(1, total - limit), min(limit, total - 1) + 1)
        return jnp.stack([one, total - one])
    lengths = jnp.asarray(split_up(number_of, total, limit, slope), jnp.int32)
    pairs = (number_of - 1) // 2
    source_of, taker = lengths[1:1 + 2 * pairs:2], lengths[2:2 + 2 * pairs:2]
    margin = jnp.minimum(source_of - 1, limit - taker)
    shifted = jax.random.randint(jax.random.fold_in(rng, 1), (pairs,), 0, 1 << 20) % (margin + 1)
    lengths = lengths.at[1:1 + 2 * pairs:2].set(source_of - shifted).at[2:2 + 2 * pairs:2].set(taker + shifted)
    return lengths[jax.random.permutation(jax.random.fold_in(rng, 2), number_of)]


def deal_out(own_key, own, number, rows, count, top, limit, lean):
    order = jax.random.permutation(own_key, count)
    heavy_load, usual = load_shares(count, rows * top, limit, lean, True), load_shares(count, rows * top, limit, lean, False)
    places = jnp.arange(count)

    def named(tallies, offset_by):
        used = int((tallies > 0).sum())
        fixed = max(1, used // 4)
        moved = fixed + (places - fixed + offset_by * (used - fixed)) % max(1, count - fixed)
        return jnp.zeros((count,), jnp.int32).at[order[jnp.where(places < fixed, places, moved)]].set(jnp.asarray(tallies, jnp.int32))

    tallies = jnp.where(number % 4 == 0, named(heavy_load, number // 4), named(usual, number - number // 4 - 1))
    mixed = jax.random.permutation(jax.random.fold_in(own, 3), count)
    giver, taker = mixed[0:count // 2 * 2:2], mixed[1:count // 2 * 2:2]
    slack = jnp.minimum(tallies[giver] - 1, limit - tallies[taker]) // 2
    slack = jnp.where((giver == order[0]) | (taker == order[0]) | (tallies[taker] == 0), 0, jnp.maximum(slack, 0))
    moved = jax.random.randint(jax.random.fold_in(own, 4), (count // 2,), 0, 1 << 20) % (slack + 1)
    tallies = tallies.at[giver].add(-moved).at[taker].add(moved)
    labels = jnp.searchsorted(jnp.cumsum(tallies), jnp.arange(rows * top), side="right").astype(jnp.int32)
    grid = labels.reshape(top, rows).T
    grid = grid[jax.random.permutation(jax.random.fold_in(own, 1), rows)]
    offset_by = jax.random.randint(jax.random.fold_in(own, 2), (rows, 1), 0, top)
    return jnp.take_along_axis(grid, (jnp.arange(top)[None, :] + offset_by) % top, axis=1)


def load_shares(number_of, total, most, lean, full):
    portions = [(1 << 20) // math.isqrt(rank ** lean) + 1 for rank in range(1, number_of + 1)]
    largest = most if full else min(most, max(-(-total // number_of), total * portions[0] // sum(portions)))
    least = 1 if total - largest >= number_of - 1 else 0
    counts, rest = [largest] + [least] * (number_of - 1), total - largest - least * (number_of - 1)
    while rest > 0:
        free = [i for i in range(1, number_of) if counts[i] < largest] or [i for i in range(1, number_of) if counts[i] < most]
        pool, budget = sum([portions[i] for i in free]), rest
        for i in free:
            more = min(most - counts[i], max(1, budget * portions[i] // pool), rest)
            counts[i] = counts[i] + more
            rest = rest - more
    return np.array(counts)


def gaussian(stream_key, extent, width, bound, cuts=(), held_as=jnp.bfloat16):
    array = jax.random.normal(stream_key, extent, jnp.float32) * width
    if len(cuts) > 0:
        array = block_scale(stream_key, extent, cuts, -0.22, 0.18) * array
    return jnp.clip(array, min=-bound, max=bound).astype(held_as)


def bell_draw_with(stream_key, extent, width, bound, cuts, heavy, kind=jnp.bfloat16):
    entries = width * jax.random.normal(stream_key, extent, jnp.float32)
    if cuts:
        entries = entries * block_scale(stream_key, extent, cuts, -0.22, 0.18)
    return jnp.clip(spiked(entries, jax.random.fold_in(stream_key, 3), *heavy), -bound, bound).astype(kind)


def setup_inputs(seed: int = 0) -> dict:
    streams_of = jax.random.split(jax.random.key(seed), 19)
    mixer_in = gaussian(streams_of[0], (LENGTH, DI), 1.0, 6.0, ((0, 16), (1, 2)))
    gate_in = gaussian(streams_of[1], (LENGTH, DI), 1.0, 6.0, ((0, 16), (1, 2)))
    residual_in = gaussian(streams_of[2], (LENGTH, D), 1.0, 6.0, ((0, 16), (1, 2)))
    conv_weight = gaussian(streams_of[3], (KCONV, DI), 0.5, 3.0, ((1, 2),), jnp.float32)
    conv_bias = gaussian(streams_of[4], (DI,), 0.5, 3.0, ((0, 2),), jnp.float32)
    state_proj = gaussian(streams_of[5], (DI, RANK + 2 * NSTATE), (2 * DI) ** -0.5, 0.046875, ((0, 2),))
    step_proj = gaussian(streams_of[6], (RANK, DI), RANK ** -0.5, 0.375, ((1, 2),))
    step_bias = jnp.clip(-4.0 + 3.0 * jax.random.uniform(streams_of[7], (DI,), jnp.float32) ** block_scale(streams_of[7], (DI,), ((0, 2),), -0.2, 0.2), -4.0, -1.0)
    decay_rate = jnp.clip(jnp.exp(math.log(4.0) - 12.0066456 * jax.random.uniform(streams_of[8], (NSTATE, DI), jnp.float32) ** block_scale(streams_of[8], (NSTATE, DI), ((1, 2),), -0.2, 0.2)), 2.441406286379788e-05, 4.0)
    skip_gain = jnp.clip(jnp.exp(math.log(4.0) - 2.7725887 * jax.random.uniform(streams_of[9], (DI,), jnp.float32) ** block_scale(streams_of[9], (DI,), ((0, 2),), -0.2, 0.2)), 0.25, 4.0)
    out_proj = bell_draw_with(streams_of[10], (DI, D), DI ** -0.5, 0.09375, ((0, 2), (1, 16)), (0, 1, 16, 2.0))
    segment_ids = jnp.searchsorted(jnp.cumsum(uneven(streams_of[11], 2, LENGTH, LENGTH - TOK, 2)), jnp.arange(LENGTH), side="right").astype(jnp.int32)
    gate_weight = gaussian(streams_of[12], (EXPERTS * QUARTERS, D, FF // QUARTERS), D ** -0.5, 0.09375, ((0, 16), (2, 2)))
    up_weight = gaussian(streams_of[13], (EXPERTS * QUARTERS, D, FF // QUARTERS), D ** -0.5, 0.09375, ((0, 16), (2, 2)))
    down_weight = bell_draw_with(streams_of[14], (EXPERTS * QUARTERS, FF // QUARTERS, D), FF ** -0.5, 0.078125, ((0, 16), (1, 2)), (1, 2, 2, 2.0))
    routes_keys = jax.random.split(jax.random.fold_in(streams_of[15], 1), LENGTH // TOK)
    routes_turns = jax.random.permutation(jax.random.fold_in(streams_of[15], 3), LENGTH // TOK)
    routes = jax.vmap(lambda own, number: deal_out(jax.random.fold_in(streams_of[15], 2), own, number, TOK, EXPERTS, TOPK, CAP, 2))(routes_keys, routes_turns).reshape((LENGTH, TOPK))
    route_weight = jnp.clip(0.2 + 0.8 * jax.random.uniform(streams_of[16], (LENGTH, TOPK), jnp.float32) ** block_scale(streams_of[16], (LENGTH, TOPK), ((0, 16),), -0.2, 0.2), 0.2, 1.0)
    keep_mask = touch_ends((jax.random.randint(streams_of[17], (BLOCKS, EXPERTS), 0, 4) < 3).astype(jnp.int32), jax.random.fold_in(streams_of[17], 1), 0, 1)
    return {"mixer_in": mixer_in, "gate_in": gate_in, "residual_in": residual_in, "conv_weight": conv_weight, "conv_bias": conv_bias, "state_proj": state_proj, "step_proj": step_proj, "step_bias": step_bias, "decay_rate": decay_rate, "skip_gain": skip_gain, "out_proj": out_proj, "segment_ids": segment_ids, "gate_weight": gate_weight, "up_weight": up_weight, "down_weight": down_weight, "routes": routes, "route_weight": route_weight, "keep_mask": keep_mask}


def combine_pair(earlier, later):
    return (earlier[0] * later[0], later[0] * earlier[1] + later[1])


def reference(mixer_in, gate_in, residual_in, conv_weight, conv_bias, state_proj, step_proj, step_bias, decay_rate, skip_gain, out_proj, segment_ids, gate_weight, up_weight, down_weight, routes, route_weight, keep_mask):
    length = mixer_in.shape[0]
    conv_taps = conv_weight.shape[0]
    padded = jnp.concatenate([jnp.zeros((conv_taps - 1, DI), jnp.bfloat16), mixer_in], axis=0)
    conv_sum = jnp.broadcast_to(conv_bias[None, :], (length, DI))
    for offset in range(conv_taps):
        conv_sum = conv_sum + conv_weight[offset][None, :] * padded[offset:offset + length].astype(jnp.float32)
    conved = jax.nn.silu(conv_sum).astype(jnp.bfloat16)
    projected = jnp.dot(conved, state_proj, preferred_element_type=jnp.float32)
    low_rank = projected[:, :RANK].astype(jnp.bfloat16)
    in_gain = projected[:, RANK:RANK + NSTATE]
    out_gain = projected[:, RANK + NSTATE:]
    step_size = jax.nn.softplus(jnp.dot(low_rank, step_proj, preferred_element_type=jnp.float32) + step_bias[None, :])
    earlier_ids = jnp.concatenate([segment_ids[:1], segment_ids[:-1]])
    kept = (segment_ids == earlier_ids).astype(jnp.float32)
    conved_f = conved.astype(jnp.float32)

    def advance(state, inputs):
        step, kept_now, driven, in_row, out_row = inputs
        factor = kept_now * jnp.exp(-step[None, :] * decay_rate)
        state = factor * state + (step * driven)[None, :] * in_row[:, None]
        return state, jnp.sum(out_row[:, None] * state, axis=0)

    initial = jnp.zeros((NSTATE, DI), jnp.float32)
    final_state, scanned = lax.scan(advance, initial, (step_size, kept, conved_f, in_gain, out_gain))
    mixer_y = scanned + skip_gain[None, :] * conved_f
    gated = (mixer_y * jax.nn.silu(gate_in.astype(jnp.float32))).astype(jnp.bfloat16)
    mixed_out = jnp.dot(gated, out_proj, preferred_element_type=jnp.float32)
    hidden_in = (residual_in.astype(jnp.float32) + mixed_out).astype(jnp.bfloat16)

    blocks = length // TOK
    quarters = gate_weight.shape[0] // EXPERTS
    flat_routes = routes.reshape(blocks, TOK * TOPK)
    onehot = (flat_routes[:, :, None] == jnp.arange(EXPERTS, dtype=jnp.int32)[None, None, :]).astype(jnp.int32)
    slot_index = jnp.sum(jnp.cumsum(onehot, axis=1) * onehot, axis=2) - 1
    block_ids = jnp.broadcast_to(jnp.arange(blocks, dtype=jnp.int32)[:, None], flat_routes.shape)
    rows_at = (block_ids * CAP + slot_index).reshape(-1)
    token_ids = (block_ids * TOK + jnp.arange(TOK * TOPK, dtype=jnp.int32)[None, :] // TOPK).reshape(-1)
    expert_of = flat_routes.reshape(-1)
    buffer = jnp.zeros((EXPERTS, blocks * CAP, D), jnp.bfloat16)
    buffer = buffer.at[expert_of, rows_at].set(hidden_in[token_ids])
    piece_width = gate_weight.shape[2] // N_TP

    def expert_part(expert_slot):
        slot_rows = buffer[expert_slot // quarters]
        gate_value = jnp.dot(slot_rows, gate_weight[expert_slot], preferred_element_type=jnp.float32)
        up_value = jnp.dot(slot_rows, up_weight[expert_slot], preferred_element_type=jnp.float32)
        hidden = (jax.nn.silu(gate_value) * up_value).astype(jnp.bfloat16)
        running = jnp.zeros((slot_rows.shape[0], D), jnp.float32)
        for tp_part in range(N_TP):
            lower = tp_part * piece_width
            partial_sum = jnp.dot(hidden[:, lower:lower + piece_width], down_weight[expert_slot, lower:lower + piece_width], preferred_element_type=jnp.float32)
            rounded = lax.optimization_barrier(partial_sum.astype(jnp.bfloat16))
            running = running + rounded.astype(jnp.float32)
        return running.astype(jnp.bfloat16)

    part_outputs = lax.map(expert_part, jnp.arange(EXPERTS * quarters, dtype=jnp.int32))
    summed = jnp.sum(part_outputs.reshape(EXPERTS, quarters, blocks * CAP, D).astype(jnp.float32), axis=1)
    picked = summed[expert_of, rows_at]
    keep_weight = keep_mask.astype(jnp.float32)[block_ids.reshape(-1), expert_of]
    weights = route_weight.reshape(-1) * keep_weight
    expert_sum = jnp.sum((weights[:, None] * picked).reshape(length, TOPK, D), axis=1)
    return (hidden_in.astype(jnp.float32) + expert_sum).astype(jnp.bfloat16)
```

```python
import math

import jax
import jax.numpy as jnp
from jax import lax
from jax.experimental import pallas as pl
from jax.experimental.pallas import tpu as pltpu
from jax.sharding import PartitionSpec as P

NSTATE = 16
RANK = 256
EXPERTS = 8
TOPK = 2
CAP = 40
LANES = 128
SUBLANES = 8
RESET = 1e30
LOG2E = math.log2(math.e)
VMEM = 40 * 1024 * 1024


def shifted(x, axis, by):
    size = lax.axis_size(axis)
    pairs = [(i, i + by) for i in range(size) if 0 <= i + by < size]
    return lax.ppermute(x, axis, pairs)


def rotated(x, axis, by):
    size = lax.axis_size(axis)
    return lax.ppermute(x, axis, [(i, (i + by) % size) for i in range(size)])


def scan_end_kernel(
    low_ref, proj_ref, bias_ref, decay_ref, conved_ref, gain_ref, kept_ref,
    step_ref, end_ref, sd_ref, u_ref,
):
    tokens, width = step_ref.shape
    chunk = end_ref.shape[2]
    step = jax.nn.softplus(
        jnp.dot(low_ref[...], proj_ref[...], preferred_element_type=jnp.float32) + bias_ref[...]
    )
    step_ref[...] = step
    sd = jnp.where(kept_ref[...] > 0, step, RESET)
    sd_ref[...] = sd.reshape(sd_ref.shape)
    total = jnp.sum(sd, axis=0, keepdims=True)
    u_ref[...] = (step * conved_ref[...].astype(jnp.float32)).reshape(u_ref.shape)
    cols = [slice(i, i + LANES) for i in range(0, width, LANES)]
    rates = [decay_ref[:, c] * -LOG2E for c in cols]

    def advance(i, state):
        for r in range(SUBLANES):
            gain = gain_ref[i * SUBLANES + r]
            state = tuple(
                jnp.exp2(sd_ref[i, r : r + 1, c] * rate) * h + u_ref[i, r : r + 1, c] * gain
                for c, rate, h in zip(cols, rates, state)
            )
        return state

    zero = tuple(jnp.zeros((NSTATE, LANES), jnp.float32) for _ in cols)
    state = jnp.concatenate(lax.fori_loop(0, tokens // SUBLANES, advance, zero), axis=1)
    high = total.astype(jnp.bfloat16).astype(jnp.float32)
    row = lax.broadcasted_iota(jnp.int32, (NSTATE, width), 0)
    tail = jnp.where(row == 0, high, total - high)
    for k in range(width // chunk):
        part = slice(k * chunk, (k + 1) * chunk)
        end_ref[k, :NSTATE, :] = state[:, part].astype(end_ref.dtype)
        end_ref[k, NSTATE:, :] = tail[:, part].astype(end_ref.dtype)


def carry_kernel(ends_ref, decay_ref, carry_ref):
    rate = decay_ref[...] * -LOG2E
    state = jnp.zeros(rate.shape, jnp.float32)
    for block in range(ends_ref.shape[0]):
        carry_ref[block] = state.astype(carry_ref.dtype)
        tail = ends_ref[block, NSTATE:, :].astype(jnp.float32)
        total = tail[0:1] + tail[1:2]
        end = ends_ref[block, :NSTATE, :].astype(jnp.float32)
        state = jnp.exp2(total * rate) * state + end


def scan_kernel(
    step_ref, decay_ref, conved_ref, gain_ref, kept_ref, carry_ref, pick_ref, skip_ref, gate_ref,
    gated_ref, sd_ref, u_ref, states_ref,
):
    tokens, width = step_ref.shape
    step = step_ref[...]
    conved = conved_ref[...].astype(jnp.float32)
    sd_ref[...] = jnp.where(kept_ref[...] > 0, step, RESET).reshape(sd_ref.shape)
    u_ref[...] = (step * conved).reshape(u_ref.shape)
    cols = [slice(i, i + LANES) for i in range(0, width, LANES)]
    rates = [decay_ref[:, c] * -LOG2E for c in cols]

    def advance(i, state):
        for r in range(SUBLANES):
            gain = gain_ref[i * SUBLANES + r]
            state = tuple(
                jnp.exp2(sd_ref[i, r : r + 1, c] * rate) * h + u_ref[i, r : r + 1, c] * gain
                for c, rate, h in zip(cols, rates, state)
            )
            rows = pl.ds(pl.multiple_of((i * SUBLANES + r) * NSTATE, NSTATE), NSTATE)
            for c, h in zip(cols, state):
                states_ref[rows, c] = h.astype(states_ref.dtype)
        return state

    carry = [carry_ref[k].astype(jnp.float32) for k in range(carry_ref.shape[0])]
    carry = jnp.concatenate(carry, axis=1)
    lax.fori_loop(0, tokens // SUBLANES, advance, tuple(carry[:, c] for c in cols))
    scanned = jnp.dot(pick_ref[...], states_ref[...], preferred_element_type=jnp.float32)
    mixer_y = scanned + skip_ref[...] * conved
    gated_ref[...] = (mixer_y * jax.nn.silu(gate_ref[...].astype(jnp.float32))).astype(
        gated_ref.dtype
    )


def whole(shape):
    return pl.BlockSpec(shape, lambda i: (0,) * len(shape))


def scan_end(low_rank, step_proj, step_bias, decay_rate, conved, gain, kept, groups):
    tokens, channels = conved.shape
    rank = low_rank.shape[1]
    width = min(512, channels)
    chunk = channels // groups
    part = lambda rows: pl.BlockSpec((rows, width), lambda i: (0, i))
    return pl.pallas_call(
        scan_end_kernel,
        grid=(channels // width,),
        in_specs=[
            whole((tokens, rank)), part(rank), part(1), part(NSTATE), part(tokens),
            whole((tokens, NSTATE, LANES)), whole((tokens, 1)),
        ],
        out_specs=[
            part(tokens),
            pl.BlockSpec((width // chunk, 2 * NSTATE, chunk), lambda i: (i, 0, 0)),
        ],
        out_shape=[
            jax.ShapeDtypeStruct((tokens, channels), jnp.float32),
            jax.ShapeDtypeStruct((groups, 2 * NSTATE, chunk), jnp.bfloat16),
        ],
        scratch_shapes=[
            pltpu.VMEM((tokens // SUBLANES, SUBLANES, width), jnp.float32),
            pltpu.VMEM((tokens // SUBLANES, SUBLANES, width), jnp.float32),
        ],
        compiler_params=pltpu.CompilerParams(vmem_limit_bytes=VMEM),
        cost_estimate=pl.CostEstimate(
            flops=5 * tokens * NSTATE * channels,
            bytes_accessed=8 * tokens * channels,
            transcendentals=tokens * NSTATE * channels,
        ),
        name="scan_end",
    )(low_rank, step_proj, step_bias[None, :], decay_rate, conved, gain, kept)


def carries(ends, decay_rate):
    groups, _, chunk = ends.shape
    return pl.pallas_call(
        carry_kernel,
        out_shape=jax.ShapeDtypeStruct((groups, NSTATE, chunk), jnp.bfloat16),
        name="carries",
    )(ends, decay_rate)


def scan_gated(step, decay_rate, conved, gain, kept, carry, pick, skip_gain, gate_in):
    tokens, channels = conved.shape
    width = min(512, channels)
    chunk = carry.shape[2]
    part = lambda rows: pl.BlockSpec((rows, width), lambda i: (0, i))
    return pl.pallas_call(
        scan_kernel,
        grid=(channels // width,),
        in_specs=[
            part(tokens), part(NSTATE), part(tokens), whole((tokens, NSTATE, LANES)),
            whole((tokens, 1)),
            pl.BlockSpec((width // chunk, NSTATE, chunk), lambda i: (i, 0, 0)),
            whole(pick.shape), part(1), part(tokens),
        ],
        out_specs=part(tokens),
        scratch_shapes=[
            pltpu.VMEM((tokens // SUBLANES, SUBLANES, width), jnp.float32),
            pltpu.VMEM((tokens // SUBLANES, SUBLANES, width), jnp.float32),
            pltpu.VMEM((tokens * NSTATE, width), jnp.bfloat16),
        ],
        out_shape=jax.ShapeDtypeStruct((tokens, channels), jnp.bfloat16),
        compiler_params=pltpu.CompilerParams(vmem_limit_bytes=VMEM),
        cost_estimate=pl.CostEstimate(
            flops=7 * tokens * NSTATE * channels,
            bytes_accessed=12 * tokens * channels,
            transcendentals=tokens * NSTATE * channels,
        ),
        name="scan_gated",
    )(step, decay_rate, conved, gain, kept, carry, pick, skip_gain[None, :], gate_in)


def summed_over(x, axis):
    total = x
    for by in range(1, lax.axis_size(axis)):
        total = total + rotated(x, axis, by)
    return total


def scattered_sum(parts, axis, mine):
    size = parts.shape[0]
    take = lambda k: lax.dynamic_index_in_dim(parts, k % size, 0, keepdims=False)
    total = take(mine).astype(jnp.float32)
    for by in range(1, size):
        sent = rotated(take(mine + by).astype(jnp.bfloat16), axis, by)
        total = total + sent.astype(jnp.float32)
    return total


def gathered(x, axis, mine, dim):
    size = lax.axis_size(axis)
    shape = x.shape[:dim] + (size * x.shape[dim],) + x.shape[dim + 1 :]
    out = jnp.zeros(shape, x.dtype)
    out = lax.dynamic_update_slice_in_dim(out, x, mine * x.shape[dim], dim)
    for by in range(1, size):
        source = lax.rem(mine + size - by, size)
        out = lax.dynamic_update_slice_in_dim(
            out, rotated(x, axis, by), source * x.shape[dim], dim
        )
    return out


def teams_swapped(x, members):
    groups = lax.axis_size("loop")
    out = [x[0]]
    for s in range(1, x.shape[0]):
        out.append(
            lax.ppermute(
                x[s],
                "loop",
                [(i, ((i // members) ^ s) * members + i % members) for i in range(groups)],
            )
        )
    return jnp.stack(out)


def per_device(
    mixer_in,
    gate_in,
    residual_in,
    conv_weight,
    conv_bias,
    state_proj,
    step_proj,
    step_bias,
    decay_rate,
    skip_gain,
    out_proj,
    segment_ids,
    gate_weight,
    up_weight,
    down_weight,
    routes,
    route_weight,
    keep_mask,
):
    tokens = mixer_in.shape[0]
    channels = mixer_in.shape[1]
    groups = lax.axis_size("loop")
    position = lax.axis_index("loop")
    shard = lax.axis_index("tp")
    shards = lax.axis_size("tp")
    conv_taps = conv_weight.shape[0]
    rim_rows = shifted(mixer_in[tokens - (conv_taps - 1) :], "loop", 1)
    extended = jnp.concatenate([rim_rows, mixer_in], axis=0)
    conv_sum = jnp.broadcast_to(conv_bias[None, :], (tokens, channels))
    for offset in range(conv_taps):
        conv_sum = conv_sum + conv_weight[offset][None, :] * extended[
            offset : offset + tokens
        ].astype(jnp.float32)
    conved = jax.nn.silu(conv_sum).astype(jnp.bfloat16)
    block_start = position * tokens
    local_ids = lax.dynamic_slice_in_dim(segment_ids, block_start, tokens)
    before_start = jnp.maximum(block_start - 1, 0)
    before_id = lax.dynamic_slice_in_dim(segment_ids, before_start, 1)
    previous = jnp.where(block_start > 0, before_id, local_ids[:1])
    earlier_ids = jnp.concatenate([previous, local_ids[:-1]])
    kept = (local_ids == earlier_ids).astype(jnp.float32)[:, None]
    projected = summed_over(
        jnp.dot(conved, state_proj, preferred_element_type=jnp.float32), "tp"
    )
    low_rank = projected[:, :RANK].astype(jnp.bfloat16)
    in_gain = projected[:, RANK : RANK + NSTATE]
    out_gain = projected[:, RANK + NSTATE :]
    gain = jnp.broadcast_to(in_gain[:, :, None], (tokens, NSTATE, LANES))
    state_rows = jnp.arange(tokens * NSTATE, dtype=jnp.int32)
    spread = state_rows[None, :] % NSTATE == jnp.arange(NSTATE, dtype=jnp.int32)[:, None]
    pick = jnp.where(
        state_rows[None, :] // NSTATE == jnp.arange(tokens, dtype=jnp.int32)[:, None],
        jnp.dot(
            out_gain.astype(jnp.bfloat16),
            spread.astype(jnp.bfloat16),
            preferred_element_type=jnp.float32,
        ),
        0.0,
    ).astype(jnp.bfloat16)
    step_size, end_state = scan_end(
        low_rank, step_proj, step_bias, decay_rate, conved, gain, kept, groups
    )
    ends = lax.all_to_all(end_state, "loop", 0, 0, tiled=True)
    chunk = channels // groups
    own_rates = lax.dynamic_slice_in_dim(decay_rate, position * chunk, chunk, 1)
    carry = lax.all_to_all(carries(ends, own_rates), "loop", 0, 0, tiled=True)
    gated = scan_gated(
        step_size, decay_rate, conved, gain, kept, carry, pick, skip_gain, gate_in
    )
    partial_mix = jnp.dot(
        gated,
        lax.all_gather(out_proj, "loop", axis=1, tiled=True),
        preferred_element_type=jnp.float32,
    )
    features = partial_mix.shape[1]
    width = features // shards
    mixed_out = scattered_sum(
        jnp.stack([partial_mix[:, k * width : (k + 1) * width] for k in range(shards)]),
        "tp",
        shard,
    )
    hidden_in = (residual_in.astype(jnp.float32) + mixed_out).astype(jnp.bfloat16)

    members = groups // EXPERTS
    team, member = position // members, position % members
    flat_routes = routes.reshape(-1)
    expert_ids = jnp.arange(EXPERTS, dtype=jnp.int32)
    onehot = (flat_routes[:, None] == expert_ids[None, :]).astype(jnp.int32)
    slot_index = jnp.sum(jnp.cumsum(onehot, axis=0) * onehot, axis=1) - 1
    target = (flat_routes ^ team) * CAP + slot_index
    selector = (jnp.arange(EXPERTS * CAP, dtype=jnp.int32)[:, None] == target[None, :]).astype(
        jnp.float32
    )
    gather_matrix = jnp.sum(selector.reshape(EXPERTS * CAP, tokens, TOPK), axis=2)
    keep_weight = jnp.sum(onehot.astype(jnp.float32) * keep_mask.astype(jnp.float32), axis=1)
    weights = route_weight.reshape(-1) * keep_weight
    weighted = jnp.sum((selector * weights[None, :]).reshape(EXPERTS * CAP, tokens, TOPK), axis=2)
    packed = jnp.dot(
        gather_matrix.astype(jnp.bfloat16), hidden_in, preferred_element_type=jnp.float32
    ).astype(jnp.bfloat16)
    arrived = teams_swapped(packed.reshape(EXPERTS, CAP, width), members)
    rows = EXPERTS * CAP
    arrived = gathered(arrived.reshape(rows, width), "tp", shard, 1)

    def from_member(by):
        pairs = [
            (i, i // members * members + (i + by) % members) for i in range(groups)
        ]
        return lambda x: lax.ppermute(x, "loop", pairs)

    slot_rows = jnp.concatenate(
        [arrived] + [from_member(by)(arrived) for by in range(1, members)], axis=0
    )
    gate_value = jnp.dot(slot_rows, gate_weight[0], preferred_element_type=jnp.float32)
    up_value = jnp.dot(slot_rows, up_weight[0], preferred_element_type=jnp.float32)
    hidden = (jax.nn.silu(gate_value) * up_value).astype(jnp.bfloat16)
    partial_out = jnp.dot(hidden, down_weight[0], preferred_element_type=jnp.float32)
    partial_out = partial_out.astype(jnp.bfloat16).reshape(members, rows, features)
    member_sum = partial_out[0].astype(jnp.float32)
    for by in range(1, members):
        back = from_member(members - by)(partial_out[by])
        member_sum = member_sum + back.astype(jnp.float32)
    shares = scattered_sum(
        jnp.stack([member_sum[:, k * width : (k + 1) * width] for k in range(shards)]),
        "tp",
        shard,
    )
    returned = teams_swapped(
        shares.astype(jnp.bfloat16).reshape(EXPERTS, CAP, width), members
    ).reshape(rows, width)
    expert_sum = jnp.dot(
        weighted.T,
        returned.astype(jnp.float32),
        precision=lax.Precision.HIGHEST,
        preferred_element_type=jnp.float32,
    )
    return (hidden_in.astype(jnp.float32) + expert_sum).astype(jnp.bfloat16)


def solution(mesh):
    return jax.shard_map(
        per_device,
        mesh=mesh,
        in_specs=(
            P("loop", "tp"),
            P("loop", "tp"),
            P("loop", "tp"),
            P(None, "tp"),
            P("tp"),
            P("tp", None),
            P(None, "tp"),
            P("tp"),
            P(None, "tp"),
            P("tp"),
            P("tp", "loop"),
            P(),
            P("loop", None, "tp"),
            P("loop", None, "tp"),
            P("loop", "tp", None),
            P("loop", None),
            P("loop", None),
            P("loop", None),
        ),
        out_specs=P("loop", "tp"),
        check_vma=False,
    )
```

```python
import math

import jax
import jax.numpy as jnp
from jax import lax
from jax.experimental import pallas as pl
from jax.experimental.pallas import tpu as pltpu
from jax.sharding import PartitionSpec as P

NSTATE = 16
RANK = 256
EXPERTS = 8
TOPK = 2
CAP = 40
LANES = 128
SUBLANES = 8
RESET = 1e30
LOG2E = math.log2(math.e)
VMEM = 40 * 1024 * 1024


def shifted(x, axis, by):
    size = lax.axis_size(axis)
    pairs = [(i, i + by) for i in range(size) if 0 <= i + by < size]
    return lax.ppermute(x, axis, pairs)


def rotated(x, axis, by):
    size = lax.axis_size(axis)
    return lax.ppermute(x, axis, [(i, (i + by) % size) for i in range(size)])


def scan_end_kernel(
    low_ref, proj_ref, bias_ref, decay_ref, conved_ref, gain_ref, kept_ref,
    step_ref, end_ref, sd_ref, u_ref,
):
    tokens, width = step_ref.shape
    chunk = end_ref.shape[2]
    step = jax.nn.softplus(
        jnp.dot(low_ref[...], proj_ref[...], preferred_element_type=jnp.float32) + bias_ref[...]
    )
    step_ref[...] = step
    sd = jnp.where(kept_ref[...] > 0, step, RESET)
    sd_ref[...] = sd.reshape(sd_ref.shape)
    total = jnp.sum(sd, axis=0, keepdims=True)
    u_ref[...] = (step * conved_ref[...].astype(jnp.float32)).reshape(u_ref.shape)
    cols = [slice(i, i + LANES) for i in range(0, width, LANES)]
    rates = [decay_ref[:, c] * -LOG2E for c in cols]

    def advance(i, state):
        for r in range(SUBLANES):
            gain = gain_ref[i * SUBLANES + r]
            state = tuple(
                jnp.exp2(sd_ref[i, r : r + 1, c] * rate) * h + u_ref[i, r : r + 1, c] * gain
                for c, rate, h in zip(cols, rates, state)
            )
        return state

    zero = tuple(jnp.zeros((NSTATE, LANES), jnp.float32) for _ in cols)
    state = jnp.concatenate(lax.fori_loop(0, tokens // SUBLANES, advance, zero), axis=1)
    high = total.astype(jnp.bfloat16).astype(jnp.float32)
    row = lax.broadcasted_iota(jnp.int32, (NSTATE, width), 0)
    tail = jnp.where(row == 0, high, total - high)
    for k in range(width // chunk):
        part = slice(k * chunk, (k + 1) * chunk)
        end_ref[k, :NSTATE, :] = state[:, part].astype(end_ref.dtype)
        end_ref[k, NSTATE:, :] = tail[:, part].astype(end_ref.dtype)


def carry_kernel(ends_ref, decay_ref, carry_ref):
    rate = decay_ref[...] * -LOG2E
    state = jnp.zeros(rate.shape, jnp.float32)
    for block in range(ends_ref.shape[0]):
        carry_ref[block] = state.astype(carry_ref.dtype)
        tail = ends_ref[block, NSTATE:, :].astype(jnp.float32)
        total = tail[0:1] + tail[1:2]
        end = ends_ref[block, :NSTATE, :].astype(jnp.float32)
        state = jnp.exp2(total * rate) * state + end


def scan_kernel(
    step_ref, decay_ref, conved_ref, gain_ref, kept_ref, carry_ref, pick_ref, skip_ref, gate_ref,
    gated_ref, sd_ref, u_ref, states_ref,
):
    tokens, width = step_ref.shape
    step = step_ref[...]
    conved = conved_ref[...].astype(jnp.float32)
    sd_ref[...] = jnp.where(kept_ref[...] > 0, step, RESET).reshape(sd_ref.shape)
    u_ref[...] = (step * conved).reshape(u_ref.shape)
    cols = [slice(i, i + LANES) for i in range(0, width, LANES)]
    rates = [decay_ref[:, c] * -LOG2E for c in cols]

    def advance(i, state):
        for r in range(SUBLANES):
            gain = gain_ref[i * SUBLANES + r]
            state = tuple(
                jnp.exp2(sd_ref[i, r : r + 1, c] * rate) * h + u_ref[i, r : r + 1, c] * gain
                for c, rate, h in zip(cols, rates, state)
            )
            rows = pl.ds(pl.multiple_of((i * SUBLANES + r) * NSTATE, NSTATE), NSTATE)
            for c, h in zip(cols, state):
                states_ref[rows, c] = h.astype(states_ref.dtype)
        return state

    carry = [carry_ref[k].astype(jnp.float32) for k in range(carry_ref.shape[0])]
    carry = jnp.concatenate(carry, axis=1)
    lax.fori_loop(0, tokens // SUBLANES, advance, tuple(carry[:, c] for c in cols))
    scanned = jnp.dot(pick_ref[...], states_ref[...], preferred_element_type=jnp.float32)
    mixer_y = scanned + skip_ref[...] * conved
    gated_ref[...] = (mixer_y * jax.nn.silu(gate_ref[...].astype(jnp.float32))).astype(
        gated_ref.dtype
    )


def whole(shape):
    return pl.BlockSpec(shape, lambda i: (0,) * len(shape))


def scan_end(low_rank, step_proj, step_bias, decay_rate, conved, gain, kept, groups):
    tokens, channels = conved.shape
    rank = low_rank.shape[1]
    width = min(512, channels)
    chunk = channels // groups
    part = lambda rows: pl.BlockSpec((rows, width), lambda i: (0, i))
    return pl.pallas_call(
        scan_end_kernel,
        grid=(channels // width,),
        in_specs=[
            whole((tokens, rank)), part(rank), part(1), part(NSTATE), part(tokens),
            whole((tokens, NSTATE, LANES)), whole((tokens, 1)),
        ],
        out_specs=[
            part(tokens),
            pl.BlockSpec((width // chunk, 2 * NSTATE, chunk), lambda i: (i, 0, 0)),
        ],
        out_shape=[
            jax.ShapeDtypeStruct((tokens, channels), jnp.float32),
            jax.ShapeDtypeStruct((groups, 2 * NSTATE, chunk), jnp.bfloat16),
        ],
        scratch_shapes=[
            pltpu.VMEM((tokens // SUBLANES, SUBLANES, width), jnp.float32),
            pltpu.VMEM((tokens // SUBLANES, SUBLANES, width), jnp.float32),
        ],
        compiler_params=pltpu.CompilerParams(vmem_limit_bytes=VMEM),
        cost_estimate=pl.CostEstimate(
            flops=5 * tokens * NSTATE * channels,
            bytes_accessed=8 * tokens * channels,
            transcendentals=tokens * NSTATE * channels,
        ),
        name="scan_end",
    )(low_rank, step_proj, step_bias[None, :], decay_rate, conved, gain, kept)


def carries(ends, decay_rate):
    groups, _, chunk = ends.shape
    return pl.pallas_call(
        carry_kernel,
        out_shape=jax.ShapeDtypeStruct((groups, NSTATE, chunk), jnp.bfloat16),
        name="carries",
    )(ends, decay_rate)


def scan_gated(step, decay_rate, conved, gain, kept, carry, pick, skip_gain, gate_in):
    tokens, channels = conved.shape
    width = min(512, channels)
    chunk = carry.shape[2]
    part = lambda rows: pl.BlockSpec((rows, width), lambda i: (0, i))
    return pl.pallas_call(
        scan_kernel,
        grid=(channels // width,),
        in_specs=[
            part(tokens), part(NSTATE), part(tokens), whole((tokens, NSTATE, LANES)),
            whole((tokens, 1)),
            pl.BlockSpec((width // chunk, NSTATE, chunk), lambda i: (i, 0, 0)),
            whole(pick.shape), part(1), part(tokens),
        ],
        out_specs=part(tokens),
        scratch_shapes=[
            pltpu.VMEM((tokens // SUBLANES, SUBLANES, width), jnp.float32),
            pltpu.VMEM((tokens // SUBLANES, SUBLANES, width), jnp.float32),
            pltpu.VMEM((tokens * NSTATE, width), jnp.bfloat16),
        ],
        out_shape=jax.ShapeDtypeStruct((tokens, channels), jnp.bfloat16),
        compiler_params=pltpu.CompilerParams(vmem_limit_bytes=VMEM),
        cost_estimate=pl.CostEstimate(
            flops=7 * tokens * NSTATE * channels,
            bytes_accessed=12 * tokens * channels,
            transcendentals=tokens * NSTATE * channels,
        ),
        name="scan_gated",
    )(step, decay_rate, conved, gain, kept, carry, pick, skip_gain[None, :], gate_in)


def summed_over(x, axis):
    total = x
    for by in range(1, lax.axis_size(axis)):
        total = total + rotated(x, axis, by)
    return total


def scattered_sum(parts, axis, mine):
    size = parts.shape[0]
    take = lambda k: lax.dynamic_index_in_dim(parts, k % size, 0, keepdims=False)
    total = take(mine).astype(jnp.float32)
    for by in range(1, size):
        sent = rotated(take(mine + by).astype(jnp.bfloat16), axis, by)
        total = total + sent.astype(jnp.float32)
    return total


def gathered(x, axis, mine, dim):
    size = lax.axis_size(axis)
    shape = x.shape[:dim] + (size * x.shape[dim],) + x.shape[dim + 1 :]
    out = jnp.zeros(shape, x.dtype)
    out = lax.dynamic_update_slice_in_dim(out, x, mine * x.shape[dim], dim)
    for by in range(1, size):
        source = lax.rem(mine + size - by, size)
        out = lax.dynamic_update_slice_in_dim(
            out, rotated(x, axis, by), source * x.shape[dim], dim
        )
    return out


def across(x, mask):
    return lax.ppermute(x, "loop", [(i, i ^ mask) for i in range(lax.axis_size("loop"))])


def teams_swapped(x, first, members):
    groups = lax.axis_size("loop")
    out = []
    for k in range(x.shape[0]):
        s = first + k
        if s == 0:
            out.append(x[k])
            continue
        pairs = [(i, ((i // members) ^ s) * members + i % members) for i in range(groups)]
        out.append(lax.ppermute(x[k], "loop", pairs))
    return jnp.concatenate(out, axis=0)


def hidden_kernel(low_ref, gather_ref, residual_ref, *refs):
    pieces, (hidden_ref, packed_ref) = refs[:-2], refs[-2:]
    for m, piece_ref in enumerate(pieces):
        block = piece_ref.shape[1] // 2
        for dc in range(2):
            place = low_ref[0] ^ (2 * m + dc)
            cols = pl.ds(pl.multiple_of(place * block, block), block)
            mixed = piece_ref[:, dc * block : (dc + 1) * block].astype(jnp.float32)
            hidden_ref[:, cols] = (residual_ref[:, cols].astype(jnp.float32) + mixed).astype(
                hidden_ref.dtype
            )
    packed_ref[...] = jnp.dot(
        gather_ref[...], hidden_ref[...], preferred_element_type=jnp.float32
    ).astype(packed_ref.dtype)


def hidden_and_packed(low, gather_matrix, residual_in, pieces):
    vmem = pl.BlockSpec(memory_space=pltpu.VMEM)
    return pl.pallas_call(
        hidden_kernel,
        in_specs=[pl.BlockSpec(memory_space=pltpu.SMEM)] + [vmem] * (2 + len(pieces)),
        out_specs=[vmem, vmem],
        out_shape=[
            jax.ShapeDtypeStruct(residual_in.shape, jnp.bfloat16),
            jax.ShapeDtypeStruct(
                (gather_matrix.shape[0], residual_in.shape[1]), jnp.bfloat16
            ),
        ],
        compiler_params=pltpu.CompilerParams(vmem_limit_bytes=VMEM),
        name="hidden_and_packed",
    )(low, gather_matrix, residual_in, *pieces)


def per_device(
    mixer_in,
    gate_in,
    residual_in,
    conv_weight,
    conv_bias,
    state_proj,
    step_proj,
    step_bias,
    decay_rate,
    skip_gain,
    out_proj,
    segment_ids,
    gate_weight,
    up_weight,
    down_weight,
    routes,
    route_weight,
    keep_mask,
):
    tokens = mixer_in.shape[0]
    channels = mixer_in.shape[1]
    groups = lax.axis_size("loop")
    position = lax.axis_index("loop")
    shard = lax.axis_index("tp")
    shards = lax.axis_size("tp")
    low = groups // shards
    own_columns = lax.all_gather(
        out_proj,
        "loop",
        axis=1,
        tiled=True,
        axis_index_groups=[[i + low * high for high in range(shards)] for i in range(low)],
    )
    conv_taps = conv_weight.shape[0]
    rim_rows = shifted(mixer_in[tokens - (conv_taps - 1) :], "loop", 1)
    extended = jnp.concatenate([rim_rows, mixer_in], axis=0)
    conv_sum = jnp.broadcast_to(conv_bias[None, :], (tokens, channels))
    for offset in range(conv_taps):
        conv_sum = conv_sum + conv_weight[offset][None, :] * extended[
            offset : offset + tokens
        ].astype(jnp.float32)
    conved = jax.nn.silu(conv_sum).astype(jnp.bfloat16)
    block_start = position * tokens
    local_ids = lax.dynamic_slice_in_dim(segment_ids, block_start, tokens)
    before_start = jnp.maximum(block_start - 1, 0)
    before_id = lax.dynamic_slice_in_dim(segment_ids, before_start, 1)
    previous = jnp.where(block_start > 0, before_id, local_ids[:1])
    earlier_ids = jnp.concatenate([previous, local_ids[:-1]])
    kept = (local_ids == earlier_ids).astype(jnp.float32)[:, None]
    projected = summed_over(
        jnp.dot(conved, state_proj, preferred_element_type=jnp.float32), "tp"
    )
    low_rank = projected[:, :RANK].astype(jnp.bfloat16)
    in_gain = projected[:, RANK : RANK + NSTATE]
    out_gain = projected[:, RANK + NSTATE :]
    gain = jnp.broadcast_to(in_gain[:, :, None], (tokens, NSTATE, LANES))
    state_rows = jnp.arange(tokens * NSTATE, dtype=jnp.int32)
    spread = state_rows[None, :] % NSTATE == jnp.arange(NSTATE, dtype=jnp.int32)[:, None]
    pick = jnp.where(
        state_rows[None, :] // NSTATE == jnp.arange(tokens, dtype=jnp.int32)[:, None],
        jnp.dot(
            out_gain.astype(jnp.bfloat16),
            spread.astype(jnp.bfloat16),
            preferred_element_type=jnp.float32,
        ),
        0.0,
    ).astype(jnp.bfloat16)
    step_size, end_state = scan_end(
        low_rank, step_proj, step_bias, decay_rate, conved, gain, kept, groups
    )
    ends = lax.all_to_all(end_state, "loop", 0, 0, tiled=True)
    chunk = channels // groups
    own_rates = lax.dynamic_slice_in_dim(decay_rate, position * chunk, chunk, 1)
    carry = lax.all_to_all(carries(ends, own_rates), "loop", 0, 0, tiled=True)
    gated = scan_gated(
        step_size, decay_rate, conved, gain, kept, carry, pick, skip_gain, gate_in
    )
    own_low = position % low
    tokens_of = [gated] + [across(gated, m) for m in range(2, low, 2)]
    own_columns, tokens_of = lax.optimization_barrier((own_columns, tokens_of))
    other_columns = across(own_columns, 1)
    all_tokens = jnp.concatenate(tokens_of, axis=0)
    block = out_proj.shape[1]
    halves = [
        jnp.dot(all_tokens, columns, preferred_element_type=jnp.float32)
        for columns in (own_columns, other_columns)
    ]
    for_shard = lambda t: jnp.concatenate(
        [lax.dynamic_slice_in_dim(part, t * block, block, 1) for part in halves], axis=1
    )
    mixed_out = for_shard(shard)
    for by in range(1, shards):
        sent = for_shard((shard + by) % shards).astype(jnp.bfloat16)
        mixed_out = mixed_out + rotated(sent, "tp", by).astype(jnp.float32)
    pieces = [mixed_out[:tokens]]
    for k in range(1, len(tokens_of)):
        rows_out = mixed_out[k * tokens : (k + 1) * tokens].astype(jnp.bfloat16)
        pieces.append(across(rows_out, 2 * k))
    width = residual_in.shape[1]
    features = width * shards

    members = groups // EXPERTS
    team, member = position // members, position % members
    flat_routes = routes.reshape(-1)
    expert_ids = jnp.arange(EXPERTS, dtype=jnp.int32)
    onehot = (flat_routes[:, None] == expert_ids[None, :]).astype(jnp.int32)
    slot_index = jnp.sum(jnp.cumsum(onehot, axis=0) * onehot, axis=1) - 1
    target = (flat_routes ^ team) * CAP + slot_index
    selector = (jnp.arange(EXPERTS * CAP, dtype=jnp.int32)[:, None] == target[None, :]).astype(
        jnp.float32
    )
    gather_matrix = jnp.sum(selector.reshape(EXPERTS * CAP, tokens, TOPK), axis=2)
    keep_weight = jnp.sum(onehot.astype(jnp.float32) * keep_mask.astype(jnp.float32), axis=1)
    weights = route_weight.reshape(-1) * keep_weight
    weighted = jnp.sum((selector * weights[None, :]).reshape(EXPERTS * CAP, tokens, TOPK), axis=2)
    hidden_in, packed = hidden_and_packed(
        own_low.astype(jnp.int32)[None], gather_matrix.astype(jnp.bfloat16), residual_in, pieces
    )
    arrived = teams_swapped(packed.reshape(EXPERTS, CAP, width), 0, members)
    rows = EXPERTS * CAP
    arrived = gathered(arrived.reshape(rows, width), "tp", shard, 1)

    def from_member(by):
        pairs = [
            (i, i // members * members + (i + by) % members) for i in range(groups)
        ]
        return lambda x: lax.ppermute(x, "loop", pairs)

    slot_rows = jnp.concatenate(
        [arrived] + [from_member(by)(arrived) for by in range(1, members)], axis=0
    )
    gate_value = jnp.dot(slot_rows, gate_weight[0], preferred_element_type=jnp.float32)
    up_value = jnp.dot(slot_rows, up_weight[0], preferred_element_type=jnp.float32)
    hidden = (jax.nn.silu(gate_value) * up_value).astype(jnp.bfloat16)
    partial_out = jnp.dot(hidden, down_weight[0], preferred_element_type=jnp.float32)
    partial_out = partial_out.astype(jnp.bfloat16).reshape(members, rows, features)
    member_sum = partial_out[0].astype(jnp.float32)
    for by in range(1, members):
        back = from_member(members - by)(partial_out[by])
        member_sum = member_sum + back.astype(jnp.float32)
    shares = scattered_sum(
        jnp.stack([member_sum[:, k * width : (k + 1) * width] for k in range(shards)]),
        "tp",
        shard,
    )
    returned = teams_swapped(
        shares.astype(jnp.bfloat16).reshape(EXPERTS, CAP, width), 0, members
    ).reshape(rows, width)
    expert_sum = jnp.dot(
        weighted.T,
        returned.astype(jnp.float32),
        precision=lax.Precision.HIGHEST,
        preferred_element_type=jnp.float32,
    )
    return (hidden_in.astype(jnp.float32) + expert_sum).astype(jnp.bfloat16)


def solution(mesh):
    return jax.shard_map(
        per_device,
        mesh=mesh,
        in_specs=(
            P("loop", "tp"),
            P("loop", "tp"),
            P("loop", "tp"),
            P(None, "tp"),
            P("tp"),
            P("tp", None),
            P(None, "tp"),
            P("tp"),
            P(None, "tp"),
            P("tp"),
            P("tp", "loop"),
            P(),
            P("loop", None, "tp"),
            P("loop", None, "tp"),
            P("loop", "tp", None),
            P("loop", None),
            P("loop", None),
            P("loop", None),
        ),
        out_specs=P("loop", "tp"),
        check_vma=False,
    )
```

```python
import math

import jax
import jax.numpy as jnp
from jax import lax
from jax.experimental import pallas as pl
from jax.experimental.pallas import tpu as pltpu
from jax.sharding import PartitionSpec as P

NSTATE = 16
RANK = 256
EXPERTS = 8
TOPK = 2
CAP = 40
LANES = 128
SUBLANES = 8
RESET = 1e30
LOG2E = math.log2(math.e)
VMEM = 40 * 1024 * 1024


def shifted(x, axis, by):
    size = lax.axis_size(axis)
    pairs = [(i, i + by) for i in range(size) if 0 <= i + by < size]
    return lax.ppermute(x, axis, pairs)


def rotated(x, axis, by):
    size = lax.axis_size(axis)
    return lax.ppermute(x, axis, [(i, (i + by) % size) for i in range(size)])


def scan_end_kernel(
    low_ref, proj_ref, bias_ref, decay_ref, conved_ref, gain_ref, kept_ref,
    step_ref, end_ref, sd_ref, u_ref,
):
    tokens, width = step_ref.shape
    chunk = end_ref.shape[2]
    step = jax.nn.softplus(
        jnp.dot(low_ref[...], proj_ref[...], preferred_element_type=jnp.float32) + bias_ref[...]
    )
    step_ref[...] = step
    sd = jnp.where(kept_ref[...] > 0, step, RESET)
    sd_ref[...] = sd.reshape(sd_ref.shape)
    total = jnp.sum(sd, axis=0, keepdims=True)
    u_ref[...] = (step * conved_ref[...].astype(jnp.float32)).reshape(u_ref.shape)
    cols = [slice(i, i + LANES) for i in range(0, width, LANES)]
    rates = [decay_ref[:, c] * -LOG2E for c in cols]

    def advance(i, state):
        for r in range(SUBLANES):
            gain = gain_ref[i * SUBLANES + r]
            state = tuple(
                jnp.exp2(sd_ref[i, r : r + 1, c] * rate) * h + u_ref[i, r : r + 1, c] * gain
                for c, rate, h in zip(cols, rates, state)
            )
        return state

    zero = tuple(jnp.zeros((NSTATE, LANES), jnp.float32) for _ in cols)
    state = jnp.concatenate(lax.fori_loop(0, tokens // SUBLANES, advance, zero), axis=1)
    high = total.astype(jnp.bfloat16).astype(jnp.float32)
    row = lax.broadcasted_iota(jnp.int32, (NSTATE, width), 0)
    tail = jnp.where(row == 0, high, total - high)
    for k in range(width // chunk):
        part = slice(k * chunk, (k + 1) * chunk)
        end_ref[k, :NSTATE, :] = state[:, part].astype(end_ref.dtype)
        end_ref[k, NSTATE:, :] = tail[:, part].astype(end_ref.dtype)


def carry_kernel(ends_ref, decay_ref, carry_ref):
    rate = decay_ref[...] * -LOG2E
    state = jnp.zeros(rate.shape, jnp.float32)
    for block in range(ends_ref.shape[0]):
        carry_ref[block] = state.astype(carry_ref.dtype)
        tail = ends_ref[block, NSTATE:, :].astype(jnp.float32)
        total = tail[0:1] + tail[1:2]
        end = ends_ref[block, :NSTATE, :].astype(jnp.float32)
        state = jnp.exp2(total * rate) * state + end


def scan_kernel(
    step_ref, decay_ref, conved_ref, gain_ref, kept_ref, carry_ref, pick_ref, skip_ref, gate_ref,
    gated_ref, sd_ref, u_ref, states_ref,
):
    tokens, width = step_ref.shape
    step = step_ref[...]
    conved = conved_ref[...].astype(jnp.float32)
    sd_ref[...] = jnp.where(kept_ref[...] > 0, step, RESET).reshape(sd_ref.shape)
    u_ref[...] = (step * conved).reshape(u_ref.shape)
    cols = [slice(i, i + LANES) for i in range(0, width, LANES)]
    rates = [decay_ref[:, c] * -LOG2E for c in cols]

    def advance(i, state):
        for r in range(SUBLANES):
            gain = gain_ref[i * SUBLANES + r]
            state = tuple(
                jnp.exp2(sd_ref[i, r : r + 1, c] * rate) * h + u_ref[i, r : r + 1, c] * gain
                for c, rate, h in zip(cols, rates, state)
            )
            rows = pl.ds(pl.multiple_of((i * SUBLANES + r) * NSTATE, NSTATE), NSTATE)
            for c, h in zip(cols, state):
                states_ref[rows, c] = h.astype(states_ref.dtype)
        return state

    carry = [carry_ref[k].astype(jnp.float32) for k in range(carry_ref.shape[0])]
    carry = jnp.concatenate(carry, axis=1)
    lax.fori_loop(0, tokens // SUBLANES, advance, tuple(carry[:, c] for c in cols))
    scanned = jnp.dot(pick_ref[...], states_ref[...], preferred_element_type=jnp.float32)
    mixer_y = scanned + skip_ref[...] * conved
    gated_ref[...] = (mixer_y * jax.nn.silu(gate_ref[...].astype(jnp.float32))).astype(
        gated_ref.dtype
    )


def whole(shape):
    return pl.BlockSpec(shape, lambda i: (0,) * len(shape))


def scan_end(low_rank, step_proj, step_bias, decay_rate, conved, gain, kept, groups):
    tokens, channels = conved.shape
    rank = low_rank.shape[1]
    width = min(512, channels)
    chunk = channels // groups
    part = lambda rows: pl.BlockSpec((rows, width), lambda i: (0, i))
    return pl.pallas_call(
        scan_end_kernel,
        grid=(channels // width,),
        in_specs=[
            whole((tokens, rank)), part(rank), part(1), part(NSTATE), part(tokens),
            whole((tokens, NSTATE, LANES)), whole((tokens, 1)),
        ],
        out_specs=[
            part(tokens),
            pl.BlockSpec((width // chunk, 2 * NSTATE, chunk), lambda i: (i, 0, 0)),
        ],
        out_shape=[
            jax.ShapeDtypeStruct((tokens, channels), jnp.float32),
            jax.ShapeDtypeStruct((groups, 2 * NSTATE, chunk), jnp.bfloat16),
        ],
        scratch_shapes=[
            pltpu.VMEM((tokens // SUBLANES, SUBLANES, width), jnp.float32),
            pltpu.VMEM((tokens // SUBLANES, SUBLANES, width), jnp.float32),
        ],
        compiler_params=pltpu.CompilerParams(vmem_limit_bytes=VMEM),
        cost_estimate=pl.CostEstimate(
            flops=5 * tokens * NSTATE * channels,
            bytes_accessed=8 * tokens * channels,
            transcendentals=tokens * NSTATE * channels,
        ),
        name="scan_end",
    )(low_rank, step_proj, step_bias[None, :], decay_rate, conved, gain, kept)


def carries(ends, decay_rate):
    groups, _, chunk = ends.shape
    return pl.pallas_call(
        carry_kernel,
        out_shape=jax.ShapeDtypeStruct((groups, NSTATE, chunk), jnp.bfloat16),
        name="carries",
    )(ends, decay_rate)


def scan_gated(step, decay_rate, conved, gain, kept, carry, pick, skip_gain, gate_in, half):
    tokens, channels = conved.shape[0], conved.shape[1] // 2
    width = min(512, channels)
    chunk = carry.shape[2]
    steps = channels // width
    first = half * steps
    part = lambda rows: pl.BlockSpec((rows, width), lambda i: (0, first + i))
    return pl.pallas_call(
        scan_kernel,
        grid=(steps,),
        in_specs=[
            part(tokens), part(NSTATE), part(tokens), whole((tokens, NSTATE, LANES)),
            whole((tokens, 1)),
            pl.BlockSpec((width // chunk, NSTATE, chunk), lambda i: (first + i, 0, 0)),
            whole(pick.shape), part(1), part(tokens),
        ],
        out_specs=pl.BlockSpec((tokens, width), lambda i: (0, i)),
        scratch_shapes=[
            pltpu.VMEM((tokens // SUBLANES, SUBLANES, width), jnp.float32),
            pltpu.VMEM((tokens // SUBLANES, SUBLANES, width), jnp.float32),
            pltpu.VMEM((tokens * NSTATE, width), jnp.bfloat16),
        ],
        out_shape=jax.ShapeDtypeStruct((tokens, channels), jnp.bfloat16),
        compiler_params=pltpu.CompilerParams(vmem_limit_bytes=VMEM),
        cost_estimate=pl.CostEstimate(
            flops=7 * tokens * NSTATE * channels,
            bytes_accessed=12 * tokens * channels,
            transcendentals=tokens * NSTATE * channels,
        ),
        name="scan_gated",
    )(step, decay_rate, conved, gain, kept, carry, pick, skip_gain[None, :], gate_in)


def lower_kernel(shard_ref, hidden_ref, weight_ref, *out_refs):
    out = jnp.dot(hidden_ref[...], weight_ref[0], preferred_element_type=jnp.float32)
    rows = out_refs[0].shape[0]
    for k, out_ref in enumerate(out_refs):
        out_ref[...] = out[k * rows : (k + 1) * rows].astype(out_ref.dtype)


def lowered(hidden, down_weight, shard, width, members):
    rows, depth = hidden.shape
    tile = min(1024, width)
    steps = width // tile
    out = jax.ShapeDtypeStruct((rows // members, width), jnp.bfloat16)
    return pl.pallas_call(
        lower_kernel,
        grid_spec=pltpu.PrefetchScalarGridSpec(
            num_scalar_prefetch=1,
            grid=(steps,),
            in_specs=[
                pl.BlockSpec((rows, depth), lambda i, t: (0, 0)),
                pl.BlockSpec((1, depth, tile), lambda i, t: (0, 0, t[0] * steps + i)),
            ],
            out_specs=[pl.BlockSpec((rows // members, tile), lambda i, t: (0, i))] * members,
        ),
        out_shape=[out] * members,
        compiler_params=pltpu.CompilerParams(vmem_limit_bytes=VMEM),
        cost_estimate=pl.CostEstimate(
            flops=2 * rows * depth * width, bytes_accessed=2 * depth * width, transcendentals=0
        ),
        name="lowered",
    )(shard.astype(jnp.int32)[None], hidden, down_weight)


def summed_over(x, axis):
    total = x
    for by in range(1, lax.axis_size(axis)):
        total = total + rotated(x, axis, by)
    return total


def gathered(x, axis, mine, dim):
    size = lax.axis_size(axis)
    shape = x.shape[:dim] + (size * x.shape[dim],) + x.shape[dim + 1 :]
    out = jnp.zeros(shape, x.dtype)
    out = lax.dynamic_update_slice_in_dim(out, x, mine * x.shape[dim], dim)
    for by in range(1, size):
        source = lax.rem(mine + size - by, size)
        out = lax.dynamic_update_slice_in_dim(
            out, rotated(x, axis, by), source * x.shape[dim], dim
        )
    return out


def across(x, mask):
    return lax.ppermute(x, "loop", [(i, i ^ mask) for i in range(lax.axis_size("loop"))])


def teams_swapped(x, first, members):
    groups = lax.axis_size("loop")
    out = []
    for k in range(x.shape[0]):
        s = first + k
        if s == 0:
            out.append(x[k])
            continue
        pairs = [(i, ((i // members) ^ s) * members + i % members) for i in range(groups)]
        out.append(lax.ppermute(x[k], "loop", pairs))
    return jnp.concatenate(out, axis=0)


def hidden_kernel(low_ref, gather_ref, residual_ref, *refs):
    pieces, (hidden_ref, packed_ref) = refs[:-2], refs[-2:]
    for m, piece_ref in enumerate(pieces):
        block = piece_ref.shape[1] // 2
        for dc in range(2):
            place = low_ref[0] ^ (2 * m + dc)
            cols = pl.ds(pl.multiple_of(place * block, block), block)
            mixed = piece_ref[:, dc * block : (dc + 1) * block].astype(jnp.float32)
            hidden_ref[:, cols] = (residual_ref[:, cols].astype(jnp.float32) + mixed).astype(
                hidden_ref.dtype
            )
    packed_ref[...] = jnp.dot(
        gather_ref[...], hidden_ref[...], preferred_element_type=jnp.float32
    ).astype(packed_ref.dtype)


def hidden_and_packed(low, gather_matrix, residual_in, pieces):
    vmem = pl.BlockSpec(memory_space=pltpu.VMEM)
    return pl.pallas_call(
        hidden_kernel,
        in_specs=[pl.BlockSpec(memory_space=pltpu.SMEM)] + [vmem] * (2 + len(pieces)),
        out_specs=[vmem, vmem],
        out_shape=[
            jax.ShapeDtypeStruct(residual_in.shape, jnp.bfloat16),
            jax.ShapeDtypeStruct(
                (gather_matrix.shape[0], residual_in.shape[1]), jnp.bfloat16
            ),
        ],
        compiler_params=pltpu.CompilerParams(vmem_limit_bytes=VMEM),
        name="hidden_and_packed",
    )(low, gather_matrix, residual_in, *pieces)


def per_device(
    mixer_in,
    gate_in,
    residual_in,
    conv_weight,
    conv_bias,
    state_proj,
    step_proj,
    step_bias,
    decay_rate,
    skip_gain,
    out_proj,
    segment_ids,
    gate_weight,
    up_weight,
    down_weight,
    routes,
    route_weight,
    keep_mask,
):
    tokens = mixer_in.shape[0]
    channels = mixer_in.shape[1]
    groups = lax.axis_size("loop")
    position = lax.axis_index("loop")
    shard = lax.axis_index("tp")
    shards = lax.axis_size("tp")
    low = groups // shards
    columns = [out_proj] + [across(out_proj, low * high) for high in range(1, shards)]
    conv_taps = conv_weight.shape[0]
    rim_rows = shifted(mixer_in[tokens - (conv_taps - 1) :], "loop", 1)
    extended = jnp.concatenate([rim_rows, mixer_in], axis=0)
    conv_sum = jnp.broadcast_to(conv_bias[None, :], (tokens, channels))
    for offset in range(conv_taps):
        conv_sum = conv_sum + conv_weight[offset][None, :] * extended[
            offset : offset + tokens
        ].astype(jnp.float32)
    conved = jax.nn.silu(conv_sum).astype(jnp.bfloat16)
    block_start = position * tokens
    local_ids = lax.dynamic_slice_in_dim(segment_ids, block_start, tokens)
    before_start = jnp.maximum(block_start - 1, 0)
    before_id = lax.dynamic_slice_in_dim(segment_ids, before_start, 1)
    previous = jnp.where(block_start > 0, before_id, local_ids[:1])
    earlier_ids = jnp.concatenate([previous, local_ids[:-1]])
    kept = (local_ids == earlier_ids).astype(jnp.float32)[:, None]
    projected = summed_over(
        jnp.dot(conved, state_proj, preferred_element_type=jnp.float32), "tp"
    )
    low_rank = projected[:, :RANK].astype(jnp.bfloat16)
    in_gain = projected[:, RANK : RANK + NSTATE]
    out_gain = projected[:, RANK + NSTATE :]
    gain = jnp.broadcast_to(in_gain[:, :, None], (tokens, NSTATE, LANES))
    state_rows = jnp.arange(tokens * NSTATE, dtype=jnp.int32)
    spread = state_rows[None, :] % NSTATE == jnp.arange(NSTATE, dtype=jnp.int32)[:, None]
    pick = jnp.where(
        state_rows[None, :] // NSTATE == jnp.arange(tokens, dtype=jnp.int32)[:, None],
        jnp.dot(
            out_gain.astype(jnp.bfloat16),
            spread.astype(jnp.bfloat16),
            preferred_element_type=jnp.float32,
        ),
        0.0,
    ).astype(jnp.bfloat16)
    step_size, end_state = scan_end(
        low_rank, step_proj, step_bias, decay_rate, conved, gain, kept, groups
    )
    ends = lax.all_to_all(end_state, "loop", 0, 0, tiled=True)
    chunk = channels // groups
    own_rates = lax.dynamic_slice_in_dim(decay_rate, position * chunk, chunk, 1)
    carry = lax.all_to_all(carries(ends, own_rates), "loop", 0, 0, tiled=True)
    own_low, own_high = position % low, position // low
    tokens_of = []
    for half in range(2):
        gated = scan_gated(
            step_size, decay_rate, conved, gain, kept, carry, pick, skip_gain, gate_in, half
        )
        tokens_of.append(
            {m: gated if m == 0 else across(gated, m) for m in (0, 2, 4) if m < low}
        )
    columns[1:], tokens_of = lax.optimization_barrier((columns[1:], tokens_of))
    for half, got in enumerate(tokens_of):
        for m in range(6, low, 2):
            one = m & -m
            if one == m:
                got[m] = across(got[0], m)
            else:
                via = one if half == 0 else m ^ one
                got[m] = across(got[via], m ^ via)
    all_tokens = [
        jnp.concatenate([got[m] for m in range(0, low, 2)], axis=0) for got in tokens_of
    ]
    depth = channels // 2
    mixes = []
    for block in columns:
        pair = jnp.concatenate([block, across(block, 1)], axis=1)
        mixes.append(
            jnp.dot(all_tokens[0], pair[:depth], preferred_element_type=jnp.float32)
            + jnp.dot(all_tokens[1], pair[depth:], preferred_element_type=jnp.float32)
        )

    def for_shard(t):
        mix = mixes[0]
        for high in range(1, shards):
            mix = jnp.where((own_high ^ t) == high, mixes[high], mix)
        return mix

    mixed_out = for_shard(shard)
    for by in range(1, shards):
        sent = for_shard((shard + by) % shards).astype(jnp.bfloat16)
        mixed_out = mixed_out + rotated(sent, "tp", by).astype(jnp.float32)
    pieces = [mixed_out[:tokens]]
    for k in range(1, low // 2):
        rows_out = mixed_out[k * tokens : (k + 1) * tokens].astype(jnp.bfloat16)
        pieces.append(across(rows_out, 2 * k))
    width = residual_in.shape[1]
    features = width * shards

    members = groups // EXPERTS
    team, member = position // members, position % members
    flat_routes = routes.reshape(-1)
    expert_ids = jnp.arange(EXPERTS, dtype=jnp.int32)
    onehot = (flat_routes[:, None] == expert_ids[None, :]).astype(jnp.int32)
    slot_index = jnp.sum(jnp.cumsum(onehot, axis=0) * onehot, axis=1) - 1
    target = (flat_routes ^ team) * CAP + slot_index
    selector = (jnp.arange(EXPERTS * CAP, dtype=jnp.int32)[:, None] == target[None, :]).astype(
        jnp.float32
    )
    gather_matrix = jnp.sum(selector.reshape(EXPERTS * CAP, tokens, TOPK), axis=2)
    keep_weight = jnp.sum(onehot.astype(jnp.float32) * keep_mask.astype(jnp.float32), axis=1)
    weights = route_weight.reshape(-1) * keep_weight
    weighted = jnp.sum((selector * weights[None, :]).reshape(EXPERTS * CAP, tokens, TOPK), axis=2)
    hidden_in, packed = hidden_and_packed(
        own_low.astype(jnp.int32)[None], gather_matrix.astype(jnp.bfloat16), residual_in, pieces
    )
    packed = packed.reshape(EXPERTS, CAP, width)
    near = EXPERTS // 2
    rows = near * CAP

    def from_member(by):
        pairs = [
            (i, i // members * members + (i + by) % members) for i in range(groups)
        ]
        return lambda x: lax.ppermute(x, "loop", pairs)

    parts = [
        gathered(teams_swapped(packed[first : first + near], first, members), "tp", shard, 1)
        for first in (near, 0)
    ]
    slot_rows = jnp.concatenate(
        parts + [from_member(by)(part) for by in range(1, members) for part in parts], axis=0
    )
    gate_value = jnp.dot(slot_rows, gate_weight[0], preferred_element_type=jnp.float32)
    up_value = jnp.dot(slot_rows, up_weight[0], preferred_element_type=jnp.float32)
    hidden = (jax.nn.silu(gate_value) * up_value).astype(jnp.bfloat16)

    def member_sum(outs):
        total = outs[0].astype(jnp.float32)
        for by in range(1, members):
            total = total + from_member(members - by)(outs[by]).astype(jnp.float32)
        return total

    def for_shard_of(hidden, t):
        return lowered(hidden, down_weight, t, width, members)

    sent = [
        member_sum(for_shard_of(hidden, (shard + by) % shards)).astype(jnp.bfloat16)
        for by in range(1, shards)
    ]
    hidden, sent = lax.optimization_barrier((hidden, sent))
    far_sums = [rotated(part[:rows], "tp", by) for by, part in enumerate(sent, 1)]
    own_outs = for_shard_of(hidden, shard)
    far_sums, own_outs, near_sent = lax.optimization_barrier(
        (far_sums, own_outs, [part[rows:] for part in sent])
    )
    near_sums = [rotated(part, "tp", by) for by, part in enumerate(near_sent, 1)]
    own_sum = member_sum(own_outs)

    def given_back(first, own, sums):
        share = own
        for part in sums:
            share = share + part.astype(jnp.float32)
        share = share.astype(jnp.bfloat16).reshape(near, CAP, width)
        return teams_swapped(share, first, members)

    far_back = given_back(near, own_sum[:rows], far_sums)
    near_sums, far_back = lax.optimization_barrier((near_sums, far_back))
    back = [given_back(0, own_sum[rows:], near_sums), far_back]
    returned = jnp.concatenate(back, axis=0).reshape(EXPERTS * CAP, width)
    expert_sum = jnp.dot(
        weighted.T,
        returned.astype(jnp.float32),
        precision=lax.Precision.HIGHEST,
        preferred_element_type=jnp.float32,
    )
    return (hidden_in.astype(jnp.float32) + expert_sum).astype(jnp.bfloat16)


def solution(mesh):
    return jax.shard_map(
        per_device,
        mesh=mesh,
        in_specs=(
            P("loop", "tp"),
            P("loop", "tp"),
            P("loop", "tp"),
            P(None, "tp"),
            P("tp"),
            P("tp", None),
            P(None, "tp"),
            P("tp"),
            P(None, "tp"),
            P("tp"),
            P("tp", "loop"),
            P(),
            P("loop", None, "tp"),
            P("loop", None, "tp"),
            P("loop", "tp", None),
            P("loop", None),
            P("loop", None),
            P("loop", None),
        ),
        out_specs=P("loop", "tp"),
        check_vma=False,
    )
```

```python
import math

import jax
import jax.numpy as jnp
from jax import lax
from jax.experimental import pallas as pl
from jax.experimental.pallas import tpu as pltpu
from jax.sharding import PartitionSpec as P

NSTATE = 16
RANK = 256
EXPERTS = 8
TOPK = 2
CAP = 40
LANES = 128
EIGHTHS = 8
SUBLANES = 8
RESET = 1e30
LOG2E = math.log2(math.e)
VMEM = 40 * 1024 * 1024
SMALL_VMEM = 16 * 1024 * 1024


def shifted(x, axis, by):
    size = lax.axis_size(axis)
    pairs = [(i, i + by) for i in range(size) if 0 <= i + by < size]
    return lax.ppermute(x, axis, pairs)


def rotated(x, axis, by):
    size = lax.axis_size(axis)
    return lax.ppermute(x, axis, [(i, (i + by) % size) for i in range(size)])


def scan_end_kernel(
    low_ref, proj_ref, bias_ref, decay_ref, conved_ref, gain_ref, kept_ref,
    step_ref, end_ref, sd_ref, u_ref,
):
    tokens, width = step_ref.shape
    chunk = end_ref.shape[2]
    step = jax.nn.softplus(
        jnp.dot(low_ref[...], proj_ref[...], preferred_element_type=jnp.float32) + bias_ref[...]
    )
    step_ref[...] = step
    sd = jnp.where(kept_ref[...] > 0, step, RESET)
    sd_ref[...] = sd.reshape(sd_ref.shape)
    total = jnp.sum(sd, axis=0, keepdims=True)
    u_ref[...] = (step * conved_ref[...].astype(jnp.float32)).reshape(u_ref.shape)
    cols = [slice(i, i + LANES) for i in range(0, width, LANES)]
    rates = [decay_ref[:, c] * -LOG2E for c in cols]

    def advance(i, state):
        for r in range(SUBLANES):
            gain = gain_ref[i * SUBLANES + r]
            state = tuple(
                jnp.exp2(sd_ref[i, r : r + 1, c] * rate) * h + u_ref[i, r : r + 1, c] * gain
                for c, rate, h in zip(cols, rates, state)
            )
        return state

    zero = tuple(jnp.zeros((NSTATE, LANES), jnp.float32) for _ in cols)
    state = jnp.concatenate(lax.fori_loop(0, tokens // SUBLANES, advance, zero), axis=1)
    high = total.astype(jnp.bfloat16).astype(jnp.float32)
    row = lax.broadcasted_iota(jnp.int32, (NSTATE, width), 0)
    tail = jnp.where(row == 0, high, total - high)
    for k in range(width // chunk):
        part = slice(k * chunk, (k + 1) * chunk)
        end_ref[k, :NSTATE, :] = state[:, part].astype(end_ref.dtype)
        end_ref[k, NSTATE:, :] = tail[:, part].astype(end_ref.dtype)


def carry_kernel(ends_ref, decay_ref, carry_ref):
    rate = decay_ref[...] * -LOG2E
    state = jnp.zeros(rate.shape, jnp.float32)
    for block in range(ends_ref.shape[0]):
        carry_ref[block] = state.astype(carry_ref.dtype)
        tail = ends_ref[block, NSTATE:, :].astype(jnp.float32)
        total = tail[0:1] + tail[1:2]
        end = ends_ref[block, :NSTATE, :].astype(jnp.float32)
        state = jnp.exp2(total * rate) * state + end


def scan_kernel(
    step_ref, decay_ref, conved_ref, gain_ref, kept_ref, carry_ref, pick_ref, skip_ref, gate_ref,
    gated_ref, sd_ref, u_ref, states_ref,
):
    tokens, width = step_ref.shape
    step = step_ref[...]
    conved = conved_ref[...].astype(jnp.float32)
    sd_ref[...] = jnp.where(kept_ref[...] > 0, step, RESET).reshape(sd_ref.shape)
    u_ref[...] = (step * conved).reshape(u_ref.shape)
    cols = [slice(i, i + LANES) for i in range(0, width, LANES)]
    rates = [decay_ref[:, c] * -LOG2E for c in cols]

    def advance(i, state):
        for r in range(SUBLANES):
            gain = gain_ref[i * SUBLANES + r]
            state = tuple(
                jnp.exp2(sd_ref[i, r : r + 1, c] * rate) * h + u_ref[i, r : r + 1, c] * gain
                for c, rate, h in zip(cols, rates, state)
            )
            rows = pl.ds(pl.multiple_of((i * SUBLANES + r) * NSTATE, NSTATE), NSTATE)
            for c, h in zip(cols, state):
                states_ref[rows, c] = h.astype(states_ref.dtype)
        return state

    carry = [carry_ref[k].astype(jnp.float32) for k in range(carry_ref.shape[0])]
    carry = jnp.concatenate(carry, axis=1)
    lax.fori_loop(0, tokens // SUBLANES, advance, tuple(carry[:, c] for c in cols))
    scanned = jnp.dot(pick_ref[...], states_ref[...], preferred_element_type=jnp.float32)
    mixer_y = scanned + skip_ref[...] * conved
    gated_ref[...] = (mixer_y * jax.nn.silu(gate_ref[...].astype(jnp.float32))).astype(
        gated_ref.dtype
    )


def whole(shape):
    return pl.BlockSpec(shape, lambda i: (0,) * len(shape))


def scan_end(low_rank, step_proj, step_bias, decay_rate, conved, gain, kept, groups):
    tokens, channels = conved.shape
    rank = low_rank.shape[1]
    width = min(512, channels)
    chunk = channels // groups
    part = lambda rows: pl.BlockSpec((rows, width), lambda i: (0, i))
    return pl.pallas_call(
        scan_end_kernel,
        grid=(channels // width,),
        in_specs=[
            whole((tokens, rank)), part(rank), part(1), part(NSTATE), part(tokens),
            whole((tokens, NSTATE, LANES)), whole((tokens, 1)),
        ],
        out_specs=[
            part(tokens),
            pl.BlockSpec((width // chunk, 2 * NSTATE, chunk), lambda i: (i, 0, 0)),
        ],
        out_shape=[
            jax.ShapeDtypeStruct((tokens, channels), jnp.float32),
            jax.ShapeDtypeStruct((groups, 2 * NSTATE, chunk), jnp.bfloat16),
        ],
        scratch_shapes=[
            pltpu.VMEM((tokens // SUBLANES, SUBLANES, width), jnp.float32),
            pltpu.VMEM((tokens // SUBLANES, SUBLANES, width), jnp.float32),
        ],
        compiler_params=pltpu.CompilerParams(vmem_limit_bytes=SMALL_VMEM),
        cost_estimate=pl.CostEstimate(
            flops=5 * tokens * NSTATE * channels,
            bytes_accessed=8 * tokens * channels,
            transcendentals=tokens * NSTATE * channels,
        ),
        name="scan_end",
    )(low_rank, step_proj, step_bias[None, :], decay_rate, conved, gain, kept)


def carries(ends, decay_rate):
    groups, _, chunk = ends.shape
    return pl.pallas_call(
        carry_kernel,
        out_shape=jax.ShapeDtypeStruct((groups, NSTATE, chunk), jnp.bfloat16),
        name="carries",
    )(ends, decay_rate)


def scan_gated(step, decay_rate, conved, gain, kept, carry, pick, skip_gain, gate_in, first, steps):
    tokens, width = conved.shape[0], conved.shape[1] // EIGHTHS
    channels = steps * width
    chunk = carry.shape[2]
    part = lambda rows: pl.BlockSpec((rows, width), lambda i: (0, first + i))
    return pl.pallas_call(
        scan_kernel,
        grid=(steps,),
        in_specs=[
            part(tokens), part(NSTATE), part(tokens), whole((tokens, NSTATE, LANES)),
            whole((tokens, 1)),
            pl.BlockSpec((width // chunk, NSTATE, chunk), lambda i: (first + i, 0, 0)),
            whole(pick.shape), part(1), part(tokens),
        ],
        out_specs=pl.BlockSpec((tokens, width), lambda i: (0, i)),
        scratch_shapes=[
            pltpu.VMEM((tokens // SUBLANES, SUBLANES, width), jnp.float32),
            pltpu.VMEM((tokens // SUBLANES, SUBLANES, width), jnp.float32),
            pltpu.VMEM((tokens * NSTATE, width), jnp.bfloat16),
        ],
        out_shape=jax.ShapeDtypeStruct((tokens, channels), jnp.bfloat16),
        compiler_params=pltpu.CompilerParams(vmem_limit_bytes=SMALL_VMEM),
        cost_estimate=pl.CostEstimate(
            flops=7 * tokens * NSTATE * channels,
            bytes_accessed=12 * tokens * channels,
            transcendentals=tokens * NSTATE * channels,
        ),
        name="scan_gated",
    )(step, decay_rate, conved, gain, kept, carry, pick, skip_gain[None, :], gate_in)


def raise_kernel(*refs):
    pieces, (gate_ref, up_ref, hidden_ref, rows_ref) = refs[:-4], refs[-4:]

    @pl.when(pl.program_id(0) == 0)
    def _():
        for k, piece_ref in enumerate(pieces):
            rows = piece_ref.shape[0]
            rows_ref[k * rows : (k + 1) * rows] = piece_ref[...]

    rows = rows_ref[...]
    gate = jnp.dot(rows, gate_ref[0], preferred_element_type=jnp.float32)
    up = jnp.dot(rows, up_ref[0], preferred_element_type=jnp.float32)
    hidden_ref[...] = (jax.nn.silu(gate) * up).astype(hidden_ref.dtype)


def raised(pieces, gate_weight, up_weight):
    rows, depth = sum(piece.shape[0] for piece in pieces), pieces[0].shape[1]
    width = gate_weight.shape[2]
    tile = min(512, width)
    weight = pl.BlockSpec((1, depth, tile), lambda i: (0, 0, i))
    return pl.pallas_call(
        raise_kernel,
        grid=(width // tile,),
        in_specs=[whole(piece.shape) for piece in pieces] + [weight, weight],
        out_specs=pl.BlockSpec((rows, tile), lambda i: (0, i)),
        out_shape=jax.ShapeDtypeStruct((rows, width), jnp.bfloat16),
        scratch_shapes=[pltpu.VMEM((rows, depth), jnp.bfloat16)],
        compiler_params=pltpu.CompilerParams(vmem_limit_bytes=56 * 1024 * 1024),
        cost_estimate=pl.CostEstimate(
            flops=4 * rows * depth * width,
            bytes_accessed=4 * depth * width,
            transcendentals=rows * width,
        ),
        name="raised",
    )(*pieces, gate_weight, up_weight)


def lower_kernel(shard_ref, hidden_ref, weight_ref, *out_refs):
    out = jnp.dot(hidden_ref[...], weight_ref[0], preferred_element_type=jnp.float32)
    rows = out_refs[0].shape[0]
    for k, out_ref in enumerate(out_refs):
        out_ref[...] = out[k * rows : (k + 1) * rows].astype(out_ref.dtype)


def lowered(hidden, down_weight, shard, width, members):
    rows, depth = hidden.shape
    tile = min(1024, width)
    steps = width // tile
    out = jax.ShapeDtypeStruct((rows // members, width), jnp.bfloat16)
    return pl.pallas_call(
        lower_kernel,
        grid_spec=pltpu.PrefetchScalarGridSpec(
            num_scalar_prefetch=1,
            grid=(steps,),
            in_specs=[
                pl.BlockSpec((rows, depth), lambda i, t: (0, 0)),
                pl.BlockSpec((1, depth, tile), lambda i, t: (0, 0, t[0] * steps + i)),
            ],
            out_specs=[pl.BlockSpec((rows // members, tile), lambda i, t: (0, i))] * members,
        ),
        out_shape=[out] * members,
        compiler_params=pltpu.CompilerParams(vmem_limit_bytes=VMEM),
        cost_estimate=pl.CostEstimate(
            flops=2 * rows * depth * width, bytes_accessed=2 * depth * width, transcendentals=0
        ),
        name="lowered",
    )(shard.astype(jnp.int32)[None], hidden, down_weight)


def summed_over(x, axis):
    total = x
    for by in range(1, lax.axis_size(axis)):
        total = total + rotated(x, axis, by)
    return total


def gathered(x, axis, mine, dim):
    size = lax.axis_size(axis)
    shape = x.shape[:dim] + (size * x.shape[dim],) + x.shape[dim + 1 :]
    out = jnp.zeros(shape, x.dtype)
    out = lax.dynamic_update_slice_in_dim(out, x, mine * x.shape[dim], dim)
    for by in range(1, size):
        source = lax.rem(mine + size - by, size)
        out = lax.dynamic_update_slice_in_dim(
            out, rotated(x, axis, by), source * x.shape[dim], dim
        )
    return out


def across(x, mask):
    return lax.ppermute(x, "loop", [(i, i ^ mask) for i in range(lax.axis_size("loop"))])


def teams_swapped(x, first, members):
    groups = lax.axis_size("loop")
    out = []
    for k in range(x.shape[0]):
        s = first + k
        if s == 0:
            out.append(x[k])
            continue
        pairs = [(i, ((i // members) ^ s) * members + i % members) for i in range(groups)]
        out.append(lax.ppermute(x[k], "loop", pairs))
    return jnp.concatenate(out, axis=0)


def hidden_kernel(low_ref, gather_ref, residual_ref, *refs):
    pieces, (hidden_ref, packed_ref) = refs[:-2], refs[-2:]
    for m, piece_ref in enumerate(pieces):
        block = piece_ref.shape[1] // 2
        for dc in range(2):
            place = low_ref[0] ^ (2 * m + dc)
            cols = pl.ds(pl.multiple_of(place * block, block), block)
            mixed = piece_ref[:, dc * block : (dc + 1) * block].astype(jnp.float32)
            hidden_ref[:, cols] = (residual_ref[:, cols].astype(jnp.float32) + mixed).astype(
                hidden_ref.dtype
            )
    packed_ref[...] = jnp.dot(
        gather_ref[...], hidden_ref[...], preferred_element_type=jnp.float32
    ).astype(packed_ref.dtype)


def hidden_and_packed(low, gather_matrix, residual_in, pieces):
    vmem = pl.BlockSpec(memory_space=pltpu.VMEM)
    return pl.pallas_call(
        hidden_kernel,
        in_specs=[pl.BlockSpec(memory_space=pltpu.SMEM)] + [vmem] * (2 + len(pieces)),
        out_specs=[vmem, vmem],
        out_shape=[
            jax.ShapeDtypeStruct(residual_in.shape, jnp.bfloat16),
            jax.ShapeDtypeStruct(
                (gather_matrix.shape[0], residual_in.shape[1]), jnp.bfloat16
            ),
        ],
        compiler_params=pltpu.CompilerParams(vmem_limit_bytes=SMALL_VMEM),
        name="hidden_and_packed",
    )(low, gather_matrix, residual_in, *pieces)


def per_device(
    mixer_in,
    gate_in,
    residual_in,
    conv_weight,
    conv_bias,
    state_proj,
    step_proj,
    step_bias,
    decay_rate,
    skip_gain,
    out_proj,
    segment_ids,
    gate_weight,
    up_weight,
    down_weight,
    routes,
    route_weight,
    keep_mask,
):
    tokens = mixer_in.shape[0]
    channels = mixer_in.shape[1]
    groups = lax.axis_size("loop")
    position = lax.axis_index("loop")
    shard = lax.axis_index("tp")
    shards = lax.axis_size("tp")
    low = groups // shards
    first_steps = 3
    first_rows = channels // EIGHTHS * first_steps
    far_first = [across(out_proj[:first_rows], low * high) for high in range(1, shards)]
    conv_taps = conv_weight.shape[0]
    rim_rows = shifted(mixer_in[tokens - (conv_taps - 1) :], "loop", 1)
    extended = jnp.concatenate([rim_rows, mixer_in], axis=0)
    conv_sum = jnp.broadcast_to(conv_bias[None, :], (tokens, channels))
    for offset in range(conv_taps):
        conv_sum = conv_sum + conv_weight[offset][None, :] * extended[
            offset : offset + tokens
        ].astype(jnp.float32)
    conved = jax.nn.silu(conv_sum).astype(jnp.bfloat16)
    block_start = position * tokens
    local_ids = lax.dynamic_slice_in_dim(segment_ids, block_start, tokens)
    before_start = jnp.maximum(block_start - 1, 0)
    before_id = lax.dynamic_slice_in_dim(segment_ids, before_start, 1)
    previous = jnp.where(block_start > 0, before_id, local_ids[:1])
    earlier_ids = jnp.concatenate([previous, local_ids[:-1]])
    kept = (local_ids == earlier_ids).astype(jnp.float32)[:, None]
    projected = summed_over(
        jnp.dot(conved, state_proj, preferred_element_type=jnp.float32), "tp"
    )
    low_rank = projected[:, :RANK].astype(jnp.bfloat16)
    in_gain = projected[:, RANK : RANK + NSTATE]
    out_gain = projected[:, RANK + NSTATE :]
    gain = jnp.broadcast_to(in_gain[:, :, None], (tokens, NSTATE, LANES))
    state_rows = jnp.arange(tokens * NSTATE, dtype=jnp.int32)
    spread = state_rows[None, :] % NSTATE == jnp.arange(NSTATE, dtype=jnp.int32)[:, None]
    pick = jnp.where(
        state_rows[None, :] // NSTATE == jnp.arange(tokens, dtype=jnp.int32)[:, None],
        jnp.dot(
            out_gain.astype(jnp.bfloat16),
            spread.astype(jnp.bfloat16),
            preferred_element_type=jnp.float32,
        ),
        0.0,
    ).astype(jnp.bfloat16)
    step_size, end_state = scan_end(
        low_rank, step_proj, step_bias, decay_rate, conved, gain, kept, groups
    )
    end_state, far_first = lax.optimization_barrier((end_state, far_first))
    ends = lax.all_to_all(end_state, "loop", 0, 0, tiled=True)
    chunk = channels // groups
    own_rates = lax.dynamic_slice_in_dim(decay_rate, position * chunk, chunk, 1)
    carry = lax.all_to_all(carries(ends, own_rates), "loop", 0, 0, tiled=True)
    later_rows, carry = lax.optimization_barrier((out_proj[first_rows:], carry))
    far_later = [across(later_rows, low * high) for high in range(1, shards)]
    own_low, own_high = position % low, position // low
    tokens_of = []
    for first, steps in ((0, first_steps), (first_steps, EIGHTHS - first_steps)):
        gated = scan_gated(
            step_size, decay_rate, conved, gain, kept, carry, pick, skip_gain, gate_in, first,
            steps,
        )
        tokens_of.append(
            {m: gated if m == 0 else across(gated, m) for m in (0, 2, 4) if m < low}
        )
    far_later, tokens_of = lax.optimization_barrier((far_later, tokens_of))
    for half, got in enumerate(tokens_of):
        for m in range(6, low, 2):
            one = m & -m
            if one == m:
                got[m] = across(got[0], m)
            else:
                via = one if half == 0 else m ^ one
                got[m] = across(got[via], m ^ via)
    all_tokens = [
        jnp.concatenate([got[m] for m in range(0, low, 2)], axis=0) for got in tokens_of
    ]
    blocks = [(out_proj[:first_rows], out_proj[first_rows:])] + list(zip(far_first, far_later))
    mixes = []
    for block in blocks:
        mix = 0.0
        for some_tokens, part in zip(all_tokens, block):
            pair = jnp.concatenate([part, across(part, 1)], axis=1)
            mix = mix + jnp.dot(some_tokens, pair, preferred_element_type=jnp.float32)
        mixes.append(mix)

    def for_shard(t):
        mix = mixes[0]
        for high in range(1, shards):
            mix = jnp.where((own_high ^ t) == high, mixes[high], mix)
        return mix

    mixed_out = for_shard(shard)
    for by in range(1, shards):
        sent = for_shard((shard + by) % shards).astype(jnp.bfloat16)
        mixed_out = mixed_out + rotated(sent, "tp", by).astype(jnp.float32)
    pieces = [mixed_out[:tokens]]
    for k in range(1, low // 2):
        rows_out = mixed_out[k * tokens : (k + 1) * tokens].astype(jnp.bfloat16)
        pieces.append(across(rows_out, 2 * k))
    width = residual_in.shape[1]
    features = width * shards

    members = groups // EXPERTS
    team, member = position // members, position % members
    flat_routes = routes.reshape(-1)
    expert_ids = jnp.arange(EXPERTS, dtype=jnp.int32)
    onehot = (flat_routes[:, None] == expert_ids[None, :]).astype(jnp.int32)
    slot_index = jnp.sum(jnp.cumsum(onehot, axis=0) * onehot, axis=1) - 1
    target = (flat_routes ^ team) * CAP + slot_index
    selector = (jnp.arange(EXPERTS * CAP, dtype=jnp.int32)[:, None] == target[None, :]).astype(
        jnp.float32
    )
    gather_matrix = jnp.sum(selector.reshape(EXPERTS * CAP, tokens, TOPK), axis=2)
    keep_weight = jnp.sum(onehot.astype(jnp.float32) * keep_mask.astype(jnp.float32), axis=1)
    weights = route_weight.reshape(-1) * keep_weight
    weighted = jnp.sum((selector * weights[None, :]).reshape(EXPERTS * CAP, tokens, TOPK), axis=2)
    hidden_in, packed = hidden_and_packed(
        own_low.astype(jnp.int32)[None], gather_matrix.astype(jnp.bfloat16), residual_in, pieces
    )
    packed = packed.reshape(EXPERTS, CAP, width)
    near = EXPERTS // 2
    rows = near * CAP

    def from_member(by):
        pairs = [
            (i, i // members * members + (i + by) % members) for i in range(groups)
        ]
        return lambda x: lax.ppermute(x, "loop", pairs)

    parts = [
        gathered(teams_swapped(packed[first : first + near], first, members), "tp", shard, 1)
        for first in (near, 0)
    ]
    pieces = parts + [from_member(by)(part) for by in range(1, members) for part in parts]
    hidden = raised(pieces, gate_weight, up_weight)

    def member_sum(outs):
        total = outs[0].astype(jnp.float32)
        for by in range(1, members):
            total = total + from_member(members - by)(outs[by]).astype(jnp.float32)
        return total

    def for_shard_of(hidden, t):
        return lowered(hidden, down_weight, t, width, members)

    sent = [
        member_sum(for_shard_of(hidden, (shard + by) % shards)).astype(jnp.bfloat16)
        for by in range(1, shards)
    ]
    hidden, sent = lax.optimization_barrier((hidden, sent))
    far_sums = [rotated(part[:rows], "tp", by) for by, part in enumerate(sent, 1)]
    own_outs = for_shard_of(hidden, shard)
    far_sums, own_outs, near_sent = lax.optimization_barrier(
        (far_sums, own_outs, [part[rows:] for part in sent])
    )
    near_sums = [rotated(part, "tp", by) for by, part in enumerate(near_sent, 1)]
    own_sum = member_sum(own_outs)

    def given_back(first, own, sums):
        share = own
        for part in sums:
            share = share + part.astype(jnp.float32)
        share = share.astype(jnp.bfloat16).reshape(near, CAP, width)
        return teams_swapped(share, first, members)

    far_back = given_back(near, own_sum[:rows], far_sums)
    near_sums, far_back = lax.optimization_barrier((near_sums, far_back))
    back = [given_back(0, own_sum[rows:], near_sums), far_back]
    returned = jnp.concatenate(back, axis=0).reshape(EXPERTS * CAP, width)
    expert_sum = jnp.dot(
        weighted.T,
        returned.astype(jnp.float32),
        precision=lax.Precision.HIGHEST,
        preferred_element_type=jnp.float32,
    )
    return (hidden_in.astype(jnp.float32) + expert_sum).astype(jnp.bfloat16)


def solution(mesh):
    return jax.shard_map(
        per_device,
        mesh=mesh,
        in_specs=(
            P("loop", "tp"),
            P("loop", "tp"),
            P("loop", "tp"),
            P(None, "tp"),
            P("tp"),
            P("tp", None),
            P(None, "tp"),
            P("tp"),
            P(None, "tp"),
            P("tp"),
            P("tp", "loop"),
            P(),
            P("loop", None, "tp"),
            P("loop", None, "tp"),
            P("loop", "tp", None),
            P("loop", None),
            P("loop", None),
            P("loop", None),
        ),
        out_specs=P("loop", "tp"),
        check_vma=False,
    )
```

```python
import functools
import math

import jax
import jax.numpy as jnp
from jax import lax
from jax.experimental import pallas as pl
from jax.experimental.pallas import tpu as pltpu
from jax.sharding import PartitionSpec as P

NSTATE = 16
RANK = 256
EXPERTS = 8
TOPK = 2
CAP = 40
LANES = 128
EIGHTHS = 8
SUBLANES = 8
RESET = 1e30
LOG2E = math.log2(math.e)
VMEM = 40 * 1024 * 1024
SMALL_VMEM = 16 * 1024 * 1024


def shifted(x, axis, by):
    size = lax.axis_size(axis)
    pairs = [(i, i + by) for i in range(size) if 0 <= i + by < size]
    return lax.ppermute(x, axis, pairs)


def rotated(x, axis, by):
    size = lax.axis_size(axis)
    return lax.ppermute(x, axis, [(i, (i + by) % size) for i in range(size)])


def scan_end_kernel(
    low_ref, proj_ref, bias_ref, decay_ref, conved_ref, gain_ref, kept_ref,
    step_ref, end_ref, sd_ref, u_ref,
):
    tokens, width = step_ref.shape
    chunk = end_ref.shape[2]
    step = jax.nn.softplus(
        jnp.dot(low_ref[...], proj_ref[...], preferred_element_type=jnp.float32) + bias_ref[...]
    )
    step_ref[...] = step
    sd = jnp.where(kept_ref[...] > 0, step, RESET)
    sd_ref[...] = sd.reshape(sd_ref.shape)
    total = jnp.sum(sd, axis=0, keepdims=True)
    u_ref[...] = (step * conved_ref[...].astype(jnp.float32)).reshape(u_ref.shape)
    cols = [slice(i, i + LANES) for i in range(0, width, LANES)]
    rates = [decay_ref[:, c] * -LOG2E for c in cols]

    def advance(i, state):
        for r in range(SUBLANES):
            gain = gain_ref[i * SUBLANES + r]
            state = tuple(
                jnp.exp2(sd_ref[i, r : r + 1, c] * rate) * h + u_ref[i, r : r + 1, c] * gain
                for c, rate, h in zip(cols, rates, state)
            )
        return state

    zero = tuple(jnp.zeros((NSTATE, LANES), jnp.float32) for _ in cols)
    state = jnp.concatenate(lax.fori_loop(0, tokens // SUBLANES, advance, zero), axis=1)
    high = total.astype(jnp.bfloat16).astype(jnp.float32)
    row = lax.broadcasted_iota(jnp.int32, (NSTATE, width), 0)
    tail = jnp.where(row == 0, high, total - high)
    for k in range(width // chunk):
        part = slice(k * chunk, (k + 1) * chunk)
        end_ref[k, :NSTATE, :] = state[:, part].astype(end_ref.dtype)
        end_ref[k, NSTATE:, :] = tail[:, part].astype(end_ref.dtype)


def carry_kernel(ends_ref, decay_ref, carry_ref):
    rate = decay_ref[...] * -LOG2E
    state = jnp.zeros(rate.shape, jnp.float32)
    for block in range(ends_ref.shape[0]):
        carry_ref[block] = state.astype(carry_ref.dtype)
        tail = ends_ref[block, NSTATE:, :].astype(jnp.float32)
        total = tail[0:1] + tail[1:2]
        end = ends_ref[block, :NSTATE, :].astype(jnp.float32)
        state = jnp.exp2(total * rate) * state + end


def scan_kernel(
    step_ref, decay_ref, conved_ref, gain_ref, kept_ref, carry_ref, pick_ref, skip_ref, gate_ref,
    gated_ref, sd_ref, u_ref, states_ref,
):
    tokens, width = step_ref.shape
    step = step_ref[...]
    conved = conved_ref[...].astype(jnp.float32)
    sd_ref[...] = jnp.where(kept_ref[...] > 0, step, RESET).reshape(sd_ref.shape)
    u_ref[...] = (step * conved).reshape(u_ref.shape)
    cols = [slice(i, i + LANES) for i in range(0, width, LANES)]
    rates = [decay_ref[:, c] * -LOG2E for c in cols]

    def advance(i, state):
        for r in range(SUBLANES):
            gain = gain_ref[i * SUBLANES + r]
            state = tuple(
                jnp.exp2(sd_ref[i, r : r + 1, c] * rate) * h + u_ref[i, r : r + 1, c] * gain
                for c, rate, h in zip(cols, rates, state)
            )
            rows = pl.ds(pl.multiple_of((i * SUBLANES + r) * NSTATE, NSTATE), NSTATE)
            for c, h in zip(cols, state):
                states_ref[rows, c] = h.astype(states_ref.dtype)
        return state

    carry = [carry_ref[k].astype(jnp.float32) for k in range(carry_ref.shape[0])]
    carry = jnp.concatenate(carry, axis=1)
    lax.fori_loop(0, tokens // SUBLANES, advance, tuple(carry[:, c] for c in cols))
    scanned = jnp.dot(pick_ref[...], states_ref[...], preferred_element_type=jnp.float32)
    mixer_y = scanned + skip_ref[...] * conved
    gated_ref[...] = (mixer_y * jax.nn.silu(gate_ref[...].astype(jnp.float32))).astype(
        gated_ref.dtype
    )


def whole(shape):
    return pl.BlockSpec(shape, lambda i: (0,) * len(shape))


def scan_end(low_rank, step_proj, step_bias, decay_rate, conved, gain, kept, groups):
    tokens, channels = conved.shape
    rank = low_rank.shape[1]
    width = min(512, channels)
    chunk = channels // groups
    part = lambda rows: pl.BlockSpec((rows, width), lambda i: (0, i))
    return pl.pallas_call(
        scan_end_kernel,
        grid=(channels // width,),
        in_specs=[
            whole((tokens, rank)), part(rank), part(1), part(NSTATE), part(tokens),
            whole((tokens, NSTATE, LANES)), whole((tokens, 1)),
        ],
        out_specs=[
            part(tokens),
            pl.BlockSpec((width // chunk, 2 * NSTATE, chunk), lambda i: (i, 0, 0)),
        ],
        out_shape=[
            jax.ShapeDtypeStruct((tokens, channels), jnp.float32),
            jax.ShapeDtypeStruct((groups, 2 * NSTATE, chunk), jnp.bfloat16),
        ],
        scratch_shapes=[
            pltpu.VMEM((tokens // SUBLANES, SUBLANES, width), jnp.float32),
            pltpu.VMEM((tokens // SUBLANES, SUBLANES, width), jnp.float32),
        ],
        compiler_params=pltpu.CompilerParams(vmem_limit_bytes=SMALL_VMEM),
        cost_estimate=pl.CostEstimate(
            flops=5 * tokens * NSTATE * channels,
            bytes_accessed=8 * tokens * channels,
            transcendentals=tokens * NSTATE * channels,
        ),
        name="scan_end",
    )(low_rank, step_proj, step_bias[None, :], decay_rate, conved, gain, kept)


def carries(ends, decay_rate):
    groups, _, chunk = ends.shape
    return pl.pallas_call(
        carry_kernel,
        out_shape=jax.ShapeDtypeStruct((groups, NSTATE, chunk), jnp.bfloat16),
        name="carries",
    )(ends, decay_rate)


def scan_gated(step, decay_rate, conved, gain, kept, carry, pick, skip_gain, gate_in, first, steps):
    tokens, width = conved.shape[0], conved.shape[1] // EIGHTHS
    channels = steps * width
    chunk = carry.shape[2]
    part = lambda rows: pl.BlockSpec((rows, width), lambda i: (0, first + i))
    return pl.pallas_call(
        scan_kernel,
        grid=(steps,),
        in_specs=[
            part(tokens), part(NSTATE), part(tokens), whole((tokens, NSTATE, LANES)),
            whole((tokens, 1)),
            pl.BlockSpec((width // chunk, NSTATE, chunk), lambda i: (first + i, 0, 0)),
            whole(pick.shape), part(1), part(tokens),
        ],
        out_specs=pl.BlockSpec((tokens, width), lambda i: (0, i)),
        scratch_shapes=[
            pltpu.VMEM((tokens // SUBLANES, SUBLANES, width), jnp.float32),
            pltpu.VMEM((tokens // SUBLANES, SUBLANES, width), jnp.float32),
            pltpu.VMEM((tokens * NSTATE, width), jnp.bfloat16),
        ],
        out_shape=jax.ShapeDtypeStruct((tokens, channels), jnp.bfloat16),
        compiler_params=pltpu.CompilerParams(vmem_limit_bytes=SMALL_VMEM),
        cost_estimate=pl.CostEstimate(
            flops=7 * tokens * NSTATE * channels,
            bytes_accessed=12 * tokens * channels,
            transcendentals=tokens * NSTATE * channels,
        ),
        name="scan_gated",
    )(step, decay_rate, conved, gain, kept, carry, pick, skip_gain[None, :], gate_in)


def raise_kernel(shard_ref, *refs, pieces, members, steps):
    piece_refs, (gate_ref, up_ref, down_ref, hidden_ref) = refs[:pieces], refs[pieces : pieces + 4]
    out_refs, (rows_ref, all_ref) = refs[pieces + 4 : -2], refs[-2:]
    step = pl.program_id(0)

    @pl.when(step == 0)
    def _():
        for k, piece_ref in enumerate(piece_refs):
            rows = piece_ref.shape[0]
            rows_ref[k * rows : (k + 1) * rows] = piece_ref[...]

    @pl.when(step < steps)
    def _():
        rows = rows_ref[...]
        tile = hidden_ref.shape[1]
        gate = jnp.dot(rows, gate_ref[0], preferred_element_type=jnp.float32)
        up = jnp.dot(rows, up_ref[0], preferred_element_type=jnp.float32)
        hidden = (jax.nn.silu(gate) * up).astype(hidden_ref.dtype)
        hidden_ref[...] = hidden
        all_ref[:, pl.ds(pl.multiple_of(step * tile, tile), tile)] = hidden

    @pl.when(step >= steps)
    def _():
        out = jnp.dot(all_ref[...], down_ref[0], preferred_element_type=jnp.float32)
        for k, out_ref in enumerate(out_refs):
            rows = out_ref.shape[0]
            out_ref[...] = out[k * rows : (k + 1) * rows].astype(out_ref.dtype)


def raised(pieces, gate_weight, up_weight, down_weight, shard, features, members):
    rows, depth = sum(piece.shape[0] for piece in pieces), pieces[0].shape[1]
    width = gate_weight.shape[2]
    tile, out_tile = min(512, width), min(512, features)
    steps, out_steps = width // tile, features // out_tile
    up_at = lambda i: jnp.minimum(i, steps - 1)
    down_at = lambda i: jnp.maximum(i - steps, 0)
    weight = pl.BlockSpec((1, depth, tile), lambda i, t: (0, 0, up_at(i)))
    outs = pl.pallas_call(
        functools.partial(raise_kernel, pieces=len(pieces), members=members, steps=steps),
        grid_spec=pltpu.PrefetchScalarGridSpec(
            num_scalar_prefetch=1,
            grid=(steps + out_steps,),
            in_specs=[pl.BlockSpec(piece.shape, lambda i, t: (0, 0)) for piece in pieces]
            + [
                weight,
                weight,
                pl.BlockSpec(
                    (1, width, out_tile), lambda i, t: (0, 0, t[0] * out_steps + down_at(i))
                ),
            ],
            out_specs=[pl.BlockSpec((rows, tile), lambda i, t: (0, up_at(i)))]
            + [pl.BlockSpec((rows // members, out_tile), lambda i, t: (0, down_at(i)))] * members,
            scratch_shapes=[
                pltpu.VMEM((rows, depth), jnp.bfloat16),
                pltpu.VMEM((rows, width), jnp.bfloat16),
            ],
        ),
        out_shape=[jax.ShapeDtypeStruct((rows, width), jnp.bfloat16)]
        + [jax.ShapeDtypeStruct((rows // members, features), jnp.bfloat16)] * members,
        compiler_params=pltpu.CompilerParams(vmem_limit_bytes=60 * 1024 * 1024),
        cost_estimate=pl.CostEstimate(
            flops=2 * rows * width * (2 * depth + features),
            bytes_accessed=2 * width * (2 * depth + features),
            transcendentals=rows * width,
        ),
        name="raised",
    )(shard.astype(jnp.int32)[None], *pieces, gate_weight, up_weight, down_weight)
    return outs[0], outs[1:]


def lower_kernel(shard_ref, hidden_ref, weight_ref, *out_refs):
    out = jnp.dot(hidden_ref[...], weight_ref[0], preferred_element_type=jnp.float32)
    rows = out_refs[0].shape[0]
    for k, out_ref in enumerate(out_refs):
        out_ref[...] = out[k * rows : (k + 1) * rows].astype(out_ref.dtype)


def lowered(hidden, down_weight, shard, width, members):
    rows, depth = hidden.shape
    tile = min(512, width)
    steps = width // tile
    out = jax.ShapeDtypeStruct((rows // members, width), jnp.bfloat16)
    return pl.pallas_call(
        lower_kernel,
        grid_spec=pltpu.PrefetchScalarGridSpec(
            num_scalar_prefetch=1,
            grid=(steps,),
            in_specs=[
                pl.BlockSpec((rows, depth), lambda i, t: (0, 0)),
                pl.BlockSpec((1, depth, tile), lambda i, t: (0, 0, t[0] * steps + i)),
            ],
            out_specs=[pl.BlockSpec((rows // members, tile), lambda i, t: (0, i))] * members,
        ),
        out_shape=[out] * members,
        compiler_params=pltpu.CompilerParams(vmem_limit_bytes=VMEM),
        cost_estimate=pl.CostEstimate(
            flops=2 * rows * depth * width, bytes_accessed=2 * depth * width, transcendentals=0
        ),
        name="lowered",
    )(shard.astype(jnp.int32)[None], hidden, down_weight)


def summed_over(x, axis):
    total = x
    for by in range(1, lax.axis_size(axis)):
        total = total + rotated(x, axis, by)
    return total


def gathered(x, axis, mine, dim):
    size = lax.axis_size(axis)
    shape = x.shape[:dim] + (size * x.shape[dim],) + x.shape[dim + 1 :]
    out = jnp.zeros(shape, x.dtype)
    out = lax.dynamic_update_slice_in_dim(out, x, mine * x.shape[dim], dim)
    for by in range(1, size):
        source = lax.rem(mine + size - by, size)
        out = lax.dynamic_update_slice_in_dim(
            out, rotated(x, axis, by), source * x.shape[dim], dim
        )
    return out


def across(x, mask):
    return lax.ppermute(x, "loop", [(i, i ^ mask) for i in range(lax.axis_size("loop"))])


def teams_swapped(x, first, members):
    groups = lax.axis_size("loop")
    out = []
    for k in range(x.shape[0]):
        s = first + k
        if s == 0:
            out.append(x[k])
            continue
        pairs = [(i, ((i // members) ^ s) * members + i % members) for i in range(groups)]
        out.append(lax.ppermute(x[k], "loop", pairs))
    return jnp.concatenate(out, axis=0)


def hidden_kernel(low_ref, gather_ref, residual_ref, *refs):
    pieces, (hidden_ref, packed_ref) = refs[:-2], refs[-2:]
    for m, piece_ref in enumerate(pieces):
        block = piece_ref.shape[1] // 2
        for dc in range(2):
            place = low_ref[0] ^ (2 * m + dc)
            cols = pl.ds(pl.multiple_of(place * block, block), block)
            mixed = piece_ref[:, dc * block : (dc + 1) * block].astype(jnp.float32)
            hidden_ref[:, cols] = (residual_ref[:, cols].astype(jnp.float32) + mixed).astype(
                hidden_ref.dtype
            )
    packed_ref[...] = jnp.dot(
        gather_ref[...], hidden_ref[...], preferred_element_type=jnp.float32
    ).astype(packed_ref.dtype)


def hidden_and_packed(low, gather_matrix, residual_in, pieces):
    vmem = pl.BlockSpec(memory_space=pltpu.VMEM)
    return pl.pallas_call(
        hidden_kernel,
        in_specs=[pl.BlockSpec(memory_space=pltpu.SMEM)] + [vmem] * (2 + len(pieces)),
        out_specs=[vmem, vmem],
        out_shape=[
            jax.ShapeDtypeStruct(residual_in.shape, jnp.bfloat16),
            jax.ShapeDtypeStruct(
                (gather_matrix.shape[0], residual_in.shape[1]), jnp.bfloat16
            ),
        ],
        compiler_params=pltpu.CompilerParams(vmem_limit_bytes=SMALL_VMEM),
        name="hidden_and_packed",
    )(low, gather_matrix, residual_in, *pieces)


def per_device(
    mixer_in,
    gate_in,
    residual_in,
    conv_weight,
    conv_bias,
    state_proj,
    step_proj,
    step_bias,
    decay_rate,
    skip_gain,
    out_proj,
    segment_ids,
    gate_weight,
    up_weight,
    down_weight,
    routes,
    route_weight,
    keep_mask,
):
    tokens = mixer_in.shape[0]
    channels = mixer_in.shape[1]
    groups = lax.axis_size("loop")
    position = lax.axis_index("loop")
    shard = lax.axis_index("tp")
    shards = lax.axis_size("tp")
    low = groups // shards
    first_steps = 3
    first_rows = channels // EIGHTHS * first_steps
    far_first = [across(out_proj[:first_rows], low * high) for high in range(1, shards)]
    conv_taps = conv_weight.shape[0]
    rim_rows = shifted(mixer_in[tokens - (conv_taps - 1) :], "loop", 1)
    extended = jnp.concatenate([rim_rows, mixer_in], axis=0)
    conv_sum = jnp.broadcast_to(conv_bias[None, :], (tokens, channels))
    for offset in range(conv_taps):
        conv_sum = conv_sum + conv_weight[offset][None, :] * extended[
            offset : offset + tokens
        ].astype(jnp.float32)
    conved = jax.nn.silu(conv_sum).astype(jnp.bfloat16)
    block_start = position * tokens
    local_ids = lax.dynamic_slice_in_dim(segment_ids, block_start, tokens)
    before_start = jnp.maximum(block_start - 1, 0)
    before_id = lax.dynamic_slice_in_dim(segment_ids, before_start, 1)
    previous = jnp.where(block_start > 0, before_id, local_ids[:1])
    earlier_ids = jnp.concatenate([previous, local_ids[:-1]])
    kept = (local_ids == earlier_ids).astype(jnp.float32)[:, None]
    projected = summed_over(
        jnp.dot(conved, state_proj, preferred_element_type=jnp.float32), "tp"
    )
    low_rank = projected[:, :RANK].astype(jnp.bfloat16)
    in_gain = projected[:, RANK : RANK + NSTATE]
    out_gain = projected[:, RANK + NSTATE :]
    gain = jnp.broadcast_to(in_gain[:, :, None], (tokens, NSTATE, LANES))
    state_rows = jnp.arange(tokens * NSTATE, dtype=jnp.int32)
    spread = state_rows[None, :] % NSTATE == jnp.arange(NSTATE, dtype=jnp.int32)[:, None]
    pick = jnp.where(
        state_rows[None, :] // NSTATE == jnp.arange(tokens, dtype=jnp.int32)[:, None],
        jnp.dot(
            out_gain.astype(jnp.bfloat16),
            spread.astype(jnp.bfloat16),
            preferred_element_type=jnp.float32,
        ),
        0.0,
    ).astype(jnp.bfloat16)
    step_size, end_state = scan_end(
        low_rank, step_proj, step_bias, decay_rate, conved, gain, kept, groups
    )
    end_state, far_first = lax.optimization_barrier((end_state, far_first))
    ends = lax.all_to_all(end_state, "loop", 0, 0, tiled=True)
    chunk = channels // groups
    own_rates = lax.dynamic_slice_in_dim(decay_rate, position * chunk, chunk, 1)
    carry = lax.all_to_all(carries(ends, own_rates), "loop", 0, 0, tiled=True)
    later_rows, carry = lax.optimization_barrier((out_proj[first_rows:], carry))
    middle_rows = channels // EIGHTHS * 2
    far_middle = [across(later_rows[:middle_rows], low * high) for high in range(1, shards)]
    last_rows, far_middle = lax.optimization_barrier((later_rows[middle_rows:], far_middle))
    far_last = [across(last_rows, low * high) for high in range(1, shards)]
    own_low, own_high = position % low, position // low
    tokens_of = []
    for first, steps in ((0, first_steps), (first_steps, EIGHTHS - first_steps)):
        gated = scan_gated(
            step_size, decay_rate, conved, gain, kept, carry, pick, skip_gain, gate_in, first,
            steps,
        )
        tokens_of.append(
            {m: gated if m == 0 else across(gated, m) for m in (0, 2, 4) if m < low}
        )
    tokens_of = lax.optimization_barrier(tokens_of)
    for got in tokens_of:
        for m in range(6, low, 2):
            one = m & -m
            got[m] = across(got[m ^ one], one) if m != one else across(got[0], m)
    far_last, tokens_of = lax.optimization_barrier((far_last, tokens_of))
    far_later = [jnp.concatenate(parts, axis=0) for parts in zip(far_middle, far_last)]
    all_tokens = [
        jnp.concatenate([got[m] for m in range(0, low, 2)], axis=0) for got in tokens_of
    ]
    blocks = [(out_proj[:first_rows], out_proj[first_rows:])] + list(zip(far_first, far_later))
    mixes = []
    for block in blocks:
        mix = 0.0
        for some_tokens, part in zip(all_tokens, block):
            pair = jnp.concatenate([part, across(part, 1)], axis=1)
            mix = mix + jnp.dot(some_tokens, pair, preferred_element_type=jnp.float32)
        mixes.append(mix)

    def for_shard(t):
        mix = mixes[0]
        for high in range(1, shards):
            mix = jnp.where((own_high ^ t) == high, mixes[high], mix)
        return mix

    mixed_out = for_shard(shard)
    for by in range(1, shards):
        sent = for_shard((shard + by) % shards).astype(jnp.bfloat16)
        mixed_out = mixed_out + rotated(sent, "tp", by).astype(jnp.float32)
    pieces = [mixed_out[:tokens]]
    for k in range(1, low // 2):
        rows_out = mixed_out[k * tokens : (k + 1) * tokens].astype(jnp.bfloat16)
        pieces.append(across(rows_out, 2 * k))
    width = residual_in.shape[1]
    features = width * shards

    members = groups // EXPERTS
    team, member = position // members, position % members
    flat_routes = routes.reshape(-1)
    expert_ids = jnp.arange(EXPERTS, dtype=jnp.int32)
    onehot = (flat_routes[:, None] == expert_ids[None, :]).astype(jnp.int32)
    slot_index = jnp.sum(jnp.cumsum(onehot, axis=0) * onehot, axis=1) - 1
    target = (flat_routes ^ team) * CAP + slot_index
    selector = (jnp.arange(EXPERTS * CAP, dtype=jnp.int32)[:, None] == target[None, :]).astype(
        jnp.float32
    )
    gather_matrix = jnp.sum(selector.reshape(EXPERTS * CAP, tokens, TOPK), axis=2)
    keep_weight = jnp.sum(onehot.astype(jnp.float32) * keep_mask.astype(jnp.float32), axis=1)
    weights = route_weight.reshape(-1) * keep_weight
    weighted = jnp.sum((selector * weights[None, :]).reshape(EXPERTS * CAP, tokens, TOPK), axis=2)
    hidden_in, packed = hidden_and_packed(
        own_low.astype(jnp.int32)[None], gather_matrix.astype(jnp.bfloat16), residual_in, pieces
    )
    packed = packed.reshape(EXPERTS, CAP, width)
    near = EXPERTS // 2
    rows = near * CAP

    def from_member(by):
        pairs = [
            (i, i // members * members + (i + by) % members) for i in range(groups)
        ]
        return lambda x: lax.ppermute(x, "loop", pairs)

    parts = [
        gathered(teams_swapped(packed[first : first + near], first, members), "tp", shard, 1)
        for first in (near, 0)
    ]
    pieces = parts + [from_member(by)(part) for by in range(1, members) for part in parts]
    hidden, outs = raised(
        pieces, gate_weight, up_weight, down_weight, (shard + 1) % shards, width, members
    )

    def member_sum(outs):
        total = outs[0].astype(jnp.float32)
        for by in range(1, members):
            total = total + from_member(members - by)(outs[by]).astype(jnp.float32)
        return total

    def for_shard_of(hidden, t):
        return lowered(hidden, down_weight, t, width, members)

    sent = [member_sum(outs).astype(jnp.bfloat16)] + [
        member_sum(for_shard_of(hidden, (shard + by) % shards)).astype(jnp.bfloat16)
        for by in range(2, shards)
    ]
    hidden, sent = lax.optimization_barrier((hidden, sent))
    far_sums = [rotated(part[:rows], "tp", by) for by, part in enumerate(sent, 1)]
    own_outs = for_shard_of(hidden, shard)
    far_sums, own_outs, near_sent = lax.optimization_barrier(
        (far_sums, own_outs, [part[rows:] for part in sent])
    )
    near_sums = [rotated(part, "tp", by) for by, part in enumerate(near_sent, 1)]
    own_sum = member_sum(own_outs)

    def shared(own, sums):
        share = own
        for part in sums:
            share = share + part.astype(jnp.float32)
        return share.astype(jnp.bfloat16).reshape(near, CAP, width)

    ahead = near // 2
    far_share = shared(own_sum[:rows], far_sums)
    far_ahead = teams_swapped(far_share[:ahead], near, members)
    near_sums, far_ahead = lax.optimization_barrier((near_sums, far_ahead))
    near_share = shared(own_sum[rows:], near_sums)
    back = [
        teams_swapped(near_share, 0, members),
        far_ahead,
        teams_swapped(far_share[ahead:], near + ahead, members),
    ]
    returned = jnp.concatenate(back, axis=0).reshape(EXPERTS * CAP, width)
    expert_sum = jnp.dot(
        weighted.T,
        returned.astype(jnp.float32),
        precision=lax.Precision.HIGHEST,
        preferred_element_type=jnp.float32,
    )
    return (hidden_in.astype(jnp.float32) + expert_sum).astype(jnp.bfloat16)


def solution(mesh):
    return jax.shard_map(
        per_device,
        mesh=mesh,
        in_specs=(
            P("loop", "tp"),
            P("loop", "tp"),
            P("loop", "tp"),
            P(None, "tp"),
            P("tp"),
            P("tp", None),
            P(None, "tp"),
            P("tp"),
            P(None, "tp"),
            P("tp"),
            P("tp", "loop"),
            P(),
            P("loop", None, "tp"),
            P("loop", None, "tp"),
            P("loop", "tp", None),
            P("loop", None),
            P("loop", None),
            P("loop", None),
        ),
        out_specs=P("loop", "tp"),
        check_vma=False,
    )
```

```python
import functools
import math

import jax
import jax.numpy as jnp
from jax import lax
from jax.experimental import pallas as pl
from jax.experimental.pallas import tpu as pltpu
from jax.sharding import PartitionSpec as P

NSTATE = 16
RANK = 256
EXPERTS = 8
TOPK = 2
CAP = 40
LANES = 128
EIGHTHS = 8
SUBLANES = 8
RESET = 1e30
LOG2E = math.log2(math.e)
VMEM = 40 * 1024 * 1024
SMALL_VMEM = 16 * 1024 * 1024


def shifted(x, axis, by):
    size = lax.axis_size(axis)
    pairs = [(i, i + by) for i in range(size) if 0 <= i + by < size]
    return lax.ppermute(x, axis, pairs)


def rotated(x, axis, by):
    size = lax.axis_size(axis)
    return lax.ppermute(x, axis, [(i, (i + by) % size) for i in range(size)])


def scan_end_kernel(
    low_ref, proj_ref, bias_ref, decay_ref, conved_ref, gain_ref, kept_ref,
    step_ref, end_ref, sd_ref, u_ref,
):
    tokens, width = step_ref.shape
    chunk = end_ref.shape[2]
    step = jax.nn.softplus(
        jnp.dot(low_ref[...], proj_ref[...], preferred_element_type=jnp.float32) + bias_ref[...]
    )
    step_ref[...] = step
    sd = jnp.where(kept_ref[...] > 0, step, RESET)
    sd_ref[...] = sd.reshape(sd_ref.shape)
    total = jnp.sum(sd, axis=0, keepdims=True)
    u_ref[...] = (step * conved_ref[...].astype(jnp.float32)).reshape(u_ref.shape)
    cols = [slice(i, i + LANES) for i in range(0, width, LANES)]
    rates = [decay_ref[:, c] * -LOG2E for c in cols]

    def advance(i, state):
        for r in range(SUBLANES):
            gain = gain_ref[i * SUBLANES + r]
            state = tuple(
                jnp.exp2(sd_ref[i, r : r + 1, c] * rate) * h + u_ref[i, r : r + 1, c] * gain
                for c, rate, h in zip(cols, rates, state)
            )
        return state

    zero = tuple(jnp.zeros((NSTATE, LANES), jnp.float32) for _ in cols)
    state = jnp.concatenate(lax.fori_loop(0, tokens // SUBLANES, advance, zero), axis=1)
    high = total.astype(jnp.bfloat16).astype(jnp.float32)
    row = lax.broadcasted_iota(jnp.int32, (NSTATE, width), 0)
    tail = jnp.where(row == 0, high, total - high)
    for k in range(width // chunk):
        part = slice(k * chunk, (k + 1) * chunk)
        end_ref[k, :NSTATE, :] = state[:, part].astype(end_ref.dtype)
        end_ref[k, NSTATE:, :] = tail[:, part].astype(end_ref.dtype)


def carry_kernel(ends_ref, decay_ref, carry_ref):
    rate = decay_ref[...] * -LOG2E
    state = jnp.zeros(rate.shape, jnp.float32)
    for block in range(ends_ref.shape[0]):
        carry_ref[block] = state.astype(carry_ref.dtype)
        tail = ends_ref[block, NSTATE:, :].astype(jnp.float32)
        total = tail[0:1] + tail[1:2]
        end = ends_ref[block, :NSTATE, :].astype(jnp.float32)
        state = jnp.exp2(total * rate) * state + end


def scan_kernel(
    step_ref, decay_ref, conved_ref, gain_ref, kept_ref, carry_ref, pick_ref, skip_ref, gate_ref,
    gated_ref, sd_ref, u_ref, states_ref,
):
    tokens, width = step_ref.shape
    step = step_ref[...]
    conved = conved_ref[...].astype(jnp.float32)
    sd_ref[...] = jnp.where(kept_ref[...] > 0, step, RESET).reshape(sd_ref.shape)
    u_ref[...] = (step * conved).reshape(u_ref.shape)
    cols = [slice(i, i + LANES) for i in range(0, width, LANES)]
    rates = [decay_ref[:, c] * -LOG2E for c in cols]

    def advance(i, state):
        for r in range(SUBLANES):
            gain = gain_ref[i * SUBLANES + r]
            state = tuple(
                jnp.exp2(sd_ref[i, r : r + 1, c] * rate) * h + u_ref[i, r : r + 1, c] * gain
                for c, rate, h in zip(cols, rates, state)
            )
            rows = pl.ds(pl.multiple_of((i * SUBLANES + r) * NSTATE, NSTATE), NSTATE)
            for c, h in zip(cols, state):
                states_ref[rows, c] = h.astype(states_ref.dtype)
        return state

    carry = [carry_ref[k].astype(jnp.float32) for k in range(carry_ref.shape[0])]
    carry = jnp.concatenate(carry, axis=1)
    lax.fori_loop(0, tokens // SUBLANES, advance, tuple(carry[:, c] for c in cols))
    scanned = jnp.dot(pick_ref[...], states_ref[...], preferred_element_type=jnp.float32)
    mixer_y = scanned + skip_ref[...] * conved
    gated_ref[...] = (mixer_y * jax.nn.silu(gate_ref[...].astype(jnp.float32))).astype(
        gated_ref.dtype
    )


def whole(shape):
    return pl.BlockSpec(shape, lambda i: (0,) * len(shape))


def scan_end(low_rank, step_proj, step_bias, decay_rate, conved, gain, kept, groups):
    tokens, channels = conved.shape
    rank = low_rank.shape[1]
    width = min(512, channels)
    chunk = channels // groups
    part = lambda rows: pl.BlockSpec((rows, width), lambda i: (0, i))
    return pl.pallas_call(
        scan_end_kernel,
        grid=(channels // width,),
        in_specs=[
            whole((tokens, rank)), part(rank), part(1), part(NSTATE), part(tokens),
            whole((tokens, NSTATE, LANES)), whole((tokens, 1)),
        ],
        out_specs=[
            part(tokens),
            pl.BlockSpec((width // chunk, 2 * NSTATE, chunk), lambda i: (i, 0, 0)),
        ],
        out_shape=[
            jax.ShapeDtypeStruct((tokens, channels), jnp.float32),
            jax.ShapeDtypeStruct((groups, 2 * NSTATE, chunk), jnp.bfloat16),
        ],
        scratch_shapes=[
            pltpu.VMEM((tokens // SUBLANES, SUBLANES, width), jnp.float32),
            pltpu.VMEM((tokens // SUBLANES, SUBLANES, width), jnp.float32),
        ],
        compiler_params=pltpu.CompilerParams(vmem_limit_bytes=SMALL_VMEM),
        cost_estimate=pl.CostEstimate(
            flops=5 * tokens * NSTATE * channels,
            bytes_accessed=8 * tokens * channels,
            transcendentals=tokens * NSTATE * channels,
        ),
        name="scan_end",
    )(low_rank, step_proj, step_bias[None, :], decay_rate, conved, gain, kept)


def carries(ends, decay_rate):
    groups, _, chunk = ends.shape
    return pl.pallas_call(
        carry_kernel,
        out_shape=jax.ShapeDtypeStruct((groups, NSTATE, chunk), jnp.bfloat16),
        name="carries",
    )(ends, decay_rate)


def scan_gated(step, decay_rate, conved, gain, kept, carry, pick, skip_gain, gate_in, first, steps):
    tokens, width = conved.shape[0], conved.shape[1] // EIGHTHS
    channels = steps * width
    chunk = carry.shape[2]
    part = lambda rows: pl.BlockSpec((rows, width), lambda i: (0, first + i))
    return pl.pallas_call(
        scan_kernel,
        grid=(steps,),
        in_specs=[
            part(tokens), part(NSTATE), part(tokens), whole((tokens, NSTATE, LANES)),
            whole((tokens, 1)),
            pl.BlockSpec((width // chunk, NSTATE, chunk), lambda i: (first + i, 0, 0)),
            whole(pick.shape), part(1), part(tokens),
        ],
        out_specs=pl.BlockSpec((tokens, width), lambda i: (0, i)),
        scratch_shapes=[
            pltpu.VMEM((tokens // SUBLANES, SUBLANES, width), jnp.float32),
            pltpu.VMEM((tokens // SUBLANES, SUBLANES, width), jnp.float32),
            pltpu.VMEM((tokens * NSTATE, width), jnp.bfloat16),
        ],
        out_shape=jax.ShapeDtypeStruct((tokens, channels), jnp.bfloat16),
        compiler_params=pltpu.CompilerParams(vmem_limit_bytes=SMALL_VMEM),
        cost_estimate=pl.CostEstimate(
            flops=7 * tokens * NSTATE * channels,
            bytes_accessed=12 * tokens * channels,
            transcendentals=tokens * NSTATE * channels,
        ),
        name="scan_gated",
    )(step, decay_rate, conved, gain, kept, carry, pick, skip_gain[None, :], gate_in)


def raise_kernel(shard_ref, *refs, pieces, members, steps):
    piece_refs, (gate_ref, up_ref, down_ref, hidden_ref) = refs[:pieces], refs[pieces : pieces + 4]
    out_refs, (rows_ref, all_ref) = refs[pieces + 4 : -2], refs[-2:]
    step = pl.program_id(0)

    @pl.when(step == 0)
    def _():
        for k, piece_ref in enumerate(piece_refs):
            rows = piece_ref.shape[0]
            rows_ref[k * rows : (k + 1) * rows] = piece_ref[...]

    @pl.when(step < steps)
    def _():
        rows = rows_ref[...]
        tile = hidden_ref.shape[1]
        gate = jnp.dot(rows, gate_ref[0], preferred_element_type=jnp.float32)
        up = jnp.dot(rows, up_ref[0], preferred_element_type=jnp.float32)
        hidden = (jax.nn.silu(gate) * up).astype(hidden_ref.dtype)
        hidden_ref[...] = hidden
        all_ref[:, pl.ds(pl.multiple_of(step * tile, tile), tile)] = hidden

    @pl.when(step >= steps)
    def _():
        out = jnp.dot(all_ref[...], down_ref[0], preferred_element_type=jnp.float32)
        for k, out_ref in enumerate(out_refs):
            rows = out_ref.shape[0]
            out_ref[...] = out[k * rows : (k + 1) * rows].astype(out_ref.dtype)


def raised(pieces, gate_weight, up_weight, down_weight, shard, features, members):
    rows, depth = sum(piece.shape[0] for piece in pieces), pieces[0].shape[1]
    width = gate_weight.shape[2]
    tile, out_tile = min(512, width), min(512, features)
    steps, out_steps = width // tile, features // out_tile
    up_at = lambda i: jnp.minimum(i, steps - 1)
    down_at = lambda i: jnp.maximum(i - steps, 0)
    weight = pl.BlockSpec((1, depth, tile), lambda i, t: (0, 0, up_at(i)))
    outs = pl.pallas_call(
        functools.partial(raise_kernel, pieces=len(pieces), members=members, steps=steps),
        grid_spec=pltpu.PrefetchScalarGridSpec(
            num_scalar_prefetch=1,
            grid=(steps + out_steps,),
            in_specs=[pl.BlockSpec(piece.shape, lambda i, t: (0, 0)) for piece in pieces]
            + [
                weight,
                weight,
                pl.BlockSpec(
                    (1, width, out_tile), lambda i, t: (0, 0, t[0] * out_steps + down_at(i))
                ),
            ],
            out_specs=[pl.BlockSpec((rows, tile), lambda i, t: (0, up_at(i)))]
            + [pl.BlockSpec((rows // members, out_tile), lambda i, t: (0, down_at(i)))] * members,
            scratch_shapes=[
                pltpu.VMEM((rows, depth), jnp.bfloat16),
                pltpu.VMEM((rows, width), jnp.bfloat16),
            ],
        ),
        out_shape=[jax.ShapeDtypeStruct((rows, width), jnp.bfloat16)]
        + [jax.ShapeDtypeStruct((rows // members, features), jnp.bfloat16)] * members,
        compiler_params=pltpu.CompilerParams(vmem_limit_bytes=60 * 1024 * 1024),
        cost_estimate=pl.CostEstimate(
            flops=2 * rows * width * (2 * depth + features),
            bytes_accessed=2 * width * (2 * depth + features),
            transcendentals=rows * width,
        ),
        name="raised",
    )(shard.astype(jnp.int32)[None], *pieces, gate_weight, up_weight, down_weight)
    return outs[0], outs[1:]


def lower_kernel(shard_ref, hidden_ref, weight_ref, *out_refs):
    out = jnp.dot(hidden_ref[...], weight_ref[0], preferred_element_type=jnp.float32)
    rows = out_refs[0].shape[0]
    for k, out_ref in enumerate(out_refs):
        out_ref[...] = out[k * rows : (k + 1) * rows].astype(out_ref.dtype)


def lowered(hidden, down_weight, shard, width, members):
    rows, depth = hidden.shape
    tile = min(512, width)
    steps = width // tile
    out = jax.ShapeDtypeStruct((rows // members, width), jnp.bfloat16)
    return pl.pallas_call(
        lower_kernel,
        grid_spec=pltpu.PrefetchScalarGridSpec(
            num_scalar_prefetch=1,
            grid=(steps,),
            in_specs=[
                pl.BlockSpec((rows, depth), lambda i, t: (0, 0)),
                pl.BlockSpec((1, depth, tile), lambda i, t: (0, 0, t[0] * steps + i)),
            ],
            out_specs=[pl.BlockSpec((rows // members, tile), lambda i, t: (0, i))] * members,
        ),
        out_shape=[out] * members,
        compiler_params=pltpu.CompilerParams(vmem_limit_bytes=VMEM),
        cost_estimate=pl.CostEstimate(
            flops=2 * rows * depth * width, bytes_accessed=2 * depth * width, transcendentals=0
        ),
        name="lowered",
    )(shard.astype(jnp.int32)[None], hidden, down_weight)


def summed_over(x, axis):
    total = x
    for by in range(1, lax.axis_size(axis)):
        total = total + rotated(x, axis, by)
    return total


def gathered(x, axis, mine, dim):
    size = lax.axis_size(axis)
    shape = x.shape[:dim] + (size * x.shape[dim],) + x.shape[dim + 1 :]
    out = jnp.zeros(shape, x.dtype)
    out = lax.dynamic_update_slice_in_dim(out, x, mine * x.shape[dim], dim)
    for by in range(1, size):
        source = lax.rem(mine + size - by, size)
        out = lax.dynamic_update_slice_in_dim(
            out, rotated(x, axis, by), source * x.shape[dim], dim
        )
    return out


def across(x, mask):
    return lax.ppermute(x, "loop", [(i, i ^ mask) for i in range(lax.axis_size("loop"))])


def teams_swapped(x, first, members):
    groups = lax.axis_size("loop")
    out = []
    for k in range(x.shape[0]):
        s = first + k
        if s == 0:
            out.append(x[k])
            continue
        pairs = [(i, ((i // members) ^ s) * members + i % members) for i in range(groups)]
        out.append(lax.ppermute(x[k], "loop", pairs))
    return jnp.concatenate(out, axis=0)


def hidden_kernel(low_ref, gather_ref, residual_ref, *refs):
    pieces, (hidden_ref, packed_ref) = refs[:-2], refs[-2:]
    for m, piece_ref in enumerate(pieces):
        block = piece_ref.shape[1] // 2
        for dc in range(2):
            place = low_ref[0] ^ (2 * m + dc)
            cols = pl.ds(pl.multiple_of(place * block, block), block)
            mixed = piece_ref[:, dc * block : (dc + 1) * block].astype(jnp.float32)
            hidden_ref[:, cols] = (residual_ref[:, cols].astype(jnp.float32) + mixed).astype(
                hidden_ref.dtype
            )
    packed_ref[...] = jnp.dot(
        gather_ref[...], hidden_ref[...], preferred_element_type=jnp.float32
    ).astype(packed_ref.dtype)


def hidden_and_packed(low, gather_matrix, residual_in, pieces):
    vmem = pl.BlockSpec(memory_space=pltpu.VMEM)
    return pl.pallas_call(
        hidden_kernel,
        in_specs=[pl.BlockSpec(memory_space=pltpu.SMEM)] + [vmem] * (2 + len(pieces)),
        out_specs=[vmem, vmem],
        out_shape=[
            jax.ShapeDtypeStruct(residual_in.shape, jnp.bfloat16),
            jax.ShapeDtypeStruct(
                (gather_matrix.shape[0], residual_in.shape[1]), jnp.bfloat16
            ),
        ],
        compiler_params=pltpu.CompilerParams(vmem_limit_bytes=SMALL_VMEM),
        name="hidden_and_packed",
    )(low, gather_matrix, residual_in, *pieces)


def per_device(
    mixer_in,
    gate_in,
    residual_in,
    conv_weight,
    conv_bias,
    state_proj,
    step_proj,
    step_bias,
    decay_rate,
    skip_gain,
    out_proj,
    segment_ids,
    gate_weight,
    up_weight,
    down_weight,
    routes,
    route_weight,
    keep_mask,
):
    tokens = mixer_in.shape[0]
    channels = mixer_in.shape[1]
    groups = lax.axis_size("loop")
    position = lax.axis_index("loop")
    shard = lax.axis_index("tp")
    shards = lax.axis_size("tp")
    low = groups // shards
    first_steps = 3
    first_rows = channels // EIGHTHS * first_steps
    far_first = [across(out_proj[:first_rows], low * high) for high in range(1, shards)]
    conv_taps = conv_weight.shape[0]
    rim_rows = shifted(mixer_in[tokens - (conv_taps - 1) :], "loop", 1)
    extended = jnp.concatenate([rim_rows, mixer_in], axis=0)
    conv_sum = jnp.broadcast_to(conv_bias[None, :], (tokens, channels))
    for offset in range(conv_taps):
        conv_sum = conv_sum + conv_weight[offset][None, :] * extended[
            offset : offset + tokens
        ].astype(jnp.float32)
    conved = jax.nn.silu(conv_sum).astype(jnp.bfloat16)
    block_start = position * tokens
    local_ids = lax.dynamic_slice_in_dim(segment_ids, block_start, tokens)
    before_start = jnp.maximum(block_start - 1, 0)
    before_id = lax.dynamic_slice_in_dim(segment_ids, before_start, 1)
    previous = jnp.where(block_start > 0, before_id, local_ids[:1])
    earlier_ids = jnp.concatenate([previous, local_ids[:-1]])
    kept = (local_ids == earlier_ids).astype(jnp.float32)[:, None]
    projected = summed_over(
        jnp.dot(conved, state_proj, preferred_element_type=jnp.float32), "tp"
    )
    low_rank = projected[:, :RANK].astype(jnp.bfloat16)
    in_gain = projected[:, RANK : RANK + NSTATE]
    out_gain = projected[:, RANK + NSTATE :]
    gain = jnp.broadcast_to(in_gain[:, :, None], (tokens, NSTATE, LANES))
    state_rows = jnp.arange(tokens * NSTATE, dtype=jnp.int32)
    spread = state_rows[None, :] % NSTATE == jnp.arange(NSTATE, dtype=jnp.int32)[:, None]
    pick = jnp.where(
        state_rows[None, :] // NSTATE == jnp.arange(tokens, dtype=jnp.int32)[:, None],
        jnp.dot(
            out_gain.astype(jnp.bfloat16),
            spread.astype(jnp.bfloat16),
            preferred_element_type=jnp.float32,
        ),
        0.0,
    ).astype(jnp.bfloat16)
    step_size, end_state = scan_end(
        low_rank, step_proj, step_bias, decay_rate, conved, gain, kept, groups
    )
    end_state, far_first = lax.optimization_barrier((end_state, far_first))
    ends = lax.all_to_all(end_state, "loop", 0, 0, tiled=True)
    chunk = channels // groups
    own_rates = lax.dynamic_slice_in_dim(decay_rate, position * chunk, chunk, 1)
    carry = lax.all_to_all(carries(ends, own_rates), "loop", 0, 0, tiled=True)
    later_rows, carry = lax.optimization_barrier((out_proj[first_rows:], carry))
    middle_rows = channels // EIGHTHS * 2
    far_middle = [across(later_rows[:middle_rows], low * high) for high in range(1, shards)]
    last_rows, far_middle = lax.optimization_barrier((later_rows[middle_rows:], far_middle))
    far_last = [across(last_rows, low * high) for high in range(1, shards)]
    own_low, own_high = position % low, position // low
    tokens_of = []
    for first, steps in ((0, first_steps), (first_steps, EIGHTHS - first_steps)):
        gated = scan_gated(
            step_size, decay_rate, conved, gain, kept, carry, pick, skip_gain, gate_in, first,
            steps,
        )
        tokens_of.append({0: gated})
    def joined(got, more):
        for m in range(6, low, 2):
            one = m & -m
            more[m] = across(got[m ^ one], one) if m != one else across(got[0], m)

    first, later = tokens_of
    for m in (2, 4):
        if m < low:
            later[m] = across(later[0], m)
    later, first = lax.optimization_barrier((later, first))
    for m in (2, 4):
        if m < low:
            first[m] = across(first[0], m)
    joined(later, later)
    far_last, later, first = lax.optimization_barrier((far_last, later, first))
    far_later = [jnp.concatenate(parts, axis=0) for parts in zip(far_middle, far_last)]
    joined(first, first)
    tokens_of = [first, later]
    all_tokens = [
        jnp.concatenate([got[m] for m in range(0, low, 2)], axis=0) for got in tokens_of
    ]
    blocks = [(out_proj[:first_rows], out_proj[first_rows:])] + list(zip(far_first, far_later))
    mixes = []
    for block in blocks:
        mix = 0.0
        for some_tokens, part in zip(all_tokens, block):
            pair = jnp.concatenate([part, across(part, 1)], axis=1)
            mix = mix + jnp.dot(some_tokens, pair, preferred_element_type=jnp.float32)
        mixes.append(mix)

    def for_shard(t):
        mix = mixes[0]
        for high in range(1, shards):
            mix = jnp.where((own_high ^ t) == high, mixes[high], mix)
        return mix

    mixed_out = for_shard(shard)
    for by in range(1, shards):
        sent = for_shard((shard + by) % shards).astype(jnp.bfloat16)
        mixed_out = mixed_out + rotated(sent, "tp", by).astype(jnp.float32)
    pieces = [mixed_out[:tokens]]
    for k in range(1, low // 2):
        rows_out = mixed_out[k * tokens : (k + 1) * tokens].astype(jnp.bfloat16)
        pieces.append(across(rows_out, 2 * k))
    width = residual_in.shape[1]
    features = width * shards

    members = groups // EXPERTS
    team, member = position // members, position % members
    flat_routes = routes.reshape(-1)
    expert_ids = jnp.arange(EXPERTS, dtype=jnp.int32)
    onehot = (flat_routes[:, None] == expert_ids[None, :]).astype(jnp.int32)
    slot_index = jnp.sum(jnp.cumsum(onehot, axis=0) * onehot, axis=1) - 1
    target = (flat_routes ^ team) * CAP + slot_index
    selector = (jnp.arange(EXPERTS * CAP, dtype=jnp.int32)[:, None] == target[None, :]).astype(
        jnp.float32
    )
    gather_matrix = jnp.sum(selector.reshape(EXPERTS * CAP, tokens, TOPK), axis=2)
    keep_weight = jnp.sum(onehot.astype(jnp.float32) * keep_mask.astype(jnp.float32), axis=1)
    weights = route_weight.reshape(-1) * keep_weight
    weighted = jnp.sum((selector * weights[None, :]).reshape(EXPERTS * CAP, tokens, TOPK), axis=2)
    hidden_in, packed = hidden_and_packed(
        own_low.astype(jnp.int32)[None], gather_matrix.astype(jnp.bfloat16), residual_in, pieces
    )
    packed = packed.reshape(EXPERTS, CAP, width)
    near = EXPERTS // 2
    rows = near * CAP

    def from_member(by):
        pairs = [
            (i, i // members * members + (i + by) % members) for i in range(groups)
        ]
        return lambda x: lax.ppermute(x, "loop", pairs)

    parts = [
        gathered(teams_swapped(packed[first : first + near], first, members), "tp", shard, 1)
        for first in (0, near)
    ]
    pieces = parts + [from_member(by)(part) for by in range(1, members) for part in parts]
    hidden, outs = raised(
        pieces, gate_weight, up_weight, down_weight, (shard + 1) % shards, width, members
    )

    def member_sum(outs):
        total = outs[0].astype(jnp.float32)
        for by in range(1, members):
            total = total + from_member(members - by)(outs[by]).astype(jnp.float32)
        return total

    def for_shard_of(hidden, t):
        return lowered(hidden, down_weight, t, width, members)

    sent = [member_sum(outs).astype(jnp.bfloat16)] + [
        member_sum(for_shard_of(hidden, (shard + by) % shards)).astype(jnp.bfloat16)
        for by in range(2, shards)
    ]
    hidden, sent = lax.optimization_barrier((hidden, sent))
    far_sums = [rotated(part[rows:], "tp", by) for by, part in enumerate(sent, 1)]
    own_outs = for_shard_of(hidden, shard)
    far_sums, own_outs, near_sent = lax.optimization_barrier(
        (far_sums, own_outs, [part[:rows] for part in sent])
    )
    near_sums = [rotated(part, "tp", by) for by, part in enumerate(near_sent, 1)]
    own_sum = member_sum(own_outs)

    def shared(own, sums):
        share = own
        for part in sums:
            share = share + part.astype(jnp.float32)
        return share.astype(jnp.bfloat16).reshape(near, CAP, width)

    ahead = near // 2
    far_share = shared(own_sum[rows:], far_sums)
    far_ahead = teams_swapped(far_share[:ahead], near, members)
    near_sums, far_ahead = lax.optimization_barrier((near_sums, far_ahead))
    near_share = shared(own_sum[:rows], near_sums)
    back = [
        teams_swapped(near_share, 0, members),
        far_ahead,
        teams_swapped(far_share[ahead:], near + ahead, members),
    ]
    returned = jnp.concatenate(back, axis=0).reshape(EXPERTS * CAP, width)
    expert_sum = jnp.dot(
        weighted.T,
        returned.astype(jnp.float32),
        precision=lax.Precision.HIGHEST,
        preferred_element_type=jnp.float32,
    )
    return (hidden_in.astype(jnp.float32) + expert_sum).astype(jnp.bfloat16)


def solution(mesh):
    return jax.shard_map(
        per_device,
        mesh=mesh,
        in_specs=(
            P("loop", "tp"),
            P("loop", "tp"),
            P("loop", "tp"),
            P(None, "tp"),
            P("tp"),
            P("tp", None),
            P(None, "tp"),
            P("tp"),
            P(None, "tp"),
            P("tp"),
            P("tp", "loop"),
            P(),
            P("loop", None, "tp"),
            P("loop", None, "tp"),
            P("loop", "tp", None),
            P("loop", None),
            P("loop", None),
            P("loop", None),
        ),
        out_specs=P("loop", "tp"),
        check_vma=False,
    )
```

```python
import functools
import math

import jax
import jax.numpy as jnp
from jax import lax
from jax.experimental import pallas as pl
from jax.experimental.pallas import tpu as pltpu
from jax.sharding import PartitionSpec as P

NSTATE = 16
RANK = 256
EXPERTS = 8
TOPK = 2
CAP = 40
LANES = 128
EIGHTHS = 8
SUBLANES = 8
RESET = 1e30
LOG2E = math.log2(math.e)
VMEM = 40 * 1024 * 1024
SMALL_VMEM = 16 * 1024 * 1024


def shifted(x, axis, by):
    size = lax.axis_size(axis)
    pairs = [(i, i + by) for i in range(size) if 0 <= i + by < size]
    return lax.ppermute(x, axis, pairs)


def rotated(x, axis, by):
    size = lax.axis_size(axis)
    return lax.ppermute(x, axis, [(i, (i + by) % size) for i in range(size)])


def scan_end_kernel(
    low_ref, proj_ref, bias_ref, decay_ref, conved_ref, gain_ref, kept_ref,
    step_ref, end_ref, sd_ref, u_ref,
):
    tokens, width = step_ref.shape
    chunk = end_ref.shape[2]
    step = jax.nn.softplus(
        jnp.dot(low_ref[...], proj_ref[...], preferred_element_type=jnp.float32) + bias_ref[...]
    )
    step_ref[...] = step
    sd = jnp.where(kept_ref[...] > 0, step, RESET)
    sd_ref[...] = sd.reshape(sd_ref.shape)
    total = jnp.sum(sd, axis=0, keepdims=True)
    u_ref[...] = (step * conved_ref[...].astype(jnp.float32)).reshape(u_ref.shape)
    cols = [slice(i, i + LANES) for i in range(0, width, LANES)]
    rates = [decay_ref[:, c] * -LOG2E for c in cols]

    def advance(i, state):
        for r in range(SUBLANES):
            gain = gain_ref[i * SUBLANES + r]
            state = tuple(
                jnp.exp2(sd_ref[i, r : r + 1, c] * rate) * h + u_ref[i, r : r + 1, c] * gain
                for c, rate, h in zip(cols, rates, state)
            )
        return state

    zero = tuple(jnp.zeros((NSTATE, LANES), jnp.float32) for _ in cols)
    state = jnp.concatenate(lax.fori_loop(0, tokens // SUBLANES, advance, zero), axis=1)
    high = total.astype(jnp.bfloat16).astype(jnp.float32)
    row = lax.broadcasted_iota(jnp.int32, (NSTATE, width), 0)
    tail = jnp.where(row == 0, high, total - high)
    for k in range(width // chunk):
        part = slice(k * chunk, (k + 1) * chunk)
        end_ref[k, :NSTATE, :] = state[:, part].astype(end_ref.dtype)
        end_ref[k, NSTATE:, :] = tail[:, part].astype(end_ref.dtype)


def carry_kernel(ends_ref, decay_ref, carry_ref):
    rate = decay_ref[...] * -LOG2E
    state = jnp.zeros(rate.shape, jnp.float32)
    for block in range(ends_ref.shape[0]):
        carry_ref[block] = state.astype(carry_ref.dtype)
        tail = ends_ref[block, NSTATE:, :].astype(jnp.float32)
        total = tail[0:1] + tail[1:2]
        end = ends_ref[block, :NSTATE, :].astype(jnp.float32)
        state = jnp.exp2(total * rate) * state + end


def scan_kernel(
    step_ref, decay_ref, conved_ref, gain_ref, kept_ref, carry_ref, pick_ref, skip_ref, gate_ref,
    gated_ref, sd_ref, u_ref, states_ref,
):
    tokens, width = step_ref.shape
    step = step_ref[...]
    conved = conved_ref[...].astype(jnp.float32)
    sd_ref[...] = jnp.where(kept_ref[...] > 0, step, RESET).reshape(sd_ref.shape)
    u_ref[...] = (step * conved).reshape(u_ref.shape)
    cols = [slice(i, i + LANES) for i in range(0, width, LANES)]
    rates = [decay_ref[:, c] * -LOG2E for c in cols]

    def advance(i, state):
        for r in range(SUBLANES):
            gain = gain_ref[i * SUBLANES + r]
            state = tuple(
                jnp.exp2(sd_ref[i, r : r + 1, c] * rate) * h + u_ref[i, r : r + 1, c] * gain
                for c, rate, h in zip(cols, rates, state)
            )
            rows = pl.ds(pl.multiple_of((i * SUBLANES + r) * NSTATE, NSTATE), NSTATE)
            for c, h in zip(cols, state):
                states_ref[rows, c] = h.astype(states_ref.dtype)
        return state

    carry = [carry_ref[k].astype(jnp.float32) for k in range(carry_ref.shape[0])]
    carry = jnp.concatenate(carry, axis=1)
    lax.fori_loop(0, tokens // SUBLANES, advance, tuple(carry[:, c] for c in cols))
    scanned = jnp.dot(pick_ref[...], states_ref[...], preferred_element_type=jnp.float32)
    mixer_y = scanned + skip_ref[...] * conved
    gated_ref[...] = (mixer_y * jax.nn.silu(gate_ref[...].astype(jnp.float32))).astype(
        gated_ref.dtype
    )


def whole(shape):
    return pl.BlockSpec(shape, lambda i: (0,) * len(shape))


def scan_end(low_rank, step_proj, step_bias, decay_rate, conved, gain, kept, groups):
    tokens, channels = conved.shape
    rank = low_rank.shape[1]
    width = min(512, channels)
    chunk = channels // groups
    part = lambda rows: pl.BlockSpec((rows, width), lambda i: (0, i))
    return pl.pallas_call(
        scan_end_kernel,
        grid=(channels // width,),
        in_specs=[
            whole((tokens, rank)), part(rank), part(1), part(NSTATE), part(tokens),
            whole((tokens, NSTATE, LANES)), whole((tokens, 1)),
        ],
        out_specs=[
            part(tokens),
            pl.BlockSpec((width // chunk, 2 * NSTATE, chunk), lambda i: (i, 0, 0)),
        ],
        out_shape=[
            jax.ShapeDtypeStruct((tokens, channels), jnp.float32),
            jax.ShapeDtypeStruct((groups, 2 * NSTATE, chunk), jnp.bfloat16),
        ],
        scratch_shapes=[
            pltpu.VMEM((tokens // SUBLANES, SUBLANES, width), jnp.float32),
            pltpu.VMEM((tokens // SUBLANES, SUBLANES, width), jnp.float32),
        ],
        compiler_params=pltpu.CompilerParams(vmem_limit_bytes=SMALL_VMEM),
        cost_estimate=pl.CostEstimate(
            flops=5 * tokens * NSTATE * channels,
            bytes_accessed=8 * tokens * channels,
            transcendentals=tokens * NSTATE * channels,
        ),
        name="scan_end",
    )(low_rank, step_proj, step_bias[None, :], decay_rate, conved, gain, kept)


def carries(ends, decay_rate):
    groups, _, chunk = ends.shape
    return pl.pallas_call(
        carry_kernel,
        out_shape=jax.ShapeDtypeStruct((groups, NSTATE, chunk), jnp.bfloat16),
        name="carries",
    )(ends, decay_rate)


def scan_gated(step, decay_rate, conved, gain, kept, carry, pick, skip_gain, gate_in, first, steps):
    tokens, width = conved.shape[0], conved.shape[1] // EIGHTHS
    channels = steps * width
    chunk = carry.shape[2]
    part = lambda rows: pl.BlockSpec((rows, width), lambda i: (0, first + i))
    return pl.pallas_call(
        scan_kernel,
        grid=(steps,),
        in_specs=[
            part(tokens), part(NSTATE), part(tokens), whole((tokens, NSTATE, LANES)),
            whole((tokens, 1)),
            pl.BlockSpec((width // chunk, NSTATE, chunk), lambda i: (first + i, 0, 0)),
            whole(pick.shape), part(1), part(tokens),
        ],
        out_specs=pl.BlockSpec((tokens, width), lambda i: (0, i)),
        scratch_shapes=[
            pltpu.VMEM((tokens // SUBLANES, SUBLANES, width), jnp.float32),
            pltpu.VMEM((tokens // SUBLANES, SUBLANES, width), jnp.float32),
            pltpu.VMEM((tokens * NSTATE, width), jnp.bfloat16),
        ],
        out_shape=jax.ShapeDtypeStruct((tokens, channels), jnp.bfloat16),
        compiler_params=pltpu.CompilerParams(vmem_limit_bytes=SMALL_VMEM),
        cost_estimate=pl.CostEstimate(
            flops=7 * tokens * NSTATE * channels,
            bytes_accessed=12 * tokens * channels,
            transcendentals=tokens * NSTATE * channels,
        ),
        name="scan_gated",
    )(step, decay_rate, conved, gain, kept, carry, pick, skip_gain[None, :], gate_in)


def raise_kernel(shard_ref, *refs, pieces, members, steps):
    piece_refs, (gate_ref, up_ref, down_ref, hidden_ref) = refs[:pieces], refs[pieces : pieces + 4]
    out_refs, (rows_ref, all_ref) = refs[pieces + 4 : -2], refs[-2:]
    step = pl.program_id(0)

    @pl.when(step == 0)
    def _():
        for k, piece_ref in enumerate(piece_refs):
            rows = piece_ref.shape[0]
            rows_ref[k * rows : (k + 1) * rows] = piece_ref[...]

    @pl.when(step < steps)
    def _():
        rows = rows_ref[...]
        tile = hidden_ref.shape[1]
        gate = jnp.dot(rows, gate_ref[0], preferred_element_type=jnp.float32)
        up = jnp.dot(rows, up_ref[0], preferred_element_type=jnp.float32)
        hidden = (jax.nn.silu(gate) * up).astype(hidden_ref.dtype)
        hidden_ref[...] = hidden
        all_ref[:, pl.ds(pl.multiple_of(step * tile, tile), tile)] = hidden

    @pl.when(step >= steps)
    def _():
        out = jnp.dot(all_ref[...], down_ref[0], preferred_element_type=jnp.float32)
        for k, out_ref in enumerate(out_refs):
            rows = out_ref.shape[0]
            out_ref[...] = out[k * rows : (k + 1) * rows].astype(out_ref.dtype)


def raised(pieces, gate_weight, up_weight, down_weight, shard, features, members):
    rows, depth = sum(piece.shape[0] for piece in pieces), pieces[0].shape[1]
    width = gate_weight.shape[2]
    tile, out_tile = min(512, width), min(512, features)
    steps, out_steps = width // tile, features // out_tile
    up_at = lambda i: jnp.minimum(i, steps - 1)
    down_at = lambda i: jnp.maximum(i - steps, 0)
    weight = pl.BlockSpec((1, depth, tile), lambda i, t: (0, 0, up_at(i)))
    outs = pl.pallas_call(
        functools.partial(raise_kernel, pieces=len(pieces), members=members, steps=steps),
        grid_spec=pltpu.PrefetchScalarGridSpec(
            num_scalar_prefetch=1,
            grid=(steps + out_steps,),
            in_specs=[pl.BlockSpec(piece.shape, lambda i, t: (0, 0)) for piece in pieces]
            + [
                weight,
                weight,
                pl.BlockSpec(
                    (1, width, out_tile), lambda i, t: (0, 0, t[0] * out_steps + down_at(i))
                ),
            ],
            out_specs=[pl.BlockSpec((rows, tile), lambda i, t: (0, up_at(i)))]
            + [pl.BlockSpec((rows // members, out_tile), lambda i, t: (0, down_at(i)))] * members,
            scratch_shapes=[
                pltpu.VMEM((rows, depth), jnp.bfloat16),
                pltpu.VMEM((rows, width), jnp.bfloat16),
            ],
        ),
        out_shape=[jax.ShapeDtypeStruct((rows, width), jnp.bfloat16)]
        + [jax.ShapeDtypeStruct((rows // members, features), jnp.bfloat16)] * members,
        compiler_params=pltpu.CompilerParams(vmem_limit_bytes=60 * 1024 * 1024),
        cost_estimate=pl.CostEstimate(
            flops=2 * rows * width * (2 * depth + features),
            bytes_accessed=2 * width * (2 * depth + features),
            transcendentals=rows * width,
        ),
        name="raised",
    )(shard.astype(jnp.int32)[None], *pieces, gate_weight, up_weight, down_weight)
    return outs[0], outs[1:]


def lower_kernel(shard_ref, hidden_ref, weight_ref, *out_refs):
    out = jnp.dot(hidden_ref[...], weight_ref[0], preferred_element_type=jnp.float32)
    rows = out_refs[0].shape[0]
    for k, out_ref in enumerate(out_refs):
        out_ref[...] = out[k * rows : (k + 1) * rows].astype(out_ref.dtype)


def lowered(hidden, down_weight, shard, width, members):
    rows, depth = hidden.shape
    tile = min(512, width)
    steps = width // tile
    out = jax.ShapeDtypeStruct((rows // members, width), jnp.bfloat16)
    return pl.pallas_call(
        lower_kernel,
        grid_spec=pltpu.PrefetchScalarGridSpec(
            num_scalar_prefetch=1,
            grid=(steps,),
            in_specs=[
                pl.BlockSpec((rows, depth), lambda i, t: (0, 0)),
                pl.BlockSpec((1, depth, tile), lambda i, t: (0, 0, t[0] * steps + i)),
            ],
            out_specs=[pl.BlockSpec((rows // members, tile), lambda i, t: (0, i))] * members,
        ),
        out_shape=[out] * members,
        compiler_params=pltpu.CompilerParams(vmem_limit_bytes=VMEM),
        cost_estimate=pl.CostEstimate(
            flops=2 * rows * depth * width, bytes_accessed=2 * depth * width, transcendentals=0
        ),
        name="lowered",
    )(shard.astype(jnp.int32)[None], hidden, down_weight)


def summed_over(x, axis):
    total = x
    for by in range(1, lax.axis_size(axis)):
        total = total + rotated(x, axis, by)
    return total


def gathered(x, axis, mine, dim):
    size = lax.axis_size(axis)
    shape = x.shape[:dim] + (size * x.shape[dim],) + x.shape[dim + 1 :]
    out = jnp.zeros(shape, x.dtype)
    out = lax.dynamic_update_slice_in_dim(out, x, mine * x.shape[dim], dim)
    for by in range(1, size):
        source = lax.rem(mine + size - by, size)
        out = lax.dynamic_update_slice_in_dim(
            out, rotated(x, axis, by), source * x.shape[dim], dim
        )
    return out


def across(x, mask):
    return lax.ppermute(x, "loop", [(i, i ^ mask) for i in range(lax.axis_size("loop"))])


def teams_swapped(x, first, members):
    groups = lax.axis_size("loop")
    out = []
    for k in range(x.shape[0]):
        s = first + k
        if s == 0:
            out.append(x[k])
            continue
        pairs = [(i, ((i // members) ^ s) * members + i % members) for i in range(groups)]
        out.append(lax.ppermute(x[k], "loop", pairs))
    return jnp.concatenate(out, axis=0)


def hidden_kernel(low_ref, gather_ref, residual_ref, *refs):
    pieces, (hidden_ref, packed_ref) = refs[:-2], refs[-2:]
    for m, piece_ref in enumerate(pieces):
        block = piece_ref.shape[1] // 2
        for dc in range(2):
            place = low_ref[0] ^ (2 * m + dc)
            cols = pl.ds(pl.multiple_of(place * block, block), block)
            mixed = piece_ref[:, dc * block : (dc + 1) * block].astype(jnp.float32)
            hidden_ref[:, cols] = (residual_ref[:, cols].astype(jnp.float32) + mixed).astype(
                hidden_ref.dtype
            )
    packed_ref[...] = jnp.dot(
        gather_ref[...], hidden_ref[...], preferred_element_type=jnp.float32
    ).astype(packed_ref.dtype)


def hidden_and_packed(low, gather_matrix, residual_in, pieces):
    vmem = pl.BlockSpec(memory_space=pltpu.VMEM)
    return pl.pallas_call(
        hidden_kernel,
        in_specs=[pl.BlockSpec(memory_space=pltpu.SMEM)] + [vmem] * (2 + len(pieces)),
        out_specs=[vmem, vmem],
        out_shape=[
            jax.ShapeDtypeStruct(residual_in.shape, jnp.bfloat16),
            jax.ShapeDtypeStruct(
                (gather_matrix.shape[0], residual_in.shape[1]), jnp.bfloat16
            ),
        ],
        compiler_params=pltpu.CompilerParams(vmem_limit_bytes=SMALL_VMEM),
        name="hidden_and_packed",
    )(low, gather_matrix, residual_in, *pieces)


def per_device(
    mixer_in,
    gate_in,
    residual_in,
    conv_weight,
    conv_bias,
    state_proj,
    step_proj,
    step_bias,
    decay_rate,
    skip_gain,
    out_proj,
    segment_ids,
    gate_weight,
    up_weight,
    down_weight,
    routes,
    route_weight,
    keep_mask,
):
    tokens = mixer_in.shape[0]
    channels = mixer_in.shape[1]
    groups = lax.axis_size("loop")
    position = lax.axis_index("loop")
    shard = lax.axis_index("tp")
    shards = lax.axis_size("tp")
    low = groups // shards
    first_steps = 2
    first_rows = channels // EIGHTHS * first_steps
    far_first = [across(out_proj[:first_rows], low * high) for high in range(1, shards)]
    conv_taps = conv_weight.shape[0]
    rim_rows = shifted(mixer_in[tokens - (conv_taps - 1) :], "loop", 1)
    extended = jnp.concatenate([rim_rows, mixer_in], axis=0)
    conv_sum = jnp.broadcast_to(conv_bias[None, :], (tokens, channels))
    for offset in range(conv_taps):
        conv_sum = conv_sum + conv_weight[offset][None, :] * extended[
            offset : offset + tokens
        ].astype(jnp.float32)
    conved = jax.nn.silu(conv_sum).astype(jnp.bfloat16)
    block_start = position * tokens
    local_ids = lax.dynamic_slice_in_dim(segment_ids, block_start, tokens)
    before_start = jnp.maximum(block_start - 1, 0)
    before_id = lax.dynamic_slice_in_dim(segment_ids, before_start, 1)
    previous = jnp.where(block_start > 0, before_id, local_ids[:1])
    earlier_ids = jnp.concatenate([previous, local_ids[:-1]])
    kept = (local_ids == earlier_ids).astype(jnp.float32)[:, None]
    projected = summed_over(
        jnp.dot(conved, state_proj, preferred_element_type=jnp.float32), "tp"
    )
    low_rank = projected[:, :RANK].astype(jnp.bfloat16)
    in_gain = projected[:, RANK : RANK + NSTATE]
    out_gain = projected[:, RANK + NSTATE :]
    gain = jnp.broadcast_to(in_gain[:, :, None], (tokens, NSTATE, LANES))
    state_rows = jnp.arange(tokens * NSTATE, dtype=jnp.int32)
    spread = state_rows[None, :] % NSTATE == jnp.arange(NSTATE, dtype=jnp.int32)[:, None]
    pick = jnp.where(
        state_rows[None, :] // NSTATE == jnp.arange(tokens, dtype=jnp.int32)[:, None],
        jnp.dot(
            out_gain.astype(jnp.bfloat16),
            spread.astype(jnp.bfloat16),
            preferred_element_type=jnp.float32,
        ),
        0.0,
    ).astype(jnp.bfloat16)
    step_size, end_state = scan_end(
        low_rank, step_proj, step_bias, decay_rate, conved, gain, kept, groups
    )
    end_state, far_first = lax.optimization_barrier((end_state, far_first))
    ends = lax.all_to_all(end_state, "loop", 0, 0, tiled=True)
    chunk = channels // groups
    own_rates = lax.dynamic_slice_in_dim(decay_rate, position * chunk, chunk, 1)
    carry = lax.all_to_all(carries(ends, own_rates), "loop", 0, 0, tiled=True)
    later_rows, carry = lax.optimization_barrier((out_proj[first_rows:], carry))
    middle_rows = channels // EIGHTHS * 2
    far_middle = [across(later_rows[:middle_rows], low * high) for high in range(1, shards)]
    last_rows, far_middle = lax.optimization_barrier((later_rows[middle_rows:], far_middle))
    far_last = [across(last_rows, low * high) for high in range(1, shards)]
    own_low, own_high = position % low, position // low
    tokens_of = []
    for first, steps in ((0, first_steps), (first_steps, EIGHTHS - first_steps)):
        gated = scan_gated(
            step_size, decay_rate, conved, gain, kept, carry, pick, skip_gain, gate_in, first,
            steps,
        )
        tokens_of.append({0: gated})
    def joined(got, more):
        for m in range(6, low, 2):
            one = m & -m
            more[m] = across(got[m ^ one], one) if m != one else across(got[0], m)

    first, later = tokens_of
    for m in (2, 4):
        if m < low:
            later[m] = across(later[0], m)
    if low > 2:
        first[2] = across(first[0], 2)
    later, first = lax.optimization_barrier((later, first))
    if low > 4:
        first[4] = across(first[0], 4)
    joined(later, later)
    far_last, later, first = lax.optimization_barrier((far_last, later, first))
    far_later = [jnp.concatenate(parts, axis=0) for parts in zip(far_middle, far_last)]
    joined(first, first)
    tokens_of = [first, later]
    all_tokens = [
        jnp.concatenate([got[m] for m in range(0, low, 2)], axis=0) for got in tokens_of
    ]
    blocks = [(out_proj[:first_rows], out_proj[first_rows:])] + list(zip(far_first, far_later))
    mixes = []
    for block in blocks:
        mix = 0.0
        for some_tokens, part in zip(all_tokens, block):
            pair = jnp.concatenate([part, across(part, 1)], axis=1)
            mix = mix + jnp.dot(some_tokens, pair, preferred_element_type=jnp.float32)
        mixes.append(mix)

    def for_shard(t):
        mix = mixes[0]
        for high in range(1, shards):
            mix = jnp.where((own_high ^ t) == high, mixes[high], mix)
        return mix

    mixed_out = for_shard(shard)
    for by in range(1, shards):
        sent = for_shard((shard + by) % shards).astype(jnp.bfloat16)
        mixed_out = mixed_out + rotated(sent, "tp", by).astype(jnp.float32)
    pieces = [mixed_out[:tokens]]
    for k in range(1, low // 2):
        rows_out = mixed_out[k * tokens : (k + 1) * tokens].astype(jnp.bfloat16)
        pieces.append(across(rows_out, 2 * k))
    width = residual_in.shape[1]
    features = width * shards

    members = groups // EXPERTS
    team, member = position // members, position % members
    flat_routes = routes.reshape(-1)
    expert_ids = jnp.arange(EXPERTS, dtype=jnp.int32)
    onehot = (flat_routes[:, None] == expert_ids[None, :]).astype(jnp.int32)
    slot_index = jnp.sum(jnp.cumsum(onehot, axis=0) * onehot, axis=1) - 1
    target = (flat_routes ^ team) * CAP + slot_index
    selector = (jnp.arange(EXPERTS * CAP, dtype=jnp.int32)[:, None] == target[None, :]).astype(
        jnp.float32
    )
    gather_matrix = jnp.sum(selector.reshape(EXPERTS * CAP, tokens, TOPK), axis=2)
    keep_weight = jnp.sum(onehot.astype(jnp.float32) * keep_mask.astype(jnp.float32), axis=1)
    weights = route_weight.reshape(-1) * keep_weight
    weighted = jnp.sum((selector * weights[None, :]).reshape(EXPERTS * CAP, tokens, TOPK), axis=2)
    hidden_in, packed = hidden_and_packed(
        own_low.astype(jnp.int32)[None], gather_matrix.astype(jnp.bfloat16), residual_in, pieces
    )
    packed = packed.reshape(EXPERTS, CAP, width)
    near = EXPERTS // 2
    rows = near * CAP

    def from_member(by):
        pairs = [
            (i, i // members * members + (i + by) % members) for i in range(groups)
        ]
        return lambda x: lax.ppermute(x, "loop", pairs)

    parts = [
        gathered(teams_swapped(packed[first : first + near], first, members), "tp", shard, 1)
        for first in (0, near)
    ]
    pieces = parts + [from_member(by)(part) for by in range(1, members) for part in parts]
    hidden, outs = raised(
        pieces, gate_weight, up_weight, down_weight, (shard + 1) % shards, width, members
    )

    def member_sum(outs):
        total = outs[0].astype(jnp.float32)
        for by in range(1, members):
            total = total + from_member(members - by)(outs[by]).astype(jnp.float32)
        return total

    def for_shard_of(hidden, t):
        return lowered(hidden, down_weight, t, width, members)

    sent = [member_sum(outs).astype(jnp.bfloat16)] + [
        member_sum(for_shard_of(hidden, (shard + by) % shards)).astype(jnp.bfloat16)
        for by in range(2, shards)
    ]
    hidden, sent = lax.optimization_barrier((hidden, sent))
    far_sums = [rotated(part[rows:], "tp", by) for by, part in enumerate(sent, 1)]
    own_outs = for_shard_of(hidden, shard)
    far_sums, own_outs, near_sent = lax.optimization_barrier(
        (far_sums, own_outs, [part[:rows] for part in sent])
    )
    near_sums = [rotated(part, "tp", by) for by, part in enumerate(near_sent, 1)]
    own_sum = member_sum(own_outs)

    def shared(own, sums):
        share = own
        for part in sums:
            share = share + part.astype(jnp.float32)
        return share.astype(jnp.bfloat16).reshape(near, CAP, width)

    ahead = near // 2
    far_share = shared(own_sum[rows:], far_sums)
    far_ahead = teams_swapped(far_share[:ahead], near, members)
    near_sums, far_ahead = lax.optimization_barrier((near_sums, far_ahead))
    near_share = shared(own_sum[:rows], near_sums)
    back = [
        teams_swapped(near_share, 0, members),
        far_ahead,
        teams_swapped(far_share[ahead:], near + ahead, members),
    ]
    returned = jnp.concatenate(back, axis=0).reshape(EXPERTS * CAP, width)
    expert_sum = jnp.dot(
        weighted.T,
        returned.astype(jnp.float32),
        precision=lax.Precision.HIGHEST,
        preferred_element_type=jnp.float32,
    )
    return (hidden_in.astype(jnp.float32) + expert_sum).astype(jnp.bfloat16)


def solution(mesh):
    return jax.shard_map(
        per_device,
        mesh=mesh,
        in_specs=(
            P("loop", "tp"),
            P("loop", "tp"),
            P("loop", "tp"),
            P(None, "tp"),
            P("tp"),
            P("tp", None),
            P(None, "tp"),
            P("tp"),
            P(None, "tp"),
            P("tp"),
            P("tp", "loop"),
            P(),
            P("loop", None, "tp"),
            P("loop", None, "tp"),
            P("loop", "tp", None),
            P("loop", None),
            P("loop", None),
            P("loop", None),
        ),
        out_specs=P("loop", "tp"),
        check_vma=False,
    )
```

```python
import functools
import math

import jax
import jax.numpy as jnp
from jax import lax
from jax.experimental import pallas as pl
from jax.experimental.pallas import tpu as pltpu
from jax.sharding import PartitionSpec as P

NSTATE = 16
RANK = 256
EXPERTS = 8
TOPK = 2
CAP = 40
LANES = 128
EIGHTHS = 8
SUBLANES = 8
RESET = 1e30
LOG2E = math.log2(math.e)
VMEM = 40 * 1024 * 1024
SMALL_VMEM = 16 * 1024 * 1024


def shifted(x, axis, by):
    size = lax.axis_size(axis)
    pairs = [(i, i + by) for i in range(size) if 0 <= i + by < size]
    return lax.ppermute(x, axis, pairs)


def rotated(x, axis, by):
    size = lax.axis_size(axis)
    return lax.ppermute(x, axis, [(i, (i + by) % size) for i in range(size)])


def scan_end_kernel(
    low_ref, proj_ref, bias_ref, decay_ref, conved_ref, gain_ref, kept_ref,
    step_ref, end_ref, sd_ref, u_ref,
):
    tokens, width = step_ref.shape
    chunk = end_ref.shape[2]
    step = jax.nn.softplus(
        jnp.dot(low_ref[...], proj_ref[...], preferred_element_type=jnp.float32) + bias_ref[...]
    )
    step_ref[...] = step
    sd = jnp.where(kept_ref[...] > 0, step, RESET)
    sd_ref[...] = sd.reshape(sd_ref.shape)
    total = jnp.sum(sd, axis=0, keepdims=True)
    u_ref[...] = (step * conved_ref[...].astype(jnp.float32)).reshape(u_ref.shape)
    cols = [slice(i, i + LANES) for i in range(0, width, LANES)]
    rates = [decay_ref[:, c] * -LOG2E for c in cols]

    def advance(i, state):
        for r in range(SUBLANES):
            gain = gain_ref[i * SUBLANES + r]
            state = tuple(
                jnp.exp2(sd_ref[i, r : r + 1, c] * rate) * h + u_ref[i, r : r + 1, c] * gain
                for c, rate, h in zip(cols, rates, state)
            )
        return state

    zero = tuple(jnp.zeros((NSTATE, LANES), jnp.float32) for _ in cols)
    state = jnp.concatenate(lax.fori_loop(0, tokens // SUBLANES, advance, zero), axis=1)
    high = total.astype(jnp.bfloat16).astype(jnp.float32)
    row = lax.broadcasted_iota(jnp.int32, (NSTATE, width), 0)
    tail = jnp.where(row == 0, high, total - high)
    for k in range(width // chunk):
        part = slice(k * chunk, (k + 1) * chunk)
        end_ref[k, :NSTATE, :] = state[:, part].astype(end_ref.dtype)
        end_ref[k, NSTATE:, :] = tail[:, part].astype(end_ref.dtype)


def carry_kernel(ends_ref, decay_ref, carry_ref):
    rate = decay_ref[...] * -LOG2E
    state = jnp.zeros(rate.shape, jnp.float32)
    for block in range(ends_ref.shape[0]):
        carry_ref[block] = state.astype(carry_ref.dtype)
        tail = ends_ref[block, NSTATE:, :].astype(jnp.float32)
        total = tail[0:1] + tail[1:2]
        end = ends_ref[block, :NSTATE, :].astype(jnp.float32)
        state = jnp.exp2(total * rate) * state + end


def scan_kernel(
    step_ref, decay_ref, conved_ref, gain_ref, kept_ref, carry_ref, pick_ref, skip_ref, gate_ref,
    gated_ref, sd_ref, u_ref, states_ref,
):
    tokens, width = step_ref.shape
    step = step_ref[...]
    conved = conved_ref[...].astype(jnp.float32)
    sd_ref[...] = jnp.where(kept_ref[...] > 0, step, RESET).reshape(sd_ref.shape)
    u_ref[...] = (step * conved).reshape(u_ref.shape)
    cols = [slice(i, i + LANES) for i in range(0, width, LANES)]
    rates = [decay_ref[:, c] * -LOG2E for c in cols]

    def advance(i, state):
        for r in range(SUBLANES):
            gain = gain_ref[i * SUBLANES + r]
            state = tuple(
                jnp.exp2(sd_ref[i, r : r + 1, c] * rate) * h + u_ref[i, r : r + 1, c] * gain
                for c, rate, h in zip(cols, rates, state)
            )
            rows = pl.ds(pl.multiple_of((i * SUBLANES + r) * NSTATE, NSTATE), NSTATE)
            for c, h in zip(cols, state):
                states_ref[rows, c] = h.astype(states_ref.dtype)
        return state

    carry = [carry_ref[k].astype(jnp.float32) for k in range(carry_ref.shape[0])]
    carry = jnp.concatenate(carry, axis=1)
    lax.fori_loop(0, tokens // SUBLANES, advance, tuple(carry[:, c] for c in cols))
    scanned = jnp.dot(pick_ref[...], states_ref[...], preferred_element_type=jnp.float32)
    mixer_y = scanned + skip_ref[...] * conved
    gated_ref[...] = (mixer_y * jax.nn.silu(gate_ref[...].astype(jnp.float32))).astype(
        gated_ref.dtype
    )


def whole(shape):
    return pl.BlockSpec(shape, lambda i: (0,) * len(shape))


def scan_end(low_rank, step_proj, step_bias, decay_rate, conved, gain, kept, groups):
    tokens, channels = conved.shape
    rank = low_rank.shape[1]
    width = min(512, channels)
    chunk = channels // groups
    part = lambda rows: pl.BlockSpec((rows, width), lambda i: (0, i))
    return pl.pallas_call(
        scan_end_kernel,
        grid=(channels // width,),
        in_specs=[
            whole((tokens, rank)), part(rank), part(1), part(NSTATE), part(tokens),
            whole((tokens, NSTATE, LANES)), whole((tokens, 1)),
        ],
        out_specs=[
            part(tokens),
            pl.BlockSpec((width // chunk, 2 * NSTATE, chunk), lambda i: (i, 0, 0)),
        ],
        out_shape=[
            jax.ShapeDtypeStruct((tokens, channels), jnp.float32),
            jax.ShapeDtypeStruct((groups, 2 * NSTATE, chunk), jnp.bfloat16),
        ],
        scratch_shapes=[
            pltpu.VMEM((tokens // SUBLANES, SUBLANES, width), jnp.float32),
            pltpu.VMEM((tokens // SUBLANES, SUBLANES, width), jnp.float32),
        ],
        compiler_params=pltpu.CompilerParams(vmem_limit_bytes=SMALL_VMEM),
        cost_estimate=pl.CostEstimate(
            flops=5 * tokens * NSTATE * channels,
            bytes_accessed=8 * tokens * channels,
            transcendentals=tokens * NSTATE * channels,
        ),
        name="scan_end",
    )(low_rank, step_proj, step_bias[None, :], decay_rate, conved, gain, kept)


def carries(ends, decay_rate):
    groups, _, chunk = ends.shape
    return pl.pallas_call(
        carry_kernel,
        out_shape=jax.ShapeDtypeStruct((groups, NSTATE, chunk), jnp.bfloat16),
        name="carries",
    )(ends, decay_rate)


def scan_gated(step, decay_rate, conved, gain, kept, carry, pick, skip_gain, gate_in, first, steps):
    tokens, width = conved.shape[0], conved.shape[1] // EIGHTHS
    channels = steps * width
    chunk = carry.shape[2]
    part = lambda rows: pl.BlockSpec((rows, width), lambda i: (0, first + i))
    return pl.pallas_call(
        scan_kernel,
        grid=(steps,),
        in_specs=[
            part(tokens), part(NSTATE), part(tokens), whole((tokens, NSTATE, LANES)),
            whole((tokens, 1)),
            pl.BlockSpec((width // chunk, NSTATE, chunk), lambda i: (first + i, 0, 0)),
            whole(pick.shape), part(1), part(tokens),
        ],
        out_specs=pl.BlockSpec((tokens, width), lambda i: (0, i)),
        scratch_shapes=[
            pltpu.VMEM((tokens // SUBLANES, SUBLANES, width), jnp.float32),
            pltpu.VMEM((tokens // SUBLANES, SUBLANES, width), jnp.float32),
            pltpu.VMEM((tokens * NSTATE, width), jnp.bfloat16),
        ],
        out_shape=jax.ShapeDtypeStruct((tokens, channels), jnp.bfloat16),
        compiler_params=pltpu.CompilerParams(vmem_limit_bytes=SMALL_VMEM),
        cost_estimate=pl.CostEstimate(
            flops=7 * tokens * NSTATE * channels,
            bytes_accessed=12 * tokens * channels,
            transcendentals=tokens * NSTATE * channels,
        ),
        name="scan_gated",
    )(step, decay_rate, conved, gain, kept, carry, pick, skip_gain[None, :], gate_in)


def raise_kernel(shard_ref, *refs, pieces, members, steps):
    piece_refs, (gate_ref, up_ref, down_ref, hidden_ref) = refs[:pieces], refs[pieces : pieces + 4]
    out_refs, (rows_ref, all_ref) = refs[pieces + 4 : -2], refs[-2:]
    step = pl.program_id(0)

    @pl.when(step == 0)
    def _():
        for k, piece_ref in enumerate(piece_refs):
            rows = piece_ref.shape[0]
            rows_ref[k * rows : (k + 1) * rows] = piece_ref[...]

    @pl.when(step < steps)
    def _():
        rows = rows_ref[...]
        tile = hidden_ref.shape[1]
        gate = jnp.dot(rows, gate_ref[0], preferred_element_type=jnp.float32)
        up = jnp.dot(rows, up_ref[0], preferred_element_type=jnp.float32)
        hidden = (jax.nn.silu(gate) * up).astype(hidden_ref.dtype)
        hidden_ref[...] = hidden
        all_ref[:, pl.ds(pl.multiple_of(step * tile, tile), tile)] = hidden

    @pl.when(step >= steps)
    def _():
        out = jnp.dot(all_ref[...], down_ref[0], preferred_element_type=jnp.float32)
        for k, out_ref in enumerate(out_refs):
            rows = out_ref.shape[0]
            out_ref[...] = out[k * rows : (k + 1) * rows].astype(out_ref.dtype)


def raised(pieces, gate_weight, up_weight, down_weight, shard, features, members):
    rows, depth = sum(piece.shape[0] for piece in pieces), pieces[0].shape[1]
    width = gate_weight.shape[2]
    tile, out_tile = min(512, width), min(512, features)
    steps, out_steps = width // tile, features // out_tile
    up_at = lambda i: jnp.minimum(i, steps - 1)
    down_at = lambda i: jnp.maximum(i - steps, 0)
    weight = pl.BlockSpec((1, depth, tile), lambda i, t: (0, 0, up_at(i)))
    outs = pl.pallas_call(
        functools.partial(raise_kernel, pieces=len(pieces), members=members, steps=steps),
        grid_spec=pltpu.PrefetchScalarGridSpec(
            num_scalar_prefetch=1,
            grid=(steps + out_steps,),
            in_specs=[pl.BlockSpec(piece.shape, lambda i, t: (0, 0)) for piece in pieces]
            + [
                weight,
                weight,
                pl.BlockSpec(
                    (1, width, out_tile), lambda i, t: (0, 0, t[0] * out_steps + down_at(i))
                ),
            ],
            out_specs=[pl.BlockSpec((rows, tile), lambda i, t: (0, up_at(i)))]
            + [pl.BlockSpec((rows // members, out_tile), lambda i, t: (0, down_at(i)))] * members,
            scratch_shapes=[
                pltpu.VMEM((rows, depth), jnp.bfloat16),
                pltpu.VMEM((rows, width), jnp.bfloat16),
            ],
        ),
        out_shape=[jax.ShapeDtypeStruct((rows, width), jnp.bfloat16)]
        + [jax.ShapeDtypeStruct((rows // members, features), jnp.bfloat16)] * members,
        compiler_params=pltpu.CompilerParams(vmem_limit_bytes=60 * 1024 * 1024),
        cost_estimate=pl.CostEstimate(
            flops=2 * rows * width * (2 * depth + features),
            bytes_accessed=2 * width * (2 * depth + features),
            transcendentals=rows * width,
        ),
        name="raised",
    )(shard.astype(jnp.int32)[None], *pieces, gate_weight, up_weight, down_weight)
    return outs[0], outs[1:]


def lower_kernel(shard_ref, hidden_ref, weight_ref, *out_refs):
    out = jnp.dot(hidden_ref[...], weight_ref[0], preferred_element_type=jnp.float32)
    rows = out_refs[0].shape[0]
    for k, out_ref in enumerate(out_refs):
        out_ref[...] = out[k * rows : (k + 1) * rows].astype(out_ref.dtype)


def lowered(hidden, down_weight, shard, width, members):
    rows, depth = hidden.shape
    tile = min(512, width)
    steps = width // tile
    out = jax.ShapeDtypeStruct((rows // members, width), jnp.bfloat16)
    return pl.pallas_call(
        lower_kernel,
        grid_spec=pltpu.PrefetchScalarGridSpec(
            num_scalar_prefetch=1,
            grid=(steps,),
            in_specs=[
                pl.BlockSpec((rows, depth), lambda i, t: (0, 0)),
                pl.BlockSpec((1, depth, tile), lambda i, t: (0, 0, t[0] * steps + i)),
            ],
            out_specs=[pl.BlockSpec((rows // members, tile), lambda i, t: (0, i))] * members,
        ),
        out_shape=[out] * members,
        compiler_params=pltpu.CompilerParams(vmem_limit_bytes=VMEM),
        cost_estimate=pl.CostEstimate(
            flops=2 * rows * depth * width, bytes_accessed=2 * depth * width, transcendentals=0
        ),
        name="lowered",
    )(shard.astype(jnp.int32)[None], hidden, down_weight)


def summed_over(x, axis):
    total = x
    for by in range(1, lax.axis_size(axis)):
        total = total + rotated(x, axis, by)
    return total


def gathered(x, axis, mine, dim):
    size = lax.axis_size(axis)
    shape = x.shape[:dim] + (size * x.shape[dim],) + x.shape[dim + 1 :]
    out = jnp.zeros(shape, x.dtype)
    out = lax.dynamic_update_slice_in_dim(out, x, mine * x.shape[dim], dim)
    for by in range(1, size):
        source = lax.rem(mine + size - by, size)
        out = lax.dynamic_update_slice_in_dim(
            out, rotated(x, axis, by), source * x.shape[dim], dim
        )
    return out


def across(x, mask):
    return lax.ppermute(x, "loop", [(i, i ^ mask) for i in range(lax.axis_size("loop"))])


def teams_swapped(x, first, members):
    groups = lax.axis_size("loop")
    out = []
    for k in range(x.shape[0]):
        s = first + k
        if s == 0:
            out.append(x[k])
            continue
        pairs = [(i, ((i // members) ^ s) * members + i % members) for i in range(groups)]
        out.append(lax.ppermute(x[k], "loop", pairs))
    return jnp.concatenate(out, axis=0)


def hidden_kernel(low_ref, gather_ref, residual_ref, *refs):
    pieces, (hidden_ref, packed_ref) = refs[:-2], refs[-2:]
    for m, piece_ref in enumerate(pieces):
        block = piece_ref.shape[1] // 2
        for dc in range(2):
            place = low_ref[0] ^ (2 * m + dc)
            cols = pl.ds(pl.multiple_of(place * block, block), block)
            mixed = piece_ref[:, dc * block : (dc + 1) * block].astype(jnp.float32)
            hidden_ref[:, cols] = (residual_ref[:, cols].astype(jnp.float32) + mixed).astype(
                hidden_ref.dtype
            )
    packed_ref[...] = jnp.dot(
        gather_ref[...], hidden_ref[...], preferred_element_type=jnp.float32
    ).astype(packed_ref.dtype)


def hidden_and_packed(low, gather_matrix, residual_in, pieces):
    vmem = pl.BlockSpec(memory_space=pltpu.VMEM)
    return pl.pallas_call(
        hidden_kernel,
        in_specs=[pl.BlockSpec(memory_space=pltpu.SMEM)] + [vmem] * (2 + len(pieces)),
        out_specs=[vmem, vmem],
        out_shape=[
            jax.ShapeDtypeStruct(residual_in.shape, jnp.bfloat16),
            jax.ShapeDtypeStruct(
                (gather_matrix.shape[0], residual_in.shape[1]), jnp.bfloat16
            ),
        ],
        compiler_params=pltpu.CompilerParams(vmem_limit_bytes=SMALL_VMEM),
        name="hidden_and_packed",
    )(low, gather_matrix, residual_in, *pieces)


def per_device(
    mixer_in,
    gate_in,
    residual_in,
    conv_weight,
    conv_bias,
    state_proj,
    step_proj,
    step_bias,
    decay_rate,
    skip_gain,
    out_proj,
    segment_ids,
    gate_weight,
    up_weight,
    down_weight,
    routes,
    route_weight,
    keep_mask,
):
    tokens = mixer_in.shape[0]
    channels = mixer_in.shape[1]
    groups = lax.axis_size("loop")
    position = lax.axis_index("loop")
    shard = lax.axis_index("tp")
    shards = lax.axis_size("tp")
    low = groups // shards
    first_steps = 2
    first_rows = channels // EIGHTHS * first_steps
    far_first = [across(out_proj[:first_rows], low * high) for high in range(1, shards)]
    conv_taps = conv_weight.shape[0]
    rim_rows = shifted(mixer_in[tokens - (conv_taps - 1) :], "loop", 1)
    extended = jnp.concatenate([rim_rows, mixer_in], axis=0)
    conv_sum = jnp.broadcast_to(conv_bias[None, :], (tokens, channels))
    for offset in range(conv_taps):
        conv_sum = conv_sum + conv_weight[offset][None, :] * extended[
            offset : offset + tokens
        ].astype(jnp.float32)
    conved = jax.nn.silu(conv_sum).astype(jnp.bfloat16)
    block_start = position * tokens
    local_ids = lax.dynamic_slice_in_dim(segment_ids, block_start, tokens)
    before_start = jnp.maximum(block_start - 1, 0)
    before_id = lax.dynamic_slice_in_dim(segment_ids, before_start, 1)
    previous = jnp.where(block_start > 0, before_id, local_ids[:1])
    earlier_ids = jnp.concatenate([previous, local_ids[:-1]])
    kept = (local_ids == earlier_ids).astype(jnp.float32)[:, None]
    projected = summed_over(
        jnp.dot(conved, state_proj, preferred_element_type=jnp.float32), "tp"
    )
    low_rank = projected[:, :RANK].astype(jnp.bfloat16)
    in_gain = projected[:, RANK : RANK + NSTATE]
    out_gain = projected[:, RANK + NSTATE :]
    gain = jnp.broadcast_to(in_gain[:, :, None], (tokens, NSTATE, LANES))
    state_rows = jnp.arange(tokens * NSTATE, dtype=jnp.int32)
    spread = state_rows[None, :] % NSTATE == jnp.arange(NSTATE, dtype=jnp.int32)[:, None]
    pick = jnp.where(
        state_rows[None, :] // NSTATE == jnp.arange(tokens, dtype=jnp.int32)[:, None],
        jnp.dot(
            out_gain.astype(jnp.bfloat16),
            spread.astype(jnp.bfloat16),
            preferred_element_type=jnp.float32,
        ),
        0.0,
    ).astype(jnp.bfloat16)
    step_size, end_state = scan_end(
        low_rank, step_proj, step_bias, decay_rate, conved, gain, kept, groups
    )
    end_state, far_first = lax.optimization_barrier((end_state, far_first))
    ends = lax.all_to_all(end_state, "loop", 0, 0, tiled=True)
    chunk = channels // groups
    own_rates = lax.dynamic_slice_in_dim(decay_rate, position * chunk, chunk, 1)
    carry = lax.all_to_all(carries(ends, own_rates), "loop", 0, 0, tiled=True)
    later_rows, carry = lax.optimization_barrier((out_proj[first_rows:], carry))
    middle_rows = channels // EIGHTHS * 3
    far_middle = [across(later_rows[:middle_rows], low * high) for high in range(1, shards)]
    last_rows, far_middle = lax.optimization_barrier((later_rows[middle_rows:], far_middle))
    far_last = [across(last_rows, low * high) for high in range(1, shards)]
    own_low, own_high = position % low, position // low
    tokens_of = []
    for first, steps in ((0, first_steps), (first_steps, EIGHTHS - first_steps)):
        gated = scan_gated(
            step_size, decay_rate, conved, gain, kept, carry, pick, skip_gain, gate_in, first,
            steps,
        )
        tokens_of.append({0: gated})
    def joined(got, more):
        for m in range(6, low, 2):
            one = m & -m
            more[m] = across(got[m ^ one], one) if m != one else across(got[0], m)

    first, later = tokens_of
    for m in (2, 4):
        if m < low:
            later[m] = across(later[0], m)
    if low > 2:
        first[2] = across(first[0], 2)
    later, first = lax.optimization_barrier((later, first))
    if low > 4:
        first[4] = across(first[0], 4)
    joined(later, later)
    far_last, later, first = lax.optimization_barrier((far_last, later, first))
    far_later = [jnp.concatenate(parts, axis=0) for parts in zip(far_middle, far_last)]
    joined(first, first)
    tokens_of = [first, later]
    all_tokens = [
        jnp.concatenate([got[m] for m in range(0, low, 2)], axis=0) for got in tokens_of
    ]
    blocks = [(out_proj[:first_rows], out_proj[first_rows:])] + list(zip(far_first, far_later))
    mixes = []
    for block in blocks:
        mix = 0.0
        for some_tokens, part in zip(all_tokens, block):
            pair = jnp.concatenate([part, across(part, 1)], axis=1)
            mix = mix + jnp.dot(some_tokens, pair, preferred_element_type=jnp.float32)
        mixes.append(mix)

    def for_shard(t):
        mix = mixes[0]
        for high in range(1, shards):
            mix = jnp.where((own_high ^ t) == high, mixes[high], mix)
        return mix

    mixed_out = for_shard(shard)
    for by in range(1, shards):
        sent = for_shard((shard + by) % shards).astype(jnp.bfloat16)
        mixed_out = mixed_out + rotated(sent, "tp", by).astype(jnp.float32)
    pieces = [mixed_out[:tokens]]
    for k in range(1, low // 2):
        rows_out = mixed_out[k * tokens : (k + 1) * tokens].astype(jnp.bfloat16)
        pieces.append(across(rows_out, 2 * k))
    width = residual_in.shape[1]
    features = width * shards

    members = groups // EXPERTS
    team, member = position // members, position % members
    flat_routes = routes.reshape(-1)
    expert_ids = jnp.arange(EXPERTS, dtype=jnp.int32)
    onehot = (flat_routes[:, None] == expert_ids[None, :]).astype(jnp.int32)
    slot_index = jnp.sum(jnp.cumsum(onehot, axis=0) * onehot, axis=1) - 1
    target = (flat_routes ^ team) * CAP + slot_index
    selector = (jnp.arange(EXPERTS * CAP, dtype=jnp.int32)[:, None] == target[None, :]).astype(
        jnp.float32
    )
    gather_matrix = jnp.sum(selector.reshape(EXPERTS * CAP, tokens, TOPK), axis=2)
    keep_weight = jnp.sum(onehot.astype(jnp.float32) * keep_mask.astype(jnp.float32), axis=1)
    weights = route_weight.reshape(-1) * keep_weight
    weighted = jnp.sum((selector * weights[None, :]).reshape(EXPERTS * CAP, tokens, TOPK), axis=2)
    hidden_in, packed = hidden_and_packed(
        own_low.astype(jnp.int32)[None], gather_matrix.astype(jnp.bfloat16), residual_in, pieces
    )
    packed = packed.reshape(EXPERTS, CAP, width)
    near = EXPERTS // 2
    rows = near * CAP

    def from_member(by):
        pairs = [
            (i, i // members * members + (i + by) % members) for i in range(groups)
        ]
        return lambda x: lax.ppermute(x, "loop", pairs)

    parts = [
        gathered(teams_swapped(packed[first : first + near], first, members), "tp", shard, 1)
        for first in (0, near)
    ]
    pieces = parts + [from_member(by)(part) for by in range(1, members) for part in parts]
    hidden, outs = raised(
        pieces, gate_weight, up_weight, down_weight, (shard + 1) % shards, width, members
    )

    def member_sum(outs):
        total = outs[0].astype(jnp.float32)
        for by in range(1, members):
            total = total + from_member(members - by)(outs[by]).astype(jnp.float32)
        return total

    def for_shard_of(hidden, t):
        return lowered(hidden, down_weight, t, width, members)

    sent = [member_sum(outs).astype(jnp.bfloat16)] + [
        member_sum(for_shard_of(hidden, (shard + by) % shards)).astype(jnp.bfloat16)
        for by in range(2, shards)
    ]
    hidden, sent = lax.optimization_barrier((hidden, sent))
    far_sums = [rotated(part[rows:], "tp", by) for by, part in enumerate(sent, 1)]
    own_outs = for_shard_of(hidden, shard)
    far_sums, own_outs, near_sent = lax.optimization_barrier(
        (far_sums, own_outs, [part[:rows] for part in sent])
    )
    near_sums = [rotated(part, "tp", by) for by, part in enumerate(near_sent, 1)]
    own_sum = member_sum(own_outs)

    def shared(own, sums):
        share = own
        for part in sums:
            share = share + part.astype(jnp.float32)
        return share.astype(jnp.bfloat16).reshape(near, CAP, width)

    ahead = near // 2
    far_share = shared(own_sum[rows:], far_sums)
    far_ahead = teams_swapped(far_share[:ahead], near, members)
    near_sums, far_ahead = lax.optimization_barrier((near_sums, far_ahead))
    near_share = shared(own_sum[:rows], near_sums)
    back = [
        teams_swapped(near_share, 0, members),
        far_ahead,
        teams_swapped(far_share[ahead:], near + ahead, members),
    ]
    returned = jnp.concatenate(back, axis=0).reshape(EXPERTS * CAP, width)
    expert_sum = jnp.dot(
        weighted.T,
        returned.astype(jnp.float32),
        precision=lax.Precision.HIGHEST,
        preferred_element_type=jnp.float32,
    )
    return (hidden_in.astype(jnp.float32) + expert_sum).astype(jnp.bfloat16)


def solution(mesh):
    return jax.shard_map(
        per_device,
        mesh=mesh,
        in_specs=(
            P("loop", "tp"),
            P("loop", "tp"),
            P("loop", "tp"),
            P(None, "tp"),
            P("tp"),
            P("tp", None),
            P(None, "tp"),
            P("tp"),
            P(None, "tp"),
            P("tp"),
            P("tp", "loop"),
            P(),
            P("loop", None, "tp"),
            P("loop", None, "tp"),
            P("loop", "tp", None),
            P("loop", None),
            P("loop", None),
            P("loop", None),
        ),
        out_specs=P("loop", "tp"),
        check_vma=False,
    )
```
